32 devices in a mesh: parts: 2 (over y), tm: 4 (over z), axial: 2 (over x), chan: 2 (over core).
Axes of the slice: x: 2, y: 2, z: 4, core: 2. Of those that a mesh axis runs over, the one named last changes fastest.
Arguments:
- frames_in: bfloat16 [48, 8, 64, 128], P(('parts', 'tm'), 'axial'), parts along dimension 0, may hold values from -6 to 6
- spatial_weight: bfloat16 [6, 3, 64, 144], P('parts', None, None, 'chan'), parts along dimension 0, may hold values from -0.25 to 0.25
- temporal_weight: bfloat16 [6, 144, 64], P('parts', 'chan'), parts along dimension 0, may hold values from -0.3125 to 0.3125
- upstream: bfloat16 [48, 8, 64, 128], P(('parts', 'tm'), 'axial'), parts along dimension 0, may hold values from -6 to 6
Outputs:
- output: bfloat16 [48, 8, 64, 128], P(('parts', 'tm'), 'axial', 'chan'), parts along dimension 0
- input_grad: bfloat16 [48, 8, 64, 128], P(('parts', 'tm'), 'axial', 'chan'), parts along dimension 0
- spatial_grad: float32 [6, 3, 64, 144], P('parts', None, None, 'chan'), parts along dimension 0
- temporal_grad: float32 [6, 144, 64], P('parts', 'chan'), parts along dimension 0
The draws below stay inside these ranges and needn't reach their ends.
There are 2 independent parts, one for each index of `parts`. The reference program is written for one: setup_inputs(seed, part) draws one part's arguments, and reference() takes and returns one part's arrays. A program takes and returns all parts, laid end to end along the dimension named above; each array names one. Nothing has to cross between parts.
All inputs are finite; a program needn't handle non-finite values.
Results may differ from the reference program's by a relative error of at most 0.009.
Values may be sent and summed in bfloat16 or wider, within the bound.
No kernel may reach another device: no remote copies, remote signals or barrier semaphores. Data moves between devices by JAX's collectives and lax.ppermute only.
A program may use at most 64 MiB of HBM per device.

```python
import math
import jax
import jax.numpy as jnp
from jax import lax

CH = 64
MID = 144
WD = 128
FRAMES = 24
ROWS = 8


def level_of(rng, dims, pieces, smallest, high):
    gain = 1.0
    for position, blocks in pieces:
        draws = jax.random.uniform(jax.random.fold_in(jax.random.fold_in(rng, 6), position), (blocks,), jnp.float32, smallest / len(pieces), high / len(pieces))
        gain = gain * jnp.repeat(jnp.exp(draws), dims[position] // blocks).reshape((-1,) + (1,) * (len(dims) - 1 - position))
    return gain


def noise(rng, extent, width, limit, shards=(), kind=jnp.bfloat16):
    entries = width * jax.random.normal(rng, extent, jnp.float32)
    if shards:
        entries = entries * level_of(rng, extent, shards, -0.22, 0.18)
    return jnp.clip(entries, -limit, limit).astype(kind)


def setup_inputs(seed: int = 0, part: int = 0) -> dict:
    arg_keys = jax.random.split(jax.random.key(seed), 5)
    part_keys = jax.random.split(jax.random.fold_in(arg_keys[4], part), 5)
    frames_in = noise(part_keys[0], (FRAMES, ROWS, CH, WD), 1.0, 6.0, ((0, 4), (1, 2)))
    spatial_weight = noise(part_keys[1], (3, 3, CH, MID), (9 * CH) ** -0.5, 0.25, ((3, 2),))
    temporal_weight = noise(part_keys[2], (3, MID, CH), (3 * MID) ** -0.5, 0.3125, ((1, 2),))
    upstream = noise(part_keys[3], (FRAMES, ROWS, CH, WD), 1.0, 6.0, ((0, 4), (1, 2)))
    return {"frames_in": frames_in, "spatial_weight": spatial_weight, "temporal_weight": temporal_weight, "upstream": upstream}


def conv_same(lhs_arr, rhs_arr, specs):
    return lax.conv_general_dilated(lhs_arr.astype(jnp.float32), rhs_arr.astype(jnp.float32), (1, 1), ((1, 1), (1, 1)), dimension_numbers=specs, preferred_element_type=jnp.float32)

def reference(frames_in, spatial_weight, temporal_weight, upstream):
    frame_total, row_total, channels, width_total = frames_in.shape
    factor = 1.0 / math.sqrt(frame_total * row_total * width_total)
    preact = conv_same(frames_in, spatial_weight, ('NHCW', 'HWIO', 'NHCW'))
    hidden = lax.optimization_barrier(jax.nn.silu(preact).astype(jnp.bfloat16))
    hidden_wide = hidden.astype(jnp.float32)
    upstream_wide = upstream.astype(jnp.float32)
    weight_wide = temporal_weight.astype(jnp.float32)
    summed = jnp.zeros(frames_in.shape, jnp.float32)
    grad_act = jnp.zeros(preact.shape, jnp.float32)
    temporal_list = []
    for offset in range(3):
        moved = jnp.roll(hidden_wide, 1 - offset, axis=0)
        summed = summed + jnp.einsum('fhmw,mc->fhcw', moved, weight_wide[offset])
        grad_act = grad_act + jnp.einsum('fhcw,mc->fhmw', jnp.roll(upstream_wide, offset - 1, axis=0), weight_wide[offset])
        temporal_list.append(jnp.einsum('fhmw,fhcw->mc', moved, upstream_wide))
    output = summed.astype(jnp.bfloat16)
    temporal_grad = jnp.stack(temporal_list) * factor
    sigma = jax.nn.sigmoid(preact)
    grad_pre = lax.optimization_barrier((grad_act * sigma * (1.0 + preact * (1.0 - sigma))).astype(jnp.bfloat16))
    grad_wide = grad_pre.astype(jnp.float32)
    padded = jnp.pad(frames_in.astype(jnp.float32), ((0, 0), (1, 1), (0, 0), (1, 1)))
    spatial_rows = []
    for i in range(3):
        spatial_rows.append(jnp.stack([jnp.einsum('fhcw,fhmw->cm', padded[:, i:i + row_total, :, j:j + width_total], grad_wide) for j in range(3)]))
    spatial_grad = jnp.stack(spatial_rows) * factor
    input_grad = conv_same(grad_wide, spatial_weight[::-1, ::-1], ('NHCW', 'HWOI', 'NHCW')).astype(jnp.bfloat16)
    return (output, input_grad, spatial_grad, temporal_grad)
```

```python
import functools
import math

import jax
import jax.numpy as jnp
from jax import lax
from jax.experimental import pallas as pl
from jax.experimental.pallas import tpu as pltpu
from jax.sharding import PartitionSpec as P

F32 = jnp.float32
BF16 = jnp.bfloat16
LANES = 128
DIRECT_RANKS = 16


def ring(count, step):
    return [(i, (i + step) % count) for i in range(count)]


def dot(a, b):
    return jnp.dot(a, b, preferred_element_type=F32)


def dot_nt(a, b):
    return lax.dot_general(a, b, (((1,), (1,)), ((), ())), preferred_element_type=F32)


def moved(value, step):
    width = value.shape[1]
    column = lax.broadcasted_iota(jnp.int32, value.shape, 1)
    edge = 0 if step > 0 else width - 1
    return jnp.where(column == edge, 0.0, pltpu.roll(value, step % width, 1))


def main_kernel(dims, refs):
    frames, rows, channels, width, mid, own_c, rank_count, chunk_count, chunk, axial_count = dims
    (x, x_lo, x_hi, u, u_lo, u_hi, sw, sw_other, tw, tw_other) = refs[:10]
    outs = refs[10:]
    out, out_lo, out_hi, ig, ig_lo, ig_hi = outs[:6]
    chunks = outs[6 : 6 + chunk_count]
    xp, wf, twf, twt, twt_full, wg, ig_acc, w_acc, t_acc, packed = outs[6 + chunk_count :]
    axial = lax.axis_index("axial")
    core = lax.axis_index("chan")
    rank = lax.axis_index("tm") * axial_count + axial
    first_c = pl.multiple_of(core * own_c, own_c)

    blocks = []
    for half in (sw, sw_other):
        for j in range(3):
            blocks.append(half[:, j].reshape(3 * channels, mid).astype(F32).T)
    wf[...] = jnp.concatenate(blocks, 0).astype(BF16)
    twf[...] = jnp.concatenate(
        [jnp.concatenate([half[k].astype(F32) for k in (2, 1, 0)], 1) for half in (tw, tw_other)], 0
    ).astype(BF16)
    for k in range(3):
        twt_full[k] = jnp.concatenate([tw[k].astype(F32), tw_other[k].astype(F32)], 0).T
    for k in range(3):
        twt[k * own_c : (k + 1) * own_c] = twt_full[k, pl.ds(first_c, own_c)].astype(BF16)
    for i in range(3):
        for j in range(3):
            at = (i * 3 + j) * own_c
            wg[at : at + own_c] = jnp.concatenate(
                [half[i, j, pl.ds(first_c, own_c)].astype(F32) for half in (sw, sw_other)], 1
            ).astype(BF16)

    has_lo = (axial > 0).astype(BF16)
    has_hi = (axial < axial_count - 1).astype(BF16)
    for f in range(frames):
        xp[f, 0] = x_lo[f, 0] * has_lo
        xp[f, rows + 1] = x_hi[f, 0] * has_hi
        for h in range(rows):
            xp[f, h + 1] = x[f, h]

    ig_acc[...] = jnp.zeros_like(ig_acc)
    w_acc[...] = jnp.zeros_like(w_acc)
    t_acc[...] = jnp.zeros_like(t_acc)

    def u_at(f, h):
        if f < 0:
            return u_lo[0, h]
        if f >= frames:
            return u_hi[0, h]
        return u[f, h]

    group = 2 if frames % 2 == 0 else 1

    def row(h, carry):
        out_terms = {}
        for first in range(0, frames, group):
            picked = range(first, first + group)
            field = jnp.concatenate([xp[f, pl.ds(h, 3)].reshape(3 * channels, width) for f in picked], 1)
            cot = jnp.concatenate(
                [jnp.concatenate([u_at(f + d, h) for d in (-1, 0, 1)], 0) for f in picked], 1
            )
            taps = dot(wf[...], field)
            act = dot(twf[...], cot)
            hid_parts, grad_parts = [], []
            own_shift = None
            for half in range(2):
                base = half * 3 * mid
                hids, grads = [], []
                for g in range(group):
                    cols = slice(g * width, (g + 1) * width)
                    pre = (
                        taps[base + mid : base + 2 * mid, cols]
                        + moved(taps[base : base + mid, cols], 1)
                        + moved(taps[base + 2 * mid : base + 3 * mid, cols], -1)
                    )
                    s = 0.5 * jnp.tanh(0.5 * pre) + 0.5
                    hids.append(pre * s)
                    grads.append(act[half * mid : (half + 1) * mid, cols] * s * (1.0 + pre * (1.0 - s)))
                if half == 0:
                    own_shift = jnp.concatenate(
                        [
                            jnp.concatenate([moved(v, -1) for v in grads], 1),
                            jnp.concatenate(grads, 1),
                            jnp.concatenate([moved(v, 1) for v in grads], 1),
                        ],
                        0,
                    ).astype(BF16)
                hid_parts.append(jnp.concatenate(hids, 1))
                grad_parts.append(jnp.concatenate(grads, 1))
            hid = jnp.concatenate(hid_parts, 0).astype(BF16)
            grad = jnp.concatenate(grad_parts, 0).astype(BF16)
            hid_own = hid_parts[0].astype(BF16)
            w_acc[...] += dot_nt(field, own_shift)
            t_acc[...] += dot_nt(hid_own, cot)
            y_out = dot(twt[...], hid)
            y_in = dot(wg[...], grad)
            for g, f in enumerate(picked):
                cols = slice(g * width, (g + 1) * width)
                for k in range(3):
                    out_terms.setdefault(f - k + 1, []).append(y_out[k * own_c : (k + 1) * own_c, cols])
                for i in range(3):
                    at = i * 3 * own_c
                    total = (
                        y_in[at + own_c : at + 2 * own_c, cols]
                        + moved(y_in[at : at + own_c, cols], -1)
                        + moved(y_in[at + 2 * own_c : at + 3 * own_c, cols], 1)
                    )
                    ig_acc[f, h + i] += total
        for f, terms in out_terms.items():
            total = functools.reduce(lambda a, b: a + b, terms)
            if f < 0:
                out_lo[0, h] = total.astype(BF16)
            elif f >= frames:
                out_hi[0, h] = total.astype(BF16)
            else:
                out[f, h] = total
        return carry

    lax.fori_loop(0, rows, row, 0)

    for f in range(frames):
        ig_lo[f] = ig_acc[f, 0].astype(BF16)
        ig_hi[f] = ig_acc[f, rows + 1].astype(BF16)
        for h in range(rows):
            ig[f, h] = ig_acc[f, h + 1]

    factor = 1.0 / math.sqrt(frames * rows * width * rank_count)
    at = 0
    packed[...] = jnp.zeros_like(packed)
    for acc in (w_acc, t_acc):
        depth, total = acc.shape
        for first in range(0, total, LANES):
            last = min(first + LANES, total)
            packed[at : at + depth, : last - first] = acc[:, first:last] * factor
            at += depth
    for step in range(chunk_count):
        to = lax.rem(rank + step, chunk_count)
        chunks[step][...] = packed[pl.ds(pl.multiple_of(to * chunk, chunk), chunk)].astype(chunks[step].dtype)


def sum_kernel(*refs):
    total = refs[0][...]
    for ref in refs[1:-1]:
        total = total + ref[...].astype(F32)
    refs[-1][...] = total.astype(BF16)


def final_kernel(dims, refs):
    frames, rows, channels, width, mid, own_c, rank_count, chunk_count, chunk, axial_count = dims
    own, from_lo, from_hi, ig_own, ig_from_lo, ig_from_hi = refs[:6]
    parts = refs[6 : 6 + chunk_count]
    out, ig, sg, tg, packed = refs[6 + chunk_count :]
    axial = lax.axis_index("axial")
    rank = lax.axis_index("tm") * axial_count + axial
    has_lo = (axial > 0).astype(F32)
    has_hi = (axial < axial_count - 1).astype(F32)
    for f in range(frames):
        for h in range(rows):
            total = own[f, h]
            if f == 0:
                total = total + from_lo[0, h].astype(F32)
            if f == frames - 1:
                total = total + from_hi[0, h].astype(F32)
            out[f, h] = total.astype(BF16)
            total = ig_own[f, h]
            if h == 0:
                total = total + ig_from_lo[f].astype(F32) * has_lo
            if h == rows - 1:
                total = total + ig_from_hi[f].astype(F32) * has_hi
            ig[f, h] = total.astype(BF16)
    for step in range(chunk_count):
        source = lax.rem(rank - step + rank_count, chunk_count)
        packed[pl.ds(pl.multiple_of(source * chunk, chunk), chunk)] = parts[step][...].astype(F32)
    unpack(packed, sg, tg, channels, mid)


def unpack(packed, sg, tg, channels, mid):
    at = 0
    wide = []
    for depth, total in ((3 * channels, 3 * mid), (mid, 3 * channels)):
        pieces = []
        for first in range(0, total, LANES):
            pieces.append(packed[at : at + depth])
            at += depth
        wide.append(jnp.concatenate(pieces, 1))
    for j in range(3):
        block = wide[0][:, j * mid : (j + 1) * mid]
        for i in range(3):
            sg[i, j] = block[i * channels : (i + 1) * channels]
    for k in range(3):
        tg[k] = wide[1][:, (2 - k) * channels : (3 - k) * channels]


def whole(count):
    return [pl.BlockSpec(memory_space=pltpu.VMEM)] * count


def shards(frames_in, spatial_weight, temporal_weight, upstream):
    frames, rows, channels, width = frames_in.shape
    mid = temporal_weight.shape[1]
    axial_count = lax.axis_size("axial")
    tm_count = lax.axis_size("tm")
    core_count = lax.axis_size("chan")
    rank_count = tm_count * axial_count
    axial = lax.axis_index("axial")
    own_c = channels // core_count
    direct = rank_count <= DIRECT_RANKS
    depth = 3 * channels * (-(-3 * mid // LANES)) + mid * (-(-3 * channels // LANES))
    if direct:
        chunk = -(-depth // (16 * rank_count)) * 16
        chunk_count = rank_count
    else:
        chunk = -(-depth // 16) * 16
        chunk_count = 1
    dims = (frames, rows, channels, width, mid, own_c, rank_count, chunk_count, chunk, axial_count)

    sw_other = lax.ppermute(spatial_weight, "chan", ring(core_count, 1))
    tw_other = lax.ppermute(temporal_weight, "chan", ring(core_count, 1))
    if axial_count == 2:
        edge = lax.dynamic_slice_in_dim(frames_in, jnp.where(axial == 0, rows - 1, 0), 1, 1)
        x_lo = x_hi = lax.ppermute(edge, "axial", ring(2, 1))
    else:
        x_lo = lax.ppermute(frames_in[:, rows - 1 :], "axial", ring(axial_count, 1))
        x_hi = lax.ppermute(frames_in[:, :1], "axial", ring(axial_count, -1))
    u_lo = lax.ppermute(upstream[frames - 1 :], "tm", ring(tm_count, 1))
    u_hi = lax.ppermute(upstream[:1], "tm", ring(tm_count, -1))

    sds = jax.ShapeDtypeStruct
    own_shape = (frames, rows, own_c, width)
    chunk_shapes = [sds((chunk, LANES), F32)] + [sds((chunk, LANES), BF16)] * (chunk_count - 1)
    results = pl.pallas_call(
        lambda *refs: main_kernel(dims, refs),
        out_shape=[
            sds(own_shape, F32),
            sds((1, rows, own_c, width), BF16),
            sds((1, rows, own_c, width), BF16),
            sds(own_shape, F32),
            sds((frames, own_c, width), BF16),
            sds((frames, own_c, width), BF16),
        ]
        + chunk_shapes,
        in_specs=whole(10),
        out_specs=whole(6 + chunk_count),
        scratch_shapes=[
            pltpu.VMEM((frames, rows + 2, channels, width), BF16),
            pltpu.VMEM((6 * mid, 3 * channels), BF16),
            pltpu.VMEM((2 * mid, 3 * channels), BF16),
            pltpu.VMEM((3 * own_c, 2 * mid), BF16),
            pltpu.VMEM((3, channels, 2 * mid), F32),
            pltpu.VMEM((9 * own_c, 2 * mid), BF16),
            pltpu.VMEM((frames, rows + 2, own_c, width), F32),
            pltpu.VMEM((3 * channels, 3 * mid), F32),
            pltpu.VMEM((mid, 3 * channels), F32),
            pltpu.VMEM((chunk * chunk_count, LANES), F32),
        ],
        compiler_params=pltpu.CompilerParams(vmem_limit_bytes=32 * 1024 * 1024),
        name="block_main",
    )(frames_in, x_lo, x_hi, upstream, u_lo, u_hi, spatial_weight, sw_other, temporal_weight, tw_other)
    out_own, out_lo, out_hi, ig_own, ig_lo, ig_hi = results[:6]
    chunks = results[6:]

    from_hi = lax.ppermute(out_lo, "tm", ring(tm_count, -1))
    from_lo = lax.ppermute(out_hi, "tm", ring(tm_count, 1))
    if axial_count == 2:
        ig_from_lo = ig_from_hi = lax.ppermute(jnp.where(axial == 0, ig_hi, ig_lo), "axial", ring(2, 1))
    else:
        ig_from_hi = lax.ppermute(ig_lo, "axial", ring(axial_count, -1))
        ig_from_lo = lax.ppermute(ig_hi, "axial", ring(axial_count, 1))

    if direct:
        both = ("tm", "axial")
        terms = [chunks[0]] + [
            lax.ppermute(chunks[step], both, ring(rank_count, step)) for step in range(1, rank_count)
        ]
        mine = pl.pallas_call(
            sum_kernel,
            out_shape=sds((chunk, LANES), BF16),
            in_specs=whole(rank_count),
            out_specs=pl.BlockSpec(memory_space=pltpu.VMEM),
            name="sum_chunks",
        )(*terms)
        parts = [mine] + [lax.ppermute(mine, both, ring(rank_count, step)) for step in range(1, rank_count)]
    else:
        parts = [lax.psum(chunks[0], ("tm", "axial"))]

    return pl.pallas_call(
        lambda *refs: final_kernel(dims, refs),
        out_shape=[
            sds(own_shape, BF16),
            sds(own_shape, BF16),
            sds((3, 3, channels, mid), F32),
            sds((3, mid, channels), F32),
        ],
        in_specs=whole(6 + chunk_count),
        out_specs=whole(4),
        scratch_shapes=[pltpu.VMEM((chunk * chunk_count, LANES), F32)],
        name="block_final",
    )(out_own, from_lo, from_hi, ig_own, ig_from_lo, ig_from_hi, *parts)


def solution(mesh):
    placed = (
        P(("parts", "tm"), "axial", None, None),
        P("parts", None, None, "chan"),
        P("parts", "chan", None),
        P(("parts", "tm"), "axial", None, None),
    )
    return jax.shard_map(
        shards,
        mesh=mesh,
        in_specs=placed,
        out_specs=(
            P(("parts", "tm"), "axial", "chan", None),
            P(("parts", "tm"), "axial", "chan", None),
            P("parts", None, None, "chan"),
            P("parts", "chan", None),
        ),
        check_vma=False,
    )
```

```python
import functools
import math

import jax
import jax.numpy as jnp
from jax import lax
from jax.experimental import pallas as pl
from jax.experimental.pallas import tpu as pltpu
from jax.sharding import PartitionSpec as P

F32 = jnp.float32
BF16 = jnp.bfloat16
LANES = 128
VMEM = pl.BlockSpec(memory_space=pltpu.VMEM)
HBM = pl.BlockSpec(memory_space=pl.ANY)


def ring(count, step):
    return [(i, (i + step) % count) for i in range(count)]


def pairs(count, stride):
    return [(i, i ^ stride) for i in range(count)]


def dot(a, b):
    return jnp.dot(a, b, preferred_element_type=F32)


def dot_nt(a, b):
    return lax.dot_general(a, b, (((1,), (1,)), ((), ())), preferred_element_type=F32)


def moved(value, step):
    width = value.shape[1]
    column = lax.broadcasted_iota(jnp.int32, value.shape, 1)
    edge = 0 if step > 0 else width - 1
    return jnp.where(column == edge, 0.0, pltpu.roll(value, step % width, 1))


def pieces(depth, total):
    blocks, row = [], 0
    for first in range(0, total - total % LANES, LANES):
        blocks.append((row, 0, 0, first, depth, LANES))
        row += depth
    rest = total % LANES
    if rest:
        fold = LANES // rest
        if LANES % rest or depth % (8 * fold):
            fold = 1
        part = depth // fold
        for g in range(fold):
            blocks.append((row, g * rest, g * part, total - rest, part, rest))
        row += part
    return blocks, row


def half_rows(depth, total):
    return -(-pieces(depth, total)[1] // 32) * 16


def stage_kernel(x, u, sw, tw, xv, uv, edge, last, first, weights, sems):
    frames, rows = x.shape[:2]
    axial_low = lax.axis_index("axial") == 0
    row = jnp.where(axial_low, rows - 1, 0)
    copies = [
        pltpu.make_async_copy(x.at[:, pl.ds(row, 1)], edge, sems.at[0]),
        pltpu.make_async_copy(u.at[pl.ds(frames - 1, 1)], last, sems.at[1]),
        pltpu.make_async_copy(u.at[pl.ds(0, 1)], first, sems.at[2]),
        pltpu.make_async_copy(sw, weights.at[pl.ds(0, 3)], sems.at[3]),
        pltpu.make_async_copy(tw, weights.at[3], sems.at[4]),
        pltpu.make_async_copy(x, xv, sems.at[5]),
        pltpu.make_async_copy(u, uv, sems.at[6]),
    ]
    for copy in copies:
        copy.start()
    for copy in copies:
        copy.wait()


def grads_kernel(dims, *refs):
    frames, rows, channels, width, mid, own_c, rank_count, axial_count, group = dims
    x, x_lo, x_hi, u, u_lo, u_hi, wt, wt_other = refs[:8]
    hid_out, grad_out, keep, send, xp, wf, twf, acc, packed = refs[8:]
    axial = lax.axis_index("axial")

    for half, w in enumerate((wt, wt_other)):
        base = half * 3 * mid
        for j in range(3):
            wf[base + j * mid : base + (j + 1) * mid] = (
                w[0:3, j].reshape(3 * channels, mid).astype(F32).T
            )
        twf[half * mid : (half + 1) * mid] = jnp.concatenate([w[3, k].astype(F32) for k in (2, 1, 0)], 0).T

    has_lo = (axial > 0).astype(BF16)
    has_hi = (axial < axial_count - 1).astype(BF16)
    for f in range(frames):
        xp[f, 0] = x_lo[f, 0] * has_lo
        xp[f, rows + 1] = x_hi[f, 0] * has_hi
        for h in range(rows):
            xp[f, h + 1] = x[f, h]

    acc[...] = jnp.zeros_like(acc)
    w_taps = wf[...].astype(BF16)
    w_act = twf[...].astype(BF16)

    def u_at(f, h):
        if f < 0:
            return u_lo[0, h]
        if f >= frames:
            return u_hi[0, h]
        return u[f, h]

    def row(h, carry):
        fields, cots, shifts, owns = [], [], [], []
        for first in range(0, frames, group):
            picked = range(first, first + group)
            field = jnp.concatenate([xp[f, pl.ds(h, 3)].reshape(3 * channels, width) for f in picked], 1)
            cot = jnp.concatenate(
                [jnp.concatenate([u_at(f + d, h) for d in (-1, 0, 1)], 0) for f in picked], 1
            )
            taps = dot(w_taps, field)
            act = dot(w_act, cot)
            hid_parts, grad_parts = [], []
            for half in range(2):
                base = half * 3 * mid
                hids, grads = [], []
                for g in range(group):
                    cols = slice(g * width, (g + 1) * width)
                    pre = (
                        taps[base + mid : base + 2 * mid, cols]
                        + moved(taps[base : base + mid, cols], 1)
                        + moved(taps[base + 2 * mid : base + 3 * mid, cols], -1)
                    )
                    s = 0.5 * jnp.tanh(0.5 * pre) + 0.5
                    hids.append(pre * s)
                    grads.append(act[half * mid : (half + 1) * mid, cols] * s * (1.0 + pre * (1.0 - s)))
                if half == 0:
                    shifts.append(
                        jnp.concatenate(
                            [
                                jnp.concatenate([moved(v, -1) for v in grads], 1),
                                jnp.concatenate(grads, 1),
                                jnp.concatenate([moved(v, 1) for v in grads], 1),
                            ],
                            0,
                        ).astype(BF16)
                    )
                    owns.append(jnp.concatenate(hids, 1).astype(BF16))
                hid_parts.append(jnp.concatenate(hids, 1))
                grad_parts.append(jnp.concatenate(grads, 1))
            hid_out[h, first // group] = jnp.concatenate(hid_parts, 0).astype(BF16)
            grad_out[h, first // group] = jnp.concatenate(grad_parts, 0).astype(BF16)
            fields.append(field)
            cots.append(cot)
        acc[:, : 3 * mid] += dot_nt(jnp.concatenate(fields, 1), jnp.concatenate(shifts, 1))
        acc[:, 3 * mid :] += dot_nt(jnp.concatenate(cots, 1), jnp.concatenate(owns, 1))
        return carry

    lax.fori_loop(0, rows, row, 0)

    factor = 1.0 / math.sqrt(frames * rows * width * rank_count)
    blocks, used = pieces(*acc.shape)
    size = packed.shape[0] // 2
    packed[...] = jnp.zeros_like(packed)
    for at, lane, source, column, depth, total in blocks:
        packed[at : at + depth, lane : lane + total] = (
            acc[source : source + depth, column : column + total] * factor
        )
    mine = lax.rem(axial, 2)
    keep[...] = packed[pl.ds(pl.multiple_of(mine * size, 16), size)]
    send[...] = packed[pl.ds(pl.multiple_of((1 - mine) * size, 16), size)].astype(send.dtype)


def fields_kernel(dims, *refs):
    frames, rows, channels, width, mid, own_c, rank_count, axial_count, group = dims
    hid_in, grad_in, wt, wt_other = refs[:4]
    out, out_lo, out_hi, ig, ig_lo, ig_hi, twt, wg, ig_acc = refs[4:]
    core = lax.axis_index("chan")
    first_c = pl.multiple_of(core * own_c, own_c)
    own = pl.ds(first_c, own_c)
    for k in range(3):
        twt[k * own_c : (k + 1) * own_c] = jnp.concatenate(
            [w[3, k, own].astype(F32) for w in (wt, wt_other)], 1
        ).astype(BF16)
    for i in range(3):
        for j in range(3):
            at = (i * 3 + j) * own_c
            wg[at : at + own_c] = jnp.concatenate([w[i, j, own].astype(F32) for w in (wt, wt_other)], 1).astype(BF16)
    ig_acc[...] = jnp.zeros_like(ig_acc)

    def row(h, carry):
        out_terms = {}
        for first in range(0, frames, group):
            y_out = dot(twt[...], hid_in[h, first // group])
            y_in = dot(wg[...], grad_in[h, first // group])
            for g in range(group):
                f = first + g
                cols = slice(g * width, (g + 1) * width)
                for k in range(3):
                    out_terms.setdefault(f - k + 1, []).append(y_out[k * own_c : (k + 1) * own_c, cols])
                for i in range(3):
                    at = i * 3 * own_c
                    ig_acc[f, h + i] += (
                        y_in[at + own_c : at + 2 * own_c, cols]
                        + moved(y_in[at : at + own_c, cols], -1)
                        + moved(y_in[at + 2 * own_c : at + 3 * own_c, cols], 1)
                    )
        for f, terms in out_terms.items():
            total = functools.reduce(lambda a, b: a + b, terms)
            if f < 0:
                out_lo[0, h] = total.astype(BF16)
            elif f >= frames:
                out_hi[0, h] = total.astype(BF16)
            else:
                out[f, h] = total
        return carry

    lax.fori_loop(0, rows, row, 0)
    for f in range(frames):
        ig_lo[f] = ig_acc[f, 0].astype(BF16)
        ig_hi[f] = ig_acc[f, rows + 1].astype(BF16)
        for h in range(rows):
            ig[f, h] = ig_acc[f, h + 1]


def outputs_kernel(axial_count, own, from_lo, from_hi, ig_own, ig_from_lo, ig_from_hi, out, ig):
    frames, rows = own.shape[:2]
    axial = lax.axis_index("axial")
    has_lo = (axial > 0).astype(F32)
    has_hi = (axial < axial_count - 1).astype(F32)
    for f in range(frames):
        for h in range(rows):
            total = own[f, h]
            if f == 0:
                total = total + from_lo[0, h].astype(F32)
            if f == frames - 1:
                total = total + from_hi[0, h].astype(F32)
            out[f, h] = total.astype(BF16)
            total = ig_own[f, h]
            if h == 0:
                total = total + ig_from_lo[f].astype(F32) * has_lo
            if h == rows - 1:
                total = total + ig_from_hi[f].astype(F32) * has_hi
            ig[f, h] = total.astype(BF16)


def unpack_kernel(mine, other, sg, tg, packed, acc):
    channels, mid = tg.shape[1:]
    size = mine.shape[0]
    half = lax.rem(lax.axis_index("axial"), 2)
    packed[pl.ds(pl.multiple_of(half * size, 16), size)] = mine[...].astype(F32)
    packed[pl.ds(pl.multiple_of((1 - half) * size, 16), size)] = other[...].astype(F32)
    for at, lane, source, column, depth, total in pieces(*acc.shape)[0]:
        acc[source : source + depth, column : column + total] = packed[at : at + depth, lane : lane + total]
    for i in range(3):
        rows = slice(i * channels, (i + 1) * channels)
        for j in range(3):
            sg[i, j] = acc[rows, j * mid : (j + 1) * mid]
        tg[2 - i] = acc[rows, 3 * mid :]


def call(kernel, name, out_shape, count, limit, scratch=(), in_specs=None, flops=0):
    return pl.pallas_call(
        kernel,
        out_shape=out_shape,
        in_specs=in_specs or [VMEM] * count,
        out_specs=[VMEM] * len(out_shape),
        scratch_shapes=list(scratch),
        compiler_params=pltpu.CompilerParams(vmem_limit_bytes=limit * 1024 * 1024),
        cost_estimate=pl.CostEstimate(flops=flops, bytes_accessed=1 << 20, transcendentals=0) if flops else None,
        name=name,
    )


def shards(frames_in, spatial_weight, temporal_weight, upstream):
    frames, rows, channels, width = frames_in.shape
    mid = temporal_weight.shape[1]
    axial_count = lax.axis_size("axial")
    tm_count = lax.axis_size("tm")
    core_count = lax.axis_size("chan")
    rank_count = tm_count * axial_count
    axial = lax.axis_index("axial")
    own_c = channels // core_count
    group = 2 if frames % 2 == 0 else 1
    dims = (frames, rows, channels, width, mid, own_c, rank_count, axial_count, group)
    size = half_rows(3 * channels, 4 * mid)
    sds = jax.ShapeDtypeStruct

    x, u, edge, last, first, weights = call(
        stage_kernel,
        "stage",
        [
            sds(frames_in.shape, BF16),
            sds(upstream.shape, BF16),
            sds((frames, 1, channels, width), BF16),
            sds((1, rows, channels, width), BF16),
            sds((1, rows, channels, width), BF16),
            sds((4, 3, channels, mid), BF16),
        ],
        4,
        4,
        [pltpu.SemaphoreType.DMA((7,))],
        [HBM] * 4,
    )(frames_in, upstream, spatial_weight, jnp.swapaxes(temporal_weight, 1, 2))
    if axial_count == 2:
        x_lo = x_hi = lax.ppermute(edge, "axial", ring(2, 1))
    else:
        x_lo = lax.ppermute(frames_in[:, rows - 1 :], "axial", ring(axial_count, 1))
        x_hi = lax.ppermute(frames_in[:, :1], "axial", ring(axial_count, -1))
    u_lo = lax.ppermute(last, "tm", ring(tm_count, 1))
    u_hi = lax.ppermute(first, "tm", ring(tm_count, -1))
    weights_other = lax.ppermute(weights, "chan", ring(core_count, 1))

    own_shape = (frames, rows, own_c, width)
    cells = (rows, frames // group, 2 * mid, group * width)
    hid, grad, keep, send = call(
        functools.partial(grads_kernel, dims),
        "weight_grads",
        [
            sds(cells, BF16),
            sds(cells, BF16),
            sds((size, LANES), F32),
            sds((size, LANES), BF16 if axial_count == 2 else F32),
        ],
        8,
        16,
        [
            pltpu.VMEM((frames, rows + 2, channels, width), BF16),
            pltpu.VMEM((6 * mid, 3 * channels), F32),
            pltpu.VMEM((2 * mid, 3 * channels), F32),
            pltpu.VMEM((3 * channels, 4 * mid), F32),
            pltpu.VMEM((2 * size, LANES), F32),
        ],
    )(x, x_lo, x_hi, u, u_lo, u_hi, weights, weights_other)

    got = lax.ppermute(send, "axial", ring(2, 1)) if axial_count == 2 else None

    out_own, out_lo, out_hi, ig_own, ig_lo, ig_hi = call(
        functools.partial(fields_kernel, dims),
        "field_products",
        [
            sds(own_shape, F32),
            sds((1, rows, own_c, width), BF16),
            sds((1, rows, own_c, width), BF16),
            sds(own_shape, F32),
            sds((frames, own_c, width), BF16),
            sds((frames, own_c, width), BF16),
        ],
        4,
        16,
        [
            pltpu.VMEM((3 * own_c, 2 * mid), BF16),
            pltpu.VMEM((9 * own_c, 2 * mid), BF16),
            pltpu.VMEM((frames, rows + 2, own_c, width), F32),
        ],
        flops=1 << 31,
    )(hid, grad, weights, weights_other)

    from_hi = lax.ppermute(out_lo, "tm", ring(tm_count, -1))
    from_lo = lax.ppermute(out_hi, "tm", ring(tm_count, 1))
    if axial_count == 2:
        ig_from_lo = ig_from_hi = lax.ppermute(jnp.where(axial == 0, ig_hi, ig_lo), "axial", ring(2, 1))
    else:
        ig_from_hi = lax.ppermute(ig_lo, "axial", ring(axial_count, -1))
        ig_from_lo = lax.ppermute(ig_hi, "axial", ring(axial_count, 1))

    if axial_count == 2 and tm_count & (tm_count - 1) == 0:
        mine = lax.optimization_barrier((keep + got.astype(F32)).astype(BF16))
        stride = 1
        while stride < tm_count:
            mine = lax.optimization_barrier(mine + lax.ppermute(mine, "tm", pairs(tm_count, stride)))
            stride *= 2
        other = lax.ppermute(mine, "axial", ring(2, 1))
    else:
        odd = lax.rem(axial, 2) == 1
        low, high = jnp.where(odd, send, keep), jnp.where(odd, keep, send)
        low, high = lax.psum((low, high), ("tm", "axial"))
        mine, other = jnp.where(odd, high, low), jnp.where(odd, low, high)

    output, input_grad = call(
        functools.partial(outputs_kernel, axial_count),
        "outputs",
        [sds(own_shape, BF16), sds(own_shape, BF16)],
        6,
        4,
        flops=1 << 29,
    )(out_own, from_lo, from_hi, ig_own, ig_from_lo, ig_from_hi)
    spatial_grad, temporal_grad = call(
        unpack_kernel,
        "unpack",
        [sds((3, 3, channels, mid), F32), sds((3, channels, mid), F32)],
        2,
        4,
        [pltpu.VMEM((2 * size, LANES), F32), pltpu.VMEM((3 * channels, 4 * mid), F32)],
    )(mine, other)
    return output, input_grad, spatial_grad, jnp.swapaxes(temporal_grad, 1, 2)


def solution(mesh):
    placed = (
        P(("parts", "tm"), "axial", None, None),
        P("parts", None, None, "chan"),
        P("parts", "chan", None),
        P(("parts", "tm"), "axial", None, None),
    )
    return jax.shard_map(
        shards,
        mesh=mesh,
        in_specs=placed,
        out_specs=(
            P(("parts", "tm"), "axial", "chan", None),
            P(("parts", "tm"), "axial", "chan", None),
            P("parts", None, None, "chan"),
            P("parts", "chan", None),
        ),
        check_vma=False,
    )
```

```python
import functools
import math

import jax
import jax.numpy as jnp
from jax import lax
from jax.experimental import pallas as pl
from jax.experimental.pallas import tpu as pltpu
from jax.sharding import PartitionSpec as P

F32 = jnp.float32
BF16 = jnp.bfloat16
LANES = 128
VMEM = pl.BlockSpec(memory_space=pltpu.VMEM)
HBM = pl.BlockSpec(memory_space=pltpu.HBM)


def ring(count, step):
    return [(i, (i + step) % count) for i in range(count)]


def pairs(count, stride):
    return [(i, i ^ stride) for i in range(count)]


def facing(count):
    order = []
    for i in range(count):
        order += [(2 * i, 2 * ((i - 1) % count) + 1), (2 * i + 1, 2 * ((i + 1) % count))]
    return order


def dot(a, b):
    return jnp.dot(a, b, preferred_element_type=F32)


def dot_nt(a, b):
    return lax.dot_general(a, b, (((1,), (1,)), ((), ())), preferred_element_type=F32)


def moved(value, step):
    width = value.shape[1]
    column = lax.broadcasted_iota(jnp.int32, value.shape, 1)
    edge = 0 if step > 0 else width - 1
    return jnp.where(column == edge, 0.0, pltpu.roll(value, step % width, 1))


def pieces(depth, total):
    blocks, row = [], 0
    for first in range(0, total - total % LANES, LANES):
        blocks.append((row, 0, 0, first, depth, LANES))
        row += depth
    rest = total % LANES
    if rest:
        fold = LANES // rest
        if LANES % rest or depth % (8 * fold):
            fold = 1
        part = depth // fold
        for g in range(fold):
            blocks.append((row, g * rest, g * part, total - rest, part, rest))
        row += part
    return blocks, row


def half_rows(depth, total):
    return -(-pieces(depth, total)[1] // 32) * 16


def stage_kernel(split, x, u, sw, tw, edge, frame, weights, sems):
    frames, rows = x.shape[:2]
    core = lax.axis_index("chan")
    if split:
        row = jnp.where(lax.axis_index("axial") == 0, rows - 1, 0)
        picked = pl.ds(core * (frames // 2), frames // 2)
    else:
        row = core * (rows - 1)
        picked = pl.ds(0, frames)
    copies = [
        pltpu.make_async_copy(u.at[core * (frames - 1)], frame, sems.at[1]),
        pltpu.make_async_copy(x.at[picked, row], edge, sems.at[0]),
        pltpu.make_async_copy(sw, weights.at[pl.ds(0, 3)], sems.at[2]),
        pltpu.make_async_copy(tw, weights.at[3], sems.at[3]),
    ]
    for copy in copies:
        copy.start()
    for copy in copies:
        copy.wait()


def prepare(w, wf, twf):
    _, _, channels, mid = w.shape
    for j in range(3):
        wf[j * mid : (j + 1) * mid] = w[0:3, j].reshape(3 * channels, mid).astype(F32).T
    twf[...] = jnp.concatenate([w[3, k].astype(F32) for k in (2, 1, 0)], 0).T
    return wf[...].astype(BF16), twf[...].astype(BF16)


def activations(w_taps, w_act, field, cot, width):
    mid = w_act.shape[0]
    taps = dot(w_taps, field)
    act = dot(w_act, cot)
    hids, grads = [], []
    for first in range(0, field.shape[1], width):
        cols = slice(first, first + width)
        pre = taps[mid : 2 * mid, cols] + moved(taps[:mid, cols], 1) + moved(taps[2 * mid :, cols], -1)
        s = 0.5 * jnp.tanh(0.5 * pre) + 0.5
        hids.append(pre * s)
        grads.append(act[:, cols] * s * (1.0 + pre * (1.0 - s)))
    return hids, grads


def gathered(xp, up, h, picked):
    depth = 3 * xp.shape[2]
    width = xp.shape[3]
    field = jnp.concatenate([xp[f, pl.ds(h, 3)].reshape(depth, width) for f in picked], 1)
    cot = jnp.concatenate([jnp.concatenate([up[f + d, h] for d in range(3)], 0) for f in picked], 1)
    return field, cot


def inner_rows(axial_count, rows):
    if axial_count == 2:
        low = lax.axis_index("axial") == 0
        return jnp.where(low, 0, 1), rows - 1, [jnp.where(low, rows - 1, 0)]
    return 1, rows - 2, [0, rows - 1]


def cell_grads(xp, up, w_taps, w_act, groups, store):
    fields, cots, shifts, owns = [], [], [], []
    width = xp.shape[3]
    for h, picked in groups:
        field, cot = gathered(xp, up, h, picked)
        hids, grads = activations(w_taps, w_act, field, cot, width)
        shifts.append(
            jnp.concatenate(
                [
                    jnp.concatenate([moved(v, -1) for v in grads], 1),
                    jnp.concatenate(grads, 1),
                    jnp.concatenate([moved(v, 1) for v in grads], 1),
                ],
                0,
            ).astype(BF16)
        )
        hids = [v.astype(BF16) for v in hids]
        owns.append(jnp.concatenate(hids, 1))
        for f, hid, grad in zip(picked, hids, grads):
            store(h, f, hid, grad.astype(BF16))
        fields.append(field)
        cots.append(cot)
    return (
        dot_nt(jnp.concatenate(fields, 1), jnp.concatenate(shifts, 1)),
        dot_nt(jnp.concatenate(cots, 1), jnp.concatenate(owns, 1)),
    )


def inner_kernel(dims, *refs):
    frames, rows, channels, width, mid, own_c, rank_count, axial_count, group = dims
    x, u, sw, tw = refs[:4]
    hid_out, grad_out, acc_out, xp, up, taps_out, act_out, wf, twf = refs[4:]
    for f in range(frames):
        for at in (0, rows + 1):
            xp[f, at] = jnp.zeros((channels, width), BF16)
        for h in range(rows):
            xp[f, h + 1] = x[f, h]
            up[f + 1, h] = u[f, h]
    for at in (0, frames + 1):
        up[at] = jnp.zeros(up.shape[1:], BF16)
    for j in range(3):
        wf[j * mid : (j + 1) * mid] = sw[:, j].reshape(3 * channels, mid).astype(F32).T
    twf[...] = jnp.concatenate([tw[k].astype(F32) for k in (2, 1, 0)], 0).T
    w_taps, w_act = wf[...].astype(BF16), twf[...].astype(BF16)
    taps_out[...] = w_taps
    act_out[...] = w_act

    first, count, _ = inner_rows(axial_count, rows)

    def store(h, f, hid, grad):
        hid_out[h - first, f - 1] = hid
        grad_out[h - first, f - 1] = grad

    groups = [(first + i, (f, f + 1)) for i in range(count) for f in range(1, frames - 1, 2)]
    w_part, t_part = cell_grads(xp, up, w_taps, w_act, groups, store)
    acc_out[:, : 3 * mid] = w_part
    acc_out[:, 3 * mid :] = t_part


def grads_kernel(dims, *refs):
    frames, rows, channels, width, mid, own_c, rank_count, axial_count, group = dims
    hid_in, grad_in, acc_in, x, u, edge, frame, swapped, taps_in, act_in = refs[:10]
    hid_out, grad_out, xp, up, keep, send, edges, acc, packed = refs[10:]
    axial = lax.axis_index("axial")
    core = lax.axis_index("chan")
    w_taps, w_act = taps_in[...], act_in[...]

    has_lo = (axial > 0).astype(BF16)
    has_hi = (axial < axial_count - 1).astype(BF16)
    part = edge.shape[0]
    edges[pl.ds(core * part, part)] = edge[...]
    edges[pl.ds((1 - core) * part, part)] = swapped[0:part]
    at_hi = 2 * part - frames
    for f in range(frames):
        xp[f, 0] = edges[f] * has_lo
        xp[f, rows + 1] = edges[at_hi + f] * has_hi
        for h in range(rows):
            xp[f, h + 1] = x[f, h + 1]
            up[f + 1, h] = u[f + 1, h]
    up[core * (frames + 1)] = frame[...]
    up[(1 - core) * (frames + 1)] = swapped[part:]

    first, count, others = inner_rows(axial_count, rows)

    def store(h, f, hid, grad):
        hid_out[h, f] = hid
        grad_out[h, f] = grad

    for i in range(count):
        for f in range(1, frames - 1):
            store(first + i, f, hid_in[i, f - 1], grad_in[i, f - 1])
    groups = [(first + i, (0, frames - 1)) for i in range(count)]
    groups += [(h, (f, f + 1)) for h in others for f in range(0, frames, 2)]
    w_part, t_part = cell_grads(xp, up, w_taps, w_act, groups, store)
    factor = 1.0 / math.sqrt(frames * rows * width * rank_count)
    acc[:, : 3 * mid] = (acc_in[:, : 3 * mid] + w_part) * factor
    acc[:, 3 * mid :] = (acc_in[:, 3 * mid :] + t_part) * factor

    blocks, used = pieces(*acc.shape)
    size = packed.shape[0] // 2
    packed[used:] = jnp.zeros((2 * size - used, LANES), F32)
    for at, lane, source, column, depth, total in blocks:
        packed[at : at + depth, lane : lane + total] = acc[source : source + depth, column : column + total]
    mine = lax.rem(axial, 2)
    keep[...] = packed[pl.ds(pl.multiple_of(mine * size, 16), size)]
    send[...] = packed[pl.ds(pl.multiple_of((1 - mine) * size, 16), size)].astype(send.dtype)


def fields_kernel(dims, *refs):
    frames, rows, channels, width, mid, own_c, rank_count, axial_count, group = dims
    hid_in, grad_in, xp, up, wt, wt_other = refs[:6]
    out, out_lo, out_hi, ig, ig_lo, ig_hi, wf, twf, twt, wg, ig_acc = refs[6:]
    core = lax.axis_index("chan")
    first_c = pl.multiple_of(core * own_c, own_c)
    own = pl.ds(first_c, own_c)
    w_taps, w_act = prepare(wt_other, wf, twf)
    for k in range(3):
        twt[k * own_c : (k + 1) * own_c] = jnp.concatenate(
            [w[3, k, own].astype(F32) for w in (wt, wt_other)], 1
        ).astype(BF16)
    for i in range(3):
        for j in range(3):
            at = (i * 3 + j) * own_c
            wg[at : at + own_c] = jnp.concatenate([w[i, j, own].astype(F32) for w in (wt, wt_other)], 1).astype(BF16)
    ig_acc[...] = jnp.zeros_like(ig_acc)

    def row(h, carry):
        out_terms = {}
        for first in range(0, frames, group):
            field, cot = gathered(xp, up, h, range(first, first + group))
            hids, grads = activations(w_taps, w_act, field, cot, width)
            picked = range(first, first + group)
            hid = [jnp.concatenate([hid_in[h, f].astype(F32), v], 0) for f, v in zip(picked, hids)]
            grad = [jnp.concatenate([grad_in[h, f].astype(F32), v], 0) for f, v in zip(picked, grads)]
            y_out = dot(twt[...], jnp.concatenate(hid, 1).astype(BF16))
            y_in = dot(wg[...], jnp.concatenate(grad, 1).astype(BF16))
            for g in range(group):
                f = first + g
                cols = slice(g * width, (g + 1) * width)
                for k in range(3):
                    out_terms.setdefault(f - k + 1, []).append(y_out[k * own_c : (k + 1) * own_c, cols])
                for i in range(3):
                    at = i * 3 * own_c
                    ig_acc[f, h + i] += (
                        y_in[at + own_c : at + 2 * own_c, cols]
                        + moved(y_in[at : at + own_c, cols], -1)
                        + moved(y_in[at + 2 * own_c : at + 3 * own_c, cols], 1)
                    )
        for f, terms in out_terms.items():
            total = functools.reduce(lambda a, b: a + b, terms)
            if f < 0:
                out_lo[0, h] = total.astype(BF16)
            elif f >= frames:
                out_hi[0, h] = total.astype(BF16)
            else:
                out[f, h] = total
        return carry

    lax.fori_loop(0, rows, row, 0)
    for f in range(frames):
        ig_lo[f] = ig_acc[f, 0].astype(BF16)
        ig_hi[f] = ig_acc[f, rows + 1].astype(BF16)
        for h in range(rows):
            ig[f, h] = ig_acc[f, h + 1]


def outputs_kernel(axial_count, own, from_lo, from_hi, ig_own, ig_from_lo, ig_from_hi, out, ig):
    frames, rows = own.shape[:2]
    axial = lax.axis_index("axial")
    has_lo = (axial > 0).astype(F32)
    has_hi = (axial < axial_count - 1).astype(F32)
    for f in range(frames):
        for h in range(rows):
            total = own[f, h]
            if f == 0:
                total = total + from_lo[0, h].astype(F32)
            if f == frames - 1:
                total = total + from_hi[0, h].astype(F32)
            out[f, h] = total.astype(BF16)
            total = ig_own[f, h]
            if h == 0:
                total = total + ig_from_lo[f].astype(F32) * has_lo
            if h == rows - 1:
                total = total + ig_from_hi[f].astype(F32) * has_hi
            ig[f, h] = total.astype(BF16)


def unpack_kernel(mine, other, sg, tg, packed, acc):
    channels, mid = tg.shape[1:]
    size = mine.shape[0]
    half = lax.rem(lax.axis_index("axial"), 2)
    packed[pl.ds(pl.multiple_of(half * size, 16), size)] = mine[...].astype(F32)
    packed[pl.ds(pl.multiple_of((1 - half) * size, 16), size)] = other[...].astype(F32)
    for at, lane, source, column, depth, total in pieces(*acc.shape)[0]:
        acc[source : source + depth, column : column + total] = packed[at : at + depth, lane : lane + total]
    for i in range(3):
        rows = slice(i * channels, (i + 1) * channels)
        for j in range(3):
            sg[i, j] = acc[rows, j * mid : (j + 1) * mid]
        tg[2 - i] = acc[rows, 3 * mid :]


def call(kernel, name, out_shape, count, limit, scratch=(), in_specs=None, flops=0, out_space=VMEM):
    return pl.pallas_call(
        kernel,
        out_shape=out_shape,
        in_specs=in_specs or [VMEM] * count,
        out_specs=[out_space] * len(out_shape),
        scratch_shapes=list(scratch),
        compiler_params=pltpu.CompilerParams(vmem_limit_bytes=limit * 1024 * 1024),
        cost_estimate=pl.CostEstimate(flops=flops, bytes_accessed=1 << 20, transcendentals=0) if flops else None,
        name=name,
    )


def shards(frames_in, spatial_weight, temporal_weight, upstream):
    frames, rows, channels, width = frames_in.shape
    mid = temporal_weight.shape[1]
    axial_count = lax.axis_size("axial")
    tm_count = lax.axis_size("tm")
    core_count = lax.axis_size("chan")
    rank_count = tm_count * axial_count
    axial = lax.axis_index("axial")
    own_c = channels // core_count
    group = 2 if frames % 2 == 0 else 1
    dims = (frames, rows, channels, width, mid, own_c, rank_count, axial_count, group)
    size = half_rows(3 * channels, 4 * mid)
    sds = jax.ShapeDtypeStruct

    split = axial_count == 2 and frames % 2 == 0
    edge_count = frames // 2 if split else frames
    turned = jnp.swapaxes(temporal_weight, 1, 2)
    edge, frame, weights = call(
        functools.partial(stage_kernel, split),
        "stage",
        [
            sds((edge_count, channels, width), BF16),
            sds((rows, channels, width), BF16),
            sds((4, 3, channels, mid), BF16),
        ],
        4,
        60,
        [pltpu.SemaphoreType.DMA((4,))],
        [HBM] * 4,
        out_space=HBM,
    )(frames_in, upstream, spatial_weight, turned)
    frame = lax.ppermute(frame, ("tm", "chan"), facing(tm_count))
    if split:
        edge = lax.ppermute(edge, "axial", ring(2, 1))
    else:
        edge = lax.ppermute(edge, ("axial", "chan"), facing(axial_count))
    weights_other = lax.ppermute(weights, "chan", ring(2, 1))

    own_shape = (frames, rows, own_c, width)
    inner = (inner_rows(axial_count, rows)[1], frames - 2, mid, width)
    cells = (rows, frames, mid, width)
    xp_shape = (frames, rows + 2, channels, width)
    up_shape = (frames + 2, rows, channels, width)
    total = (3 * channels, 4 * mid)
    hid, grad, acc, xp, up, w_taps, w_act = call(
        functools.partial(inner_kernel, dims),
        "inner_cells",
        [
            sds(inner, BF16),
            sds(inner, BF16),
            sds(total, F32),
            sds(xp_shape, BF16),
            sds(up_shape, BF16),
            sds((3 * mid, 3 * channels), BF16),
            sds((mid, 3 * channels), BF16),
        ],
        4,
        16,
        [pltpu.VMEM((3 * mid, 3 * channels), F32), pltpu.VMEM((mid, 3 * channels), F32)],
        flops=1 << 31,
    )(frames_in, upstream, spatial_weight, turned)
    edge, frame, acc = lax.optimization_barrier((edge, frame, acc))
    swapped = lax.ppermute(jnp.concatenate([edge, frame], 0), "chan", ring(2, 1))
    hid, grad, xp, up, keep, send = call(
        functools.partial(grads_kernel, dims),
        "weight_grads",
        [
            sds(cells, BF16),
            sds(cells, BF16),
            sds(xp_shape, BF16),
            sds(up_shape, BF16),
            sds((size, LANES), F32),
            sds((size, LANES), BF16 if axial_count == 2 else F32),
        ],
        10,
        16,
        [
            pltpu.VMEM((2 * edge_count, channels, width), BF16),
            pltpu.VMEM(total, F32),
            pltpu.VMEM((2 * size, LANES), F32),
        ],
    )(hid, grad, acc, xp, up, edge, frame, swapped, w_taps, w_act)

    got = lax.ppermute(send, "axial", ring(2, 1)) if axial_count == 2 else None

    out_own, out_lo, out_hi, ig_own, ig_lo, ig_hi = call(
        functools.partial(fields_kernel, dims),
        "field_products",
        [
            sds(own_shape, F32),
            sds((1, rows, own_c, width), BF16),
            sds((1, rows, own_c, width), BF16),
            sds(own_shape, F32),
            sds((frames, own_c, width), BF16),
            sds((frames, own_c, width), BF16),
        ],
        6,
        16,
        [
            pltpu.VMEM((3 * mid, 3 * channels), F32),
            pltpu.VMEM((mid, 3 * channels), F32),
            pltpu.VMEM((3 * own_c, 2 * mid), BF16),
            pltpu.VMEM((9 * own_c, 2 * mid), BF16),
            pltpu.VMEM((frames, rows + 2, own_c, width), F32),
        ],
        flops=1 << 31,
    )(hid, grad, xp, up, weights, weights_other)
    if got is not None:
        got, out_lo, out_hi, ig_lo, ig_hi = lax.optimization_barrier((got, out_lo, out_hi, ig_lo, ig_hi))

    from_hi = lax.ppermute(out_lo, "tm", ring(tm_count, -1))
    from_lo = lax.ppermute(out_hi, "tm", ring(tm_count, 1))
    if axial_count == 2:
        ig_from_lo = ig_from_hi = lax.ppermute(jnp.where(axial == 0, ig_hi, ig_lo), "axial", ring(2, 1))
    else:
        ig_from_hi = lax.ppermute(ig_lo, "axial", ring(axial_count, -1))
        ig_from_lo = lax.ppermute(ig_hi, "axial", ring(axial_count, 1))

    if axial_count == 2 and tm_count & (tm_count - 1) == 0:
        mine = lax.optimization_barrier((keep + got.astype(F32)).astype(BF16))
        stride = 1
        while stride < tm_count:
            mine = lax.optimization_barrier(mine + lax.ppermute(mine, "tm", pairs(tm_count, stride)))
            stride *= 2
        other = lax.ppermute(mine, "axial", ring(2, 1))
    else:
        odd = lax.rem(axial, 2) == 1
        low, high = jnp.where(odd, send, keep), jnp.where(odd, keep, send)
        low, high = lax.psum((low, high), ("tm", "axial"))
        mine, other = jnp.where(odd, high, low), jnp.where(odd, low, high)

    output, input_grad = call(
        functools.partial(outputs_kernel, axial_count),
        "outputs",
        [sds(own_shape, BF16), sds(own_shape, BF16)],
        6,
        4,
        flops=1 << 29,
    )(out_own, from_lo, from_hi, ig_own, ig_from_lo, ig_from_hi)
    spatial_grad, temporal_grad = call(
        unpack_kernel,
        "unpack",
        [sds((3, 3, channels, mid), F32), sds((3, channels, mid), F32)],
        2,
        4,
        [pltpu.VMEM((2 * size, LANES), F32), pltpu.VMEM((3 * channels, 4 * mid), F32)],
    )(mine, other)
    return output, input_grad, spatial_grad, jnp.swapaxes(temporal_grad, 1, 2)


def solution(mesh):
    placed = (
        P(("parts", "tm"), "axial", None, None),
        P("parts", None, None, "chan"),
        P("parts", "chan", None),
        P(("parts", "tm"), "axial", None, None),
    )
    return jax.shard_map(
        shards,
        mesh=mesh,
        in_specs=placed,
        out_specs=(
            P(("parts", "tm"), "axial", "chan", None),
            P(("parts", "tm"), "axial", "chan", None),
            P("parts", None, None, "chan"),
            P("parts", "chan", None),
        ),
        check_vma=False,
    )
```

```python
import functools
import math

import jax
import jax.numpy as jnp
from jax import lax
from jax.experimental import pallas as pl
from jax.experimental.pallas import tpu as pltpu
from jax.sharding import PartitionSpec as P

F32 = jnp.float32
BF16 = jnp.bfloat16
LANES = 128
HBM = pl.BlockSpec(memory_space=pltpu.HBM)
VMEM = pl.BlockSpec(memory_space=pltpu.VMEM)


def ring(count, step):
    return [(i, (i + step) % count) for i in range(count)]


def pairs(count, stride):
    return [(i, i ^ stride) for i in range(count)]


def facing(count):
    order = []
    for i in range(count):
        order += [(2 * i, 2 * ((i - 1) % count) + 1), (2 * i + 1, 2 * ((i + 1) % count))]
    return order


def dot(a, b):
    return jnp.dot(a, b, preferred_element_type=F32)


def dot_nt(a, b):
    return lax.dot_general(a, b, (((1,), (1,)), ((), ())), preferred_element_type=F32)


def moved(value, step):
    width = value.shape[1]
    column = lax.broadcasted_iota(jnp.int32, value.shape, 1)
    edge = 0 if step > 0 else width - 1
    return jnp.where(column == edge, 0.0, pltpu.roll(value, step % width, 1))


def pieces(depth, total):
    blocks, row = [], 0
    for first in range(0, total - total % LANES, LANES):
        blocks.append((row, 0, 0, first, depth, LANES))
        row += depth
    rest = total % LANES
    if rest:
        fold = LANES // rest
        if LANES % rest or depth % (8 * fold):
            fold = 1
        part = depth // fold
        for g in range(fold):
            blocks.append((row, g * rest, g * part, total - rest, part, rest))
        row += part
    return blocks, row


def half_rows(depth, total):
    return -(-pieces(depth, total)[1] // 32) * 16


def stage_kernel(split, x, u, edge, frame, sems):
    frames, rows = x.shape[:2]
    core = lax.axis_index("chan")
    if split:
        row = jnp.where(lax.axis_index("axial") == 0, rows - 1, 0)
        picked = pl.ds(core * (frames // 2), frames // 2)
    else:
        row = core * (rows - 1)
        picked = pl.ds(0, frames)
    copies = [
        pltpu.make_async_copy(u.at[core * (frames - 1)], frame, sems.at[0]),
        pltpu.make_async_copy(x.at[picked, row], edge, sems.at[1]),
    ]
    for copy in copies:
        copy.start()
    for copy in copies:
        copy.wait()


def prepare(sw, tw, wf, twf):
    channels, mid = tw.shape[1:]
    for j in range(3):
        wf[j * mid : (j + 1) * mid] = sw[:, j].reshape(3 * channels, mid).astype(F32).T
    twf[...] = jnp.concatenate([tw[k].astype(F32) for k in (2, 1, 0)], 0).T
    return wf[...].astype(BF16), twf[...].astype(BF16)


def activations(w_taps, w_act, field, cot, width):
    mid = w_act.shape[0]
    taps = dot(w_taps, field)
    act = dot(w_act, cot)
    hids, grads = [], []
    for first in range(0, field.shape[1], width):
        cols = slice(first, first + width)
        pre = taps[mid : 2 * mid, cols] + moved(taps[:mid, cols], 1) + moved(taps[2 * mid :, cols], -1)
        s = 0.5 * jnp.tanh(0.5 * pre) + 0.5
        hids.append(pre * s)
        grads.append(act[:, cols] * s * (1.0 + pre * (1.0 - s)))
    return hids, grads


def gathered(xp, up, h, picked):
    depth = 3 * xp.shape[2]
    width = xp.shape[3]
    field = jnp.concatenate([xp[f, pl.ds(h, 3)].reshape(depth, width) for f in picked], 1)
    cot = jnp.concatenate([jnp.concatenate([up[f + d, h] for d in range(3)], 0) for f in picked], 1)
    return field, cot


def inner_rows(axial_count, rows):
    if axial_count == 2:
        low = lax.axis_index("axial") == 0
        return jnp.where(low, 0, 1), rows - 1, [jnp.where(low, rows - 1, 0)]
    return 1, rows - 2, [0, rows - 1]


def cell_grads(xp, up, w_taps, w_act, groups, store):
    fields, cots, shifts, owns = [], [], [], []
    width = xp.shape[3]
    for h, picked in groups:
        field, cot = gathered(xp, up, h, picked)
        hids, grads = activations(w_taps, w_act, field, cot, width)
        shifts.append(
            jnp.concatenate(
                [
                    jnp.concatenate([moved(v, -1) for v in grads], 1),
                    jnp.concatenate(grads, 1),
                    jnp.concatenate([moved(v, 1) for v in grads], 1),
                ],
                0,
            ).astype(BF16)
        )
        hids = [v.astype(BF16) for v in hids]
        owns.append(jnp.concatenate(hids, 1))
        for f, hid, grad in zip(picked, hids, grads):
            store(h, f, hid, grad.astype(BF16))
        fields.append(field)
        cots.append(cot)
    return (
        dot_nt(jnp.concatenate(fields, 1), jnp.concatenate(shifts, 1)),
        dot_nt(jnp.concatenate(cots, 1), jnp.concatenate(owns, 1)),
    )


def inner_kernel(dims, *refs):
    frames, rows, channels, width, mid, own_c, rank_count, axial_count, group = dims
    x, u, sw, tw = refs[:4]
    hid_out, grad_out, acc_out, xp, up, taps_out, act_out, wf, twf = refs[4:]
    for f in range(frames):
        for at in (0, rows + 1):
            xp[f, at] = jnp.zeros((channels, width), BF16)
        for h in range(rows):
            xp[f, h + 1] = x[f, h]
            up[f + 1, h] = u[f, h]
    for at in (0, frames + 1):
        up[at] = jnp.zeros(up.shape[1:], BF16)
    w_taps, w_act = prepare(sw, tw, wf, twf)
    taps_out[...] = w_taps
    act_out[...] = w_act

    first, count, _ = inner_rows(axial_count, rows)

    def store(h, f, hid, grad):
        hid_out[h - first, f - 1] = hid
        grad_out[h - first, f - 1] = grad

    groups = [(first + i, (f, f + 1)) for i in range(count) for f in range(1, frames - 1, 2)]
    w_part, t_part = cell_grads(xp, up, w_taps, w_act, groups, store)
    acc_out[:, : 3 * mid] = w_part
    acc_out[:, 3 * mid :] = t_part


def grads_kernel(dims, *refs):
    frames, rows, channels, width, mid, own_c, rank_count, axial_count, group = dims
    hid_in, grad_in, acc_in, x, u, edge, frame, swapped, taps_in, act_in = refs[:10]
    hid_out, grad_out, xp, up, keep, send, edges, acc, packed = refs[10:]
    axial = lax.axis_index("axial")
    core = lax.axis_index("chan")
    w_taps, w_act = taps_in[...], act_in[...]

    has_lo = (axial > 0).astype(BF16)
    has_hi = (axial < axial_count - 1).astype(BF16)
    part = edge.shape[0]
    edges[pl.ds(core * part, part)] = edge[...]
    edges[pl.ds((1 - core) * part, part)] = swapped[0:part]
    at_hi = 2 * part - frames
    for f in range(frames):
        xp[f, 0] = edges[f] * has_lo
        xp[f, rows + 1] = edges[at_hi + f] * has_hi
        for h in range(rows):
            xp[f, h + 1] = x[f, h + 1]
            up[f + 1, h] = u[f + 1, h]
    up[core * (frames + 1)] = frame[...]
    up[(1 - core) * (frames + 1)] = swapped[part:]

    first, count, others = inner_rows(axial_count, rows)

    def store(h, f, hid, grad):
        hid_out[h, f] = hid
        grad_out[h, f] = grad

    for i in range(count):
        for f in range(1, frames - 1):
            store(first + i, f, hid_in[i, f - 1], grad_in[i, f - 1])
    groups = [(first + i, (0, frames - 1)) for i in range(count)]
    groups += [(h, (f, f + 1)) for h in others for f in range(0, frames, 2)]
    w_part, t_part = cell_grads(xp, up, w_taps, w_act, groups, store)
    factor = 1.0 / math.sqrt(frames * rows * width * rank_count)
    acc[:, : 3 * mid] = (acc_in[:, : 3 * mid] + w_part) * factor
    acc[:, 3 * mid :] = (acc_in[:, 3 * mid :] + t_part) * factor

    blocks, used = pieces(*acc.shape)
    size = packed.shape[0] // 2
    packed[used:] = jnp.zeros((2 * size - used, LANES), F32)
    for at, lane, source, column, depth, total in blocks:
        packed[at : at + depth, lane : lane + total] = acc[source : source + depth, column : column + total]
    mine = lax.rem(axial, 2)
    keep[...] = packed[pl.ds(pl.multiple_of(mine * size, 16), size)]
    send[...] = packed[pl.ds(pl.multiple_of((1 - mine) * size, 16), size)].astype(send.dtype)


def fields_kernel(dims, *refs):
    frames, rows, channels, width, mid, own_c, rank_count, axial_count, group = dims
    hid_in, grad_in, xp, up, sw, tw, sw_other, tw_other = refs[:8]
    out, out_lo, out_hi, ig, ig_lo, ig_hi, wf, twf, twt, wg, ig_acc = refs[8:]
    core = lax.axis_index("chan")
    first_c = pl.multiple_of(core * own_c, own_c)
    own = pl.ds(first_c, own_c)
    w_taps, w_act = prepare(sw_other, tw_other, wf, twf)
    for k in range(3):
        twt[k * own_c : (k + 1) * own_c] = jnp.concatenate(
            [w[k, own].astype(F32) for w in (tw, tw_other)], 1
        ).astype(BF16)
    for i in range(3):
        for j in range(3):
            at = (i * 3 + j) * own_c
            wg[at : at + own_c] = jnp.concatenate([w[i, j, own].astype(F32) for w in (sw, sw_other)], 1).astype(BF16)
    ig_acc[...] = jnp.zeros_like(ig_acc)

    def row(h, carry):
        out_terms = {}
        for first in range(0, frames, group):
            field, cot = gathered(xp, up, h, range(first, first + group))
            hids, grads = activations(w_taps, w_act, field, cot, width)
            picked = range(first, first + group)
            hid = [jnp.concatenate([hid_in[h, f].astype(F32), v], 0) for f, v in zip(picked, hids)]
            grad = [jnp.concatenate([grad_in[h, f].astype(F32), v], 0) for f, v in zip(picked, grads)]
            y_out = dot(twt[...], jnp.concatenate(hid, 1).astype(BF16))
            y_in = dot(wg[...], jnp.concatenate(grad, 1).astype(BF16))
            for g in range(group):
                f = first + g
                cols = slice(g * width, (g + 1) * width)
                for k in range(3):
                    out_terms.setdefault(f - k + 1, []).append(y_out[k * own_c : (k + 1) * own_c, cols])
                for i in range(3):
                    at = i * 3 * own_c
                    ig_acc[f, h + i] += (
                        y_in[at + own_c : at + 2 * own_c, cols]
                        + moved(y_in[at : at + own_c, cols], -1)
                        + moved(y_in[at + 2 * own_c : at + 3 * own_c, cols], 1)
                    )
        for f, terms in out_terms.items():
            total = functools.reduce(lambda a, b: a + b, terms)
            if f < 0:
                out_lo[0, h] = total.astype(BF16)
            elif f >= frames:
                out_hi[0, h] = total.astype(BF16)
            else:
                out[f, h] = total
        return carry

    lax.fori_loop(0, rows, row, 0)
    for f in range(frames):
        ig_lo[f] = ig_acc[f, 0].astype(BF16)
        ig_hi[f] = ig_acc[f, rows + 1].astype(BF16)
        for h in range(rows):
            ig[f, h] = ig_acc[f, h + 1]


def outputs_kernel(axial_count, own, from_lo, from_hi, ig_own, ig_from_lo, ig_from_hi, out, ig):
    frames, rows = own.shape[:2]
    axial = lax.axis_index("axial")
    has_lo = (axial > 0).astype(F32)
    has_hi = (axial < axial_count - 1).astype(F32)
    for f in range(frames):
        for h in range(rows):
            total = own[f, h]
            if f == 0:
                total = total + from_lo[0, h].astype(F32)
            if f == frames - 1:
                total = total + from_hi[0, h].astype(F32)
            out[f, h] = total.astype(BF16)
            total = ig_own[f, h]
            if h == 0:
                total = total + ig_from_lo[f].astype(F32) * has_lo
            if h == rows - 1:
                total = total + ig_from_hi[f].astype(F32) * has_hi
            ig[f, h] = total.astype(BF16)


def unpack_kernel(mine, other, sg, tg, packed, acc):
    channels, mid = tg.shape[1:]
    size = mine.shape[0]
    half = lax.rem(lax.axis_index("axial"), 2)
    packed[pl.ds(pl.multiple_of(half * size, 16), size)] = mine[...].astype(F32)
    packed[pl.ds(pl.multiple_of((1 - half) * size, 16), size)] = other[...].astype(F32)
    for at, lane, source, column, depth, total in pieces(*acc.shape)[0]:
        acc[source : source + depth, column : column + total] = packed[at : at + depth, lane : lane + total]
    for i in range(3):
        rows = slice(i * channels, (i + 1) * channels)
        for j in range(3):
            sg[i, j] = acc[rows, j * mid : (j + 1) * mid]
        tg[2 - i] = acc[rows, 3 * mid :]


def call(kernel, name, out_shape, count, limit, scratch=(), in_specs=None, flops=0):
    return pl.pallas_call(
        kernel,
        out_shape=out_shape,
        in_specs=in_specs or [VMEM] * count,
        out_specs=[VMEM] * len(out_shape),
        scratch_shapes=list(scratch),
        compiler_params=pltpu.CompilerParams(vmem_limit_bytes=int(limit * 1024 * 1024)),
        cost_estimate=pl.CostEstimate(flops=flops, bytes_accessed=1 << 20, transcendentals=0) if flops else None,
        name=name,
    )


def shards(frames_in, spatial_weight, temporal_weight, upstream):
    frames, rows, channels, width = frames_in.shape
    mid = temporal_weight.shape[1]
    axial_count = lax.axis_size("axial")
    tm_count = lax.axis_size("tm")
    core_count = lax.axis_size("chan")
    rank_count = tm_count * axial_count
    axial = lax.axis_index("axial")
    own_c = channels // core_count
    group = 2 if frames % 2 == 0 else 1
    dims = (frames, rows, channels, width, mid, own_c, rank_count, axial_count, group)
    size = half_rows(3 * channels, 4 * mid)
    sds = jax.ShapeDtypeStruct

    split = axial_count == 2 and frames % 2 == 0
    edge_count = frames // 2 if split else frames
    turned = jnp.swapaxes(temporal_weight, 1, 2)
    edge, frame = call(
        functools.partial(stage_kernel, split),
        "stage",
        [sds((edge_count, channels, width), BF16), sds((rows, channels, width), BF16)],
        2,
        60,
        [pltpu.SemaphoreType.DMA((2,))],
        [HBM] * 2,
    )(frames_in, upstream)
    frame = lax.ppermute(frame, ("tm", "chan"), facing(tm_count))
    if split:
        edge = lax.ppermute(edge, "axial", ring(2, 1))
    else:
        edge = lax.ppermute(edge, ("axial", "chan"), facing(axial_count))
    sw_other = lax.ppermute(spatial_weight, "chan", ring(2, 1))
    tw_other = lax.ppermute(turned, "chan", ring(2, 1))

    own_shape = (frames, rows, own_c, width)
    inner = (inner_rows(axial_count, rows)[1], frames - 2, mid, width)
    cells = (rows, frames, mid, width)
    xp_shape = (frames, rows + 2, channels, width)
    up_shape = (frames + 2, rows, channels, width)
    total = (3 * channels, 4 * mid)
    hid, grad, acc, xp, up, w_taps, w_act = call(
        functools.partial(inner_kernel, dims),
        "inner_cells",
        [
            sds(inner, BF16),
            sds(inner, BF16),
            sds(total, F32),
            sds(xp_shape, BF16),
            sds(up_shape, BF16),
            sds((3 * mid, 3 * channels), BF16),
            sds((mid, 3 * channels), BF16),
        ],
        4,
        16,
        [pltpu.VMEM((3 * mid, 3 * channels), F32), pltpu.VMEM((mid, 3 * channels), F32)],
        flops=1 << 31,
    )(frames_in, upstream, spatial_weight, turned)
    edge, frame, acc = lax.optimization_barrier((edge, frame, acc))
    swapped = lax.ppermute(jnp.concatenate([edge, frame], 0), "chan", ring(2, 1))
    hid, grad, xp, up, keep, send = call(
        functools.partial(grads_kernel, dims),
        "weight_grads",
        [
            sds(cells, BF16),
            sds(cells, BF16),
            sds(xp_shape, BF16),
            sds(up_shape, BF16),
            sds((size, LANES), F32),
            sds((size, LANES), BF16 if axial_count == 2 else F32),
        ],
        10,
        16,
        [
            pltpu.VMEM((2 * edge_count, channels, width), BF16),
            pltpu.VMEM(total, F32),
            pltpu.VMEM((2 * size, LANES), F32),
        ],
    )(hid, grad, acc, xp, up, edge, frame, swapped, w_taps, w_act)

    got = lax.ppermute(send, "axial", ring(2, 1)) if axial_count == 2 else None

    out_own, out_lo, out_hi, ig_own, ig_lo, ig_hi = call(
        functools.partial(fields_kernel, dims),
        "field_products",
        [
            sds(own_shape, F32),
            sds((1, rows, own_c, width), BF16),
            sds((1, rows, own_c, width), BF16),
            sds(own_shape, F32),
            sds((frames, own_c, width), BF16),
            sds((frames, own_c, width), BF16),
        ],
        8,
        16,
        [
            pltpu.VMEM((3 * mid, 3 * channels), F32),
            pltpu.VMEM((mid, 3 * channels), F32),
            pltpu.VMEM((3 * own_c, 2 * mid), BF16),
            pltpu.VMEM((9 * own_c, 2 * mid), BF16),
            pltpu.VMEM((frames, rows + 2, own_c, width), F32),
        ],
        flops=1 << 31,
    )(hid, grad, xp, up, spatial_weight, turned, sw_other, tw_other)
    if got is not None:
        got, out_lo, out_hi, ig_lo, ig_hi = lax.optimization_barrier((got, out_lo, out_hi, ig_lo, ig_hi))

    from_hi = lax.ppermute(out_lo, "tm", ring(tm_count, -1))
    from_lo = lax.ppermute(out_hi, "tm", ring(tm_count, 1))
    if axial_count == 2:
        ig_from_lo = ig_from_hi = lax.ppermute(jnp.where(axial == 0, ig_hi, ig_lo), "axial", ring(2, 1))
    else:
        ig_from_hi = lax.ppermute(ig_lo, "axial", ring(axial_count, -1))
        ig_from_lo = lax.ppermute(ig_hi, "axial", ring(axial_count, 1))

    if axial_count == 2 and tm_count & (tm_count - 1) == 0:
        mine = lax.optimization_barrier((keep + got.astype(F32)).astype(BF16))
        stride = 1
        while stride < tm_count:
            mine = lax.optimization_barrier(mine + lax.ppermute(mine, "tm", pairs(tm_count, stride)))
            stride *= 2
        other = lax.ppermute(mine, "axial", ring(2, 1))
    else:
        odd = lax.rem(axial, 2) == 1
        low, high = jnp.where(odd, send, keep), jnp.where(odd, keep, send)
        low, high = lax.psum((low, high), ("tm", "axial"))
        mine, other = jnp.where(odd, high, low), jnp.where(odd, low, high)

    output, input_grad = call(
        functools.partial(outputs_kernel, axial_count),
        "outputs",
        [sds(own_shape, BF16), sds(own_shape, BF16)],
        6,
        4,
        flops=1 << 29,
    )(out_own, from_lo, from_hi, ig_own, ig_from_lo, ig_from_hi)
    spatial_grad, temporal_grad = call(
        unpack_kernel,
        "unpack",
        [sds((3, 3, channels, mid), F32), sds((3, channels, mid), F32)],
        2,
        4,
        [pltpu.VMEM((2 * size, LANES), F32), pltpu.VMEM((3 * channels, 4 * mid), F32)],
    )(mine, other)
    return output, input_grad, spatial_grad, jnp.swapaxes(temporal_grad, 1, 2)


def solution(mesh):
    placed = (
        P(("parts", "tm"), "axial", None, None),
        P("parts", None, None, "chan"),
        P("parts", "chan", None),
        P(("parts", "tm"), "axial", None, None),
    )
    return jax.shard_map(
        shards,
        mesh=mesh,
        in_specs=placed,
        out_specs=(
            P(("parts", "tm"), "axial", "chan", None),
            P(("parts", "tm"), "axial", "chan", None),
            P("parts", None, None, "chan"),
            P("parts", "chan", None),
        ),
        check_vma=False,
    )
```

```python
import functools
import math

import jax
import jax.numpy as jnp
from jax import lax
from jax.experimental import pallas as pl
from jax.experimental.pallas import tpu as pltpu
from jax.sharding import PartitionSpec as P

F32 = jnp.float32
BF16 = jnp.bfloat16
LANES = 128
HBM = pl.BlockSpec(memory_space=pltpu.HBM)
VMEM = pl.BlockSpec(memory_space=pltpu.VMEM)


def ring(count, step):
    return [(i, (i + step) % count) for i in range(count)]


def pairs(count, stride):
    return [(i, i ^ stride) for i in range(count)]


def facing(count):
    order = []
    for i in range(count):
        order += [(2 * i, 2 * ((i - 1) % count) + 1), (2 * i + 1, 2 * ((i + 1) % count))]
    return order


def dot(a, b):
    return jnp.dot(a, b, preferred_element_type=F32)


def dot_nt(a, b):
    return lax.dot_general(a, b, (((1,), (1,)), ((), ())), preferred_element_type=F32)


def moved(value, step):
    width = value.shape[1]
    column = lax.broadcasted_iota(jnp.int32, value.shape, 1)
    edge = 0 if step > 0 else width - 1
    return jnp.where(column == edge, 0.0, pltpu.roll(value, step % width, 1))


def pieces(depth, total):
    blocks, row = [], 0
    for first in range(0, total - total % LANES, LANES):
        blocks.append((row, 0, 0, first, depth, LANES))
        row += depth
    rest = total % LANES
    if rest:
        fold = LANES // rest
        if LANES % rest or depth % (8 * fold):
            fold = 1
        part = depth // fold
        for g in range(fold):
            blocks.append((row, g * rest, g * part, total - rest, part, rest))
        row += part
    return blocks, row


def padded(count):
    return -(-count // 16) * 16


def with_rows(value, count):
    if value.shape[0] == count:
        return value
    return jnp.concatenate([value, jnp.zeros((count - value.shape[0], value.shape[1]), value.dtype)], 0)


def half_rows(depth, total):
    return -(-pieces(depth, total)[1] // 32) * 16


def stage_kernel(split, x, u, edge, frame, sems):
    frames, rows = x.shape[:2]
    core = lax.axis_index("chan")
    if split:
        row = jnp.where(lax.axis_index("axial") == 0, rows - 1, 0)
        picked = pl.ds(core * (frames // 2), frames // 2)
    else:
        row = core * (rows - 1)
        picked = pl.ds(0, frames)
    copies = [
        pltpu.make_async_copy(u.at[core * (frames - 1)], frame, sems.at[0]),
        pltpu.make_async_copy(x.at[picked, row], edge, sems.at[1]),
    ]
    for copy in copies:
        copy.start()
    for copy in copies:
        copy.wait()


def prepare(sw, tw, wf, twf):
    channels, mid = tw.shape[1:]
    for j in range(3):
        wf[j * mid : (j + 1) * mid] = sw[:, j].reshape(3 * channels, mid).astype(F32).T
    twf[...] = jnp.concatenate([tw[k].astype(F32) for k in (2, 1, 0)], 0).T
    return wf[...].astype(BF16), twf[...].astype(BF16)


def activations(w_taps, w_act, field, cot, width):
    mid = w_act.shape[0]
    taps = dot(w_taps, field)
    act = dot(w_act, cot)
    hids, grads = [], []
    for first in range(0, field.shape[1], width):
        cols = slice(first, first + width)
        pre = taps[mid : 2 * mid, cols] + moved(taps[:mid, cols], 1) + moved(taps[2 * mid :, cols], -1)
        s = 0.5 * jnp.tanh(0.5 * pre) + 0.5
        hids.append(pre * s)
        grads.append(act[:, cols] * s * (1.0 + pre * (1.0 - s)))
    return hids, grads


def gathered(xp, up, h, picked):
    depth = 3 * xp.shape[2]
    width = xp.shape[3]
    field = jnp.concatenate([xp[f, pl.ds(h, 3)].reshape(depth, width) for f in picked], 1)
    cot = jnp.concatenate([jnp.concatenate([up[f + d, h] for d in range(3)], 0) for f in picked], 1)
    return field, cot


def inner_rows(axial_count, rows):
    if axial_count == 2:
        low = lax.axis_index("axial") == 0
        return jnp.where(low, 0, 1), rows - 1, [jnp.where(low, rows - 1, 0)]
    return 1, rows - 2, [0, rows - 1]


def cell_grads(xp, up, w_taps, w_act, groups, store):
    fields, cots, shifts, owns = [], [], [], []
    width = xp.shape[3]
    for h, picked in groups:
        field, cot = gathered(xp, up, h, picked)
        hids, grads = activations(w_taps, w_act, field, cot, width)
        shifts.append(
            jnp.concatenate(
                [
                    jnp.concatenate([moved(v, -1) for v in grads], 1),
                    jnp.concatenate(grads, 1),
                    jnp.concatenate([moved(v, 1) for v in grads], 1),
                ],
                0,
            ).astype(BF16)
        )
        hids = [with_rows(v, padded(v.shape[0])).astype(BF16) for v in hids]
        owns.append(jnp.concatenate(hids, 1))
        for f, hid, grad in zip(picked, hids, grads):
            store(h, f, hid, with_rows(grad, padded(grad.shape[0])).astype(BF16))
        fields.append(field)
        cots.append(cot)
    return (
        dot_nt(jnp.concatenate(fields, 1), jnp.concatenate(shifts, 1)),
        dot_nt(jnp.concatenate(cots, 1), jnp.concatenate(owns, 1))[:, : w_act.shape[0]],
    )


def inner_kernel(dims, *refs):
    frames, rows, channels, width, mid, own_c, rank_count, axial_count, group = dims
    x, u, sw, tw = refs[:4]
    hid_out, grad_out, acc_out, xp, up, taps_out, act_out, wf, twf = refs[4:]
    for f in range(frames):
        for at in (0, rows + 1):
            xp[f, at] = jnp.zeros((channels, width), BF16)
        for h in range(rows):
            xp[f, h + 1] = x[f, h]
            up[f + 1, h] = u[f, h]
    for at in (0, frames + 1):
        up[at] = jnp.zeros(up.shape[1:], BF16)
    w_taps, w_act = prepare(sw, tw, wf, twf)
    taps_out[...] = w_taps
    act_out[...] = w_act

    first, count, _ = inner_rows(axial_count, rows)

    def store(h, f, hid, grad):
        hid_out[h - first, f - 1] = hid
        grad_out[h - first, f - 1] = grad

    groups = [(first + i, (f, f + 1)) for i in range(count) for f in range(1, frames - 1, 2)]
    w_part, t_part = cell_grads(xp, up, w_taps, w_act, groups, store)
    acc_out[:, : 3 * mid] = w_part
    acc_out[:, 3 * mid :] = t_part


def grads_kernel(dims, *refs):
    frames, rows, channels, width, mid, own_c, rank_count, axial_count, group = dims
    hid_in, grad_in, acc_in, x, u, edge, frame, swapped, taps_in, act_in = refs[:10]
    hid_out, grad_out, xp, up, half_0, half_1, edges, acc, packed = refs[10:]
    axial = lax.axis_index("axial")
    core = lax.axis_index("chan")
    w_taps, w_act = taps_in[...], act_in[...]

    has_lo = (axial > 0).astype(BF16)
    has_hi = (axial < axial_count - 1).astype(BF16)
    part = edge.shape[0]
    edges[pl.ds(core * part, part)] = edge[...]
    edges[pl.ds((1 - core) * part, part)] = swapped[0:part]
    at_hi = 2 * part - frames
    for f in range(frames):
        xp[f, 0] = edges[f] * has_lo
        xp[f, rows + 1] = edges[at_hi + f] * has_hi
        for h in range(rows):
            xp[f, h + 1] = x[f, h + 1]
            up[f + 1, h] = u[f + 1, h]
    up[core * (frames + 1)] = frame[...]
    up[(1 - core) * (frames + 1)] = swapped[part:]

    first, count, others = inner_rows(axial_count, rows)

    def store(h, f, hid, grad):
        hid_out[h, f] = hid
        grad_out[h, f] = grad

    for i in range(count):
        for f in range(1, frames - 1):
            store(first + i, f, hid_in[i, f - 1], grad_in[i, f - 1])
    groups = [(first + i, (0, frames - 1)) for i in range(count)]
    groups += [(h, (f, f + 1)) for h in others for f in range(0, frames, 2)]
    w_part, t_part = cell_grads(xp, up, w_taps, w_act, groups, store)
    factor = 1.0 / math.sqrt(frames * rows * width * rank_count)
    acc[:, : 3 * mid] = (acc_in[:, : 3 * mid] + w_part) * factor
    acc[:, 3 * mid :] = (acc_in[:, 3 * mid :] + t_part) * factor

    blocks, used = pieces(*acc.shape)
    size = packed.shape[0] // 2
    packed[used:] = jnp.zeros((2 * size - used, LANES), F32)
    for at, lane, source, column, depth, total in blocks:
        packed[at : at + depth, lane : lane + total] = acc[source : source + depth, column : column + total]
    half_0[...] = packed[:size].astype(half_0.dtype)
    half_1[...] = packed[size:].astype(half_1.dtype)


def others_kernel(dims, *refs):
    frames, rows, channels, width, mid, own_c, rank_count, axial_count, group = dims
    xp, up, sw, tw, hid_out, grad_out, wf, twf = refs
    w_taps, w_act = prepare(sw, tw, wf, twf)
    for h in range(rows):
        for first in range(0, frames, group):
            picked = range(first, first + group)
            field, cot = gathered(xp, up, h, picked)
            for f, hid, grad in zip(picked, *activations(w_taps, w_act, field, cot, width)):
                hid_out[h, f] = with_rows(hid, padded(mid)).astype(BF16)
                grad_out[h, f] = with_rows(grad, padded(mid)).astype(BF16)


def fields_kernel(dims, fast, *refs):
    frames, rows, channels, width, mid, own_c, rank_count, axial_count, group = dims
    hid_in, grad_in, hid_other, grad_other, sw, tw, sw_other, tw_other = refs[:8]
    out, out_a, out_b, ig, ig_a, ig_b, twt, wg, ig_acc, out_edges = refs[8:]
    own = pl.ds(pl.multiple_of(lax.axis_index("chan") * own_c, own_c), own_c)
    blank = jnp.zeros((own_c, padded(mid) - mid), F32)

    def both(a, b):
        return jnp.concatenate([a.astype(F32), blank, b.astype(F32), blank], 1).astype(BF16)

    for k in range(3):
        twt[k * own_c : (k + 1) * own_c] = both(tw[k, own], tw_other[k, own])
    for i in range(3):
        for j in range(3):
            at = (i * 3 + j) * own_c
            wg[at : at + own_c] = both(sw[i, j, own], sw_other[i, j, own])
    w_out, w_in = twt[...], wg[...]

    for h in range(rows):
        out_terms = {}
        for first in range(0, frames, group):
            picked = range(first, first + group)
            hid = jnp.concatenate([jnp.concatenate([hid_in[h, f], hid_other[h, f]], 0) for f in picked], 1)
            grad = jnp.concatenate([jnp.concatenate([grad_in[h, f], grad_other[h, f]], 0) for f in picked], 1)
            y_out = dot(w_out, hid)
            y_in = dot(w_in, grad)
            for g, f in enumerate(picked):
                cols = slice(g * width, (g + 1) * width)
                for k in range(3):
                    out_terms.setdefault(f - k + 1, []).append(y_out[k * own_c : (k + 1) * own_c, cols])
                for i in range(3):
                    at = i * 3 * own_c
                    total = (
                        y_in[at + own_c : at + 2 * own_c, cols]
                        + moved(y_in[at : at + own_c, cols], -1)
                        + moved(y_in[at + 2 * own_c : at + 3 * own_c, cols], 1)
                    )
                    if h == 0 or i == 2:
                        ig_acc[f, h + i] = total
                    else:
                        ig_acc[f, h + i] += total
        for f, terms in out_terms.items():
            total = functools.reduce(lambda a, b: a + b, terms)
            if f < 0:
                out_edges[0, h] = total.astype(BF16)
            elif f >= frames:
                out_edges[1, h] = total.astype(BF16)
            else:
                out[f, h] = total

    odd = lax.rem(lax.axis_index("tm"), 2) if fast else 1
    high = jnp.where(lax.axis_index("axial") == 0, rows + 1, 0) if fast else 0
    out_a[...] = out_edges[1 - odd]
    out_b[...] = out_edges[odd]
    for f in range(frames):
        ig_a[f] = ig_acc[f, high].astype(BF16)
        ig_b[f] = ig_acc[f, rows + 1].astype(BF16)
        for h in range(rows):
            ig[f, h] = ig_acc[f, h + 1]


def unpack(packed, acc, sg, tg):
    channels, mid = tg.shape[1:]
    for at, lane, source, column, depth, total in pieces(*acc.shape)[0]:
        acc[source : source + depth, column : column + total] = packed[at : at + depth, lane : lane + total]
    for i in range(3):
        rows = slice(i * channels, (i + 1) * channels)
        for j in range(3):
            sg[i, j] = acc[rows, j * mid : (j + 1) * mid]
        tg[2 - i] = acc[rows, 3 * mid :]


def add_edges(axial_count, own, from_lo, from_hi, ig_own, ig_from_lo, ig_from_hi, out, ig):
    frames, rows = own.shape[:2]
    axial = lax.axis_index("axial")
    has_lo = (axial > 0).astype(F32)
    has_hi = (axial < axial_count - 1).astype(F32)
    for f in range(frames):
        for h in range(rows):
            total = own[f, h]
            if f == 0:
                total = total + from_lo(h).astype(F32)
            if f == frames - 1:
                total = total + from_hi(h).astype(F32)
            out[f, h] = total.astype(BF16)
            total = ig_own[f, h]
            if h == 0:
                total = total + ig_from_lo(f).astype(F32) * has_lo
            if h == rows - 1:
                total = total + ig_from_hi(f).astype(F32) * has_hi
            ig[f, h] = total.astype(BF16)


def last_kernel(own, ig_own, half_0, got_0, half_1, got_1, got_a, out, ig, sg, tg, packed, acc, edges):
    frames, rows, own_c, width = own.shape
    size = half_0.shape[0]
    odd = lax.rem(lax.axis_index("tm"), 2)
    edges[1 - odd] = got_a[...]
    edges[odd] = got_1[size:].reshape(rows, own_c, width)
    add_edges(
        2,
        own,
        lambda h: edges[0, h],
        lambda h: edges[1, h],
        ig_own,
        lambda f: got_0[size + f * own_c : size + (f + 1) * own_c],
        lambda f: got_0[size + f * own_c : size + (f + 1) * own_c],
        out,
        ig,
    )
    packed[:size] = half_0[...].astype(F32) + got_0[:size].astype(F32)
    packed[size:] = half_1[...].astype(F32) + got_1[:size].astype(F32)
    unpack(packed, acc, sg, tg)


def last_kernel_general(axial_count, *refs):
    own, ig_own, half_0, half_1, from_lo, from_hi, ig_from_lo, ig_from_hi, out, ig, sg, tg, packed, acc, edges = refs
    add_edges(
        axial_count,
        own,
        lambda h: from_lo[h],
        lambda h: from_hi[h],
        ig_own,
        lambda f: ig_from_lo[f],
        lambda f: ig_from_hi[f],
        out,
        ig,
    )
    size = half_0.shape[0]
    packed[:size] = half_0[...]
    packed[size:] = half_1[...]
    unpack(packed, acc, sg, tg)


def call(kernel, name, out_shape, count, limit, scratch=(), in_specs=None, flops=0):
    return pl.pallas_call(
        kernel,
        out_shape=out_shape,
        in_specs=in_specs or [VMEM] * count,
        out_specs=[VMEM] * len(out_shape),
        scratch_shapes=list(scratch),
        compiler_params=pltpu.CompilerParams(vmem_limit_bytes=int(limit * 1024 * 1024)),
        cost_estimate=pl.CostEstimate(flops=flops, bytes_accessed=1 << 20, transcendentals=0) if flops else None,
        name=name,
    )


def shards(frames_in, spatial_weight, temporal_weight, upstream):
    frames, rows, channels, width = frames_in.shape
    mid = temporal_weight.shape[1]
    axial_count = lax.axis_size("axial")
    tm_count = lax.axis_size("tm")
    core_count = lax.axis_size("chan")
    rank_count = tm_count * axial_count
    axial = lax.axis_index("axial")
    own_c = channels // core_count
    group = 2 if frames % 2 == 0 else 1
    dims = (frames, rows, channels, width, mid, own_c, rank_count, axial_count, group)
    size = half_rows(3 * channels, 4 * mid)
    sds = jax.ShapeDtypeStruct

    split = axial_count == 2 and frames % 2 == 0
    edge_count = frames // 2 if split else frames
    turned = jnp.swapaxes(temporal_weight, 1, 2)
    edge, frame = call(
        functools.partial(stage_kernel, split),
        "stage",
        [sds((edge_count, channels, width), BF16), sds((rows, channels, width), BF16)],
        2,
        60,
        [pltpu.SemaphoreType.DMA((2,))],
        [HBM] * 2,
    )(frames_in, upstream)
    frame = lax.ppermute(frame, ("tm", "chan"), facing(tm_count))
    if split:
        edge = lax.ppermute(edge, "axial", ring(2, 1))
    else:
        edge = lax.ppermute(edge, ("axial", "chan"), facing(axial_count))
    sw_other = lax.ppermute(spatial_weight, "chan", ring(2, 1))
    tw_other = lax.ppermute(turned, "chan", ring(2, 1))

    own_shape = (frames, rows, own_c, width)
    inner = (inner_rows(axial_count, rows)[1], frames - 2, padded(mid), width)
    cells = (rows, frames, padded(mid), width)
    xp_shape = (frames, rows + 2, channels, width)
    up_shape = (frames + 2, rows, channels, width)
    total = (3 * channels, 4 * mid)
    forms = [pltpu.VMEM((3 * mid, 3 * channels), F32), pltpu.VMEM((mid, 3 * channels), F32)]
    fast = axial_count == 2 and tm_count == 4
    hid, grad, acc, xp, up, w_taps, w_act = call(
        functools.partial(inner_kernel, dims),
        "inner_cells",
        [
            sds(inner, BF16),
            sds(inner, BF16),
            sds(total, F32),
            sds(xp_shape, BF16),
            sds(up_shape, BF16),
            sds((3 * mid, 3 * channels), BF16),
            sds((mid, 3 * channels), BF16),
        ],
        4,
        16,
        forms,
        flops=1 << 31,
    )(frames_in, upstream, spatial_weight, turned)
    edge, frame, acc = lax.optimization_barrier((edge, frame, acc))
    swapped = lax.ppermute(jnp.concatenate([edge, frame], 0), "chan", ring(2, 1))
    half_type = BF16 if fast else F32
    hid, grad, xp, up, half_0, half_1 = call(
        functools.partial(grads_kernel, dims),
        "weight_grads",
        [
            sds(cells, BF16),
            sds(cells, BF16),
            sds(xp_shape, BF16),
            sds(up_shape, BF16),
            sds((size, LANES), half_type),
            sds((size, LANES), half_type),
        ],
        10,
        16,
        [
            pltpu.VMEM((2 * edge_count, channels, width), BF16),
            pltpu.VMEM(total, F32),
            pltpu.VMEM((2 * size, LANES), F32),
        ],
    )(hid, grad, acc, xp, up, edge, frame, swapped, w_taps, w_act)

    if fast:
        near, far = pairs(4, 1), [(0, 3), (1, 2), (2, 1), (3, 0)]
        got_0 = lax.ppermute(half_0, "tm", near)
        got_1 = lax.ppermute(half_1, "axial", ring(2, 1))

    hid_other, grad_other = call(
        functools.partial(others_kernel, dims),
        "other_cells",
        [sds(cells, BF16), sds(cells, BF16)],
        4,
        16,
        forms,
        flops=1 << 31,
    )(xp, up, sw_other, tw_other)

    if fast:
        got_0, got_1, hid_other = lax.optimization_barrier((got_0, got_1, hid_other))
        half_0, half_1 = lax.optimization_barrier((half_0 + got_0, half_1 + got_1))
        got_0 = lax.ppermute(half_0, "tm", pairs(4, 2))
        got_1 = lax.ppermute(half_1, "tm", near)

    own_shape = (frames, rows, own_c, width)
    out_edge, ig_edge = sds((rows, own_c, width), BF16), sds((frames, own_c, width), BF16)
    out_own, out_a, out_b, ig_own, ig_a, ig_b = call(
        functools.partial(fields_kernel, dims, fast),
        "field_products",
        [sds(own_shape, F32), out_edge, out_edge, sds(own_shape, F32), ig_edge, ig_edge],
        8,
        16,
        [
            pltpu.VMEM((3 * own_c, 2 * padded(mid)), BF16),
            pltpu.VMEM((9 * own_c, 2 * padded(mid)), BF16),
            pltpu.VMEM((frames, rows + 2, own_c, width), F32),
            pltpu.VMEM((2, rows, own_c, width), BF16),
        ],
        flops=1 << 31,
    )(hid, grad, hid_other, grad_other, spatial_weight, turned, sw_other, tw_other)

    outs = [
        sds(own_shape, BF16),
        sds(own_shape, BF16),
        sds((3, 3, channels, mid), F32),
        sds((3, channels, mid), F32),
    ]
    scratch = [
        pltpu.VMEM((2 * size, LANES), F32),
        pltpu.VMEM(total, F32),
        pltpu.VMEM((2, rows, own_c, width), BF16),
    ]
    if fast:
        got_0, got_1, out_a, out_b, ig_a = lax.optimization_barrier((got_0, got_1, out_a, out_b, ig_a))
        half_0, half_1 = lax.optimization_barrier((half_0 + got_0, half_1 + got_1))
        got_1 = lax.ppermute(jnp.concatenate([half_1, out_b.reshape(-1, width)], 0), "tm", far)
        got_0 = lax.ppermute(jnp.concatenate([half_0, ig_a.reshape(-1, width)], 0), "axial", ring(2, 1))
        got_a = lax.ppermute(out_a, "tm", near)
        results = call(last_kernel, "last", outs, 7, 8, scratch)(
            out_own, ig_own, half_0, got_0, half_1, got_1, got_a
        )
    else:
        half_0, half_1 = lax.psum((half_0, half_1), ("tm", "axial"))
        from_hi = lax.ppermute(out_a, "tm", ring(tm_count, -1))
        from_lo = lax.ppermute(out_b, "tm", ring(tm_count, 1))
        ig_from_hi = lax.ppermute(ig_a, "axial", ring(axial_count, -1))
        ig_from_lo = lax.ppermute(ig_b, "axial", ring(axial_count, 1))
        results = call(functools.partial(last_kernel_general, axial_count), "last", outs, 8, 8, scratch)(
            out_own, ig_own, half_0, half_1, from_lo, from_hi, ig_from_lo, ig_from_hi
        )
    output, input_grad, spatial_grad, temporal_grad = results
    return output, input_grad, spatial_grad, jnp.swapaxes(temporal_grad, 1, 2)


def solution(mesh):
    placed = (
        P(("parts", "tm"), "axial", None, None),
        P("parts", None, None, "chan"),
        P("parts", "chan", None),
        P(("parts", "tm"), "axial", None, None),
    )
    return jax.shard_map(
        shards,
        mesh=mesh,
        in_specs=placed,
        out_specs=(
            P(("parts", "tm"), "axial", "chan", None),
            P(("parts", "tm"), "axial", "chan", None),
            P("parts", None, None, "chan"),
            P("parts", "chan", None),
        ),
        check_vma=False,
    )
```

```python
import functools
import math

import jax
import jax.numpy as jnp
from jax import lax
from jax.experimental import pallas as pl
from jax.experimental.pallas import tpu as pltpu
from jax.sharding import PartitionSpec as P

F32 = jnp.float32
BF16 = jnp.bfloat16
LANES = 128
HBM = pl.BlockSpec(memory_space=pltpu.HBM)
VMEM = pl.BlockSpec(memory_space=pltpu.VMEM)


def ring(count, step):
    return [(i, (i + step) % count) for i in range(count)]


def pairs(count, stride):
    return [(i, i ^ stride) for i in range(count)]


def facing(count):
    order = []
    for i in range(count):
        order += [(2 * i, 2 * ((i - 1) % count) + 1), (2 * i + 1, 2 * ((i + 1) % count))]
    return order


def dot(a, b):
    return jnp.dot(a, b, preferred_element_type=F32)


def dot_nt(a, b):
    return lax.dot_general(a, b, (((1,), (1,)), ((), ())), preferred_element_type=F32)


def moved(value, step):
    width = value.shape[1]
    column = lax.broadcasted_iota(jnp.int32, value.shape, 1)
    edge = 0 if step > 0 else width - 1
    return jnp.where(column == edge, 0.0, pltpu.roll(value, step % width, 1))


def pieces(depth, total):
    blocks, row = [], 0
    for first in range(0, total - total % LANES, LANES):
        blocks.append((row, 0, 0, first, depth, LANES))
        row += depth
    rest = total % LANES
    if rest:
        fold = LANES // rest
        if LANES % rest or depth % (8 * fold):
            fold = 1
        part = depth // fold
        for g in range(fold):
            blocks.append((row, g * rest, g * part, total - rest, part, rest))
        row += part
    return blocks, row


def padded(count):
    return -(-count // 16) * 16


def with_rows(value, count):
    if value.shape[0] == count:
        return value
    return jnp.concatenate([value, jnp.zeros((count - value.shape[0], value.shape[1]), value.dtype)], 0)


def half_rows(depth, total):
    return -(-pieces(depth, total)[1] // 32) * 16


def stage_kernel(split, x, u, edge, frame, sems):
    frames, rows = x.shape[:2]
    core = lax.axis_index("chan")
    if split:
        row = jnp.where(lax.axis_index("axial") == 0, rows - 1, 0)
        picked = pl.ds(core * (frames // 2), frames // 2)
    else:
        row = core * (rows - 1)
        picked = pl.ds(0, frames)
    copies = [
        pltpu.make_async_copy(u.at[core * (frames - 1)], frame, sems.at[0]),
        pltpu.make_async_copy(x.at[picked, row], edge, sems.at[1]),
    ]
    for copy in copies:
        copy.start()
    for copy in copies:
        copy.wait()


def prepare(sw, tw, wf, twf):
    channels, mid = tw.shape[1:]
    for j in range(3):
        wf[j * mid : (j + 1) * mid] = sw[:, j].reshape(3 * channels, mid).astype(F32).T
    twf[...] = jnp.concatenate([tw[k].astype(F32) for k in (2, 1, 0)], 0).T
    return wf[...].astype(BF16), twf[...].astype(BF16)


def activations(w_taps, w_act, field, cot, width):
    mid = w_act.shape[0]
    taps = dot(w_taps, field)
    act = dot(w_act, cot)
    hids, grads = [], []
    for first in range(0, field.shape[1], width):
        cols = slice(first, first + width)
        pre = taps[mid : 2 * mid, cols] + moved(taps[:mid, cols], 1) + moved(taps[2 * mid :, cols], -1)
        s = 0.5 * jnp.tanh(0.5 * pre) + 0.5
        hids.append(pre * s)
        grads.append(act[:, cols] * s * (1.0 + pre * (1.0 - s)))
    return hids, grads


def gathered(xp, up, h, picked):
    depth = 3 * xp.shape[2]
    width = xp.shape[3]
    field = jnp.concatenate([xp[f, pl.ds(h, 3)].reshape(depth, width) for f in picked], 1)
    cot = jnp.concatenate([jnp.concatenate([up[f + d, h] for d in range(3)], 0) for f in picked], 1)
    return field, cot


def inner_rows(axial_count, rows):
    if axial_count == 2:
        low = lax.axis_index("axial") == 0
        return jnp.where(low, 0, 1), rows - 1, [jnp.where(low, rows - 1, 0)]
    return 1, rows - 2, [0, rows - 1]


def cell_grads(xp, up, w_taps, w_act, groups, store):
    fields, cots, shifts, owns = [], [], [], []
    width = xp.shape[3]
    for h, picked in groups:
        field, cot = gathered(xp, up, h, picked)
        hids, grads = activations(w_taps, w_act, field, cot, width)
        shifts.append(
            jnp.concatenate(
                [
                    jnp.concatenate([moved(v, -1) for v in grads], 1),
                    jnp.concatenate(grads, 1),
                    jnp.concatenate([moved(v, 1) for v in grads], 1),
                ],
                0,
            ).astype(BF16)
        )
        hids = [with_rows(v, padded(v.shape[0])).astype(BF16) for v in hids]
        owns.append(jnp.concatenate(hids, 1))
        for f, hid, grad in zip(picked, hids, grads):
            store(h, f, hid, with_rows(grad, padded(grad.shape[0])).astype(BF16))
        fields.append(field)
        cots.append(cot)
    return (
        dot_nt(jnp.concatenate(fields, 1), jnp.concatenate(shifts, 1)),
        dot_nt(jnp.concatenate(cots, 1), jnp.concatenate(owns, 1))[:, : w_act.shape[0]],
    )


def inner_kernel(dims, *refs):
    frames, rows, channels, width, mid, own_c, rank_count, axial_count, group = dims
    x, u, sw, tw = refs[:4]
    hid_out, grad_out, acc_out, xp, up, taps_out, act_out, wf, twf = refs[4:]
    for f in range(frames):
        for at in (0, rows + 1):
            xp[f, at] = jnp.zeros((channels, width), BF16)
        for h in range(rows):
            xp[f, h + 1] = x[f, h]
            up[f + 1, h] = u[f, h]
    for at in (0, frames + 1):
        up[at] = jnp.zeros(up.shape[1:], BF16)
    w_taps, w_act = prepare(sw, tw, wf, twf)
    taps_out[...] = w_taps
    act_out[...] = w_act

    first, count, _ = inner_rows(axial_count, rows)

    def store(h, f, hid, grad):
        hid_out[h - first, f - 1] = hid
        grad_out[h - first, f - 1] = grad

    groups = [(first + i, (f, f + 1)) for i in range(count) for f in range(1, frames - 1, 2)]
    w_part, t_part = cell_grads(xp, up, w_taps, w_act, groups, store)
    acc_out[:, : 3 * mid] = w_part
    acc_out[:, 3 * mid :] = t_part


def grads_kernel(dims, *refs):
    frames, rows, channels, width, mid, own_c, rank_count, axial_count, group = dims
    hid_in, grad_in, acc_in, x, u, edge, frame, swapped, taps_in, act_in = refs[:10]
    hid_out, grad_out, xp, up, half_0, half_1, edges, acc, packed = refs[10:]
    axial = lax.axis_index("axial")
    core = lax.axis_index("chan")
    w_taps, w_act = taps_in[...], act_in[...]

    has_lo = (axial > 0).astype(BF16)
    has_hi = (axial < axial_count - 1).astype(BF16)
    part = edge.shape[0]
    edges[pl.ds(core * part, part)] = edge[...]
    edges[pl.ds((1 - core) * part, part)] = swapped[0:part]
    at_hi = 2 * part - frames
    for f in range(frames):
        xp[f, 0] = edges[f] * has_lo
        xp[f, rows + 1] = edges[at_hi + f] * has_hi
        for h in range(rows):
            xp[f, h + 1] = x[f, h + 1]
            up[f + 1, h] = u[f + 1, h]
    up[core * (frames + 1)] = frame[...]
    up[(1 - core) * (frames + 1)] = swapped[part:]

    first, count, others = inner_rows(axial_count, rows)

    def store(h, f, hid, grad):
        hid_out[h, f] = hid
        grad_out[h, f] = grad

    for i in range(count):
        for f in range(1, frames - 1):
            store(first + i, f, hid_in[i, f - 1], grad_in[i, f - 1])
    groups = [(first + i, (0, frames - 1)) for i in range(count)]
    groups += [(h, (f, f + 1)) for h in others for f in range(0, frames, 2)]
    w_part, t_part = cell_grads(xp, up, w_taps, w_act, groups, store)
    factor = 1.0 / math.sqrt(frames * rows * width * rank_count)
    acc[:, : 3 * mid] = (acc_in[:, : 3 * mid] + w_part) * factor
    acc[:, 3 * mid :] = (acc_in[:, 3 * mid :] + t_part) * factor

    blocks, used = pieces(*acc.shape)
    size = packed.shape[0] // 2
    packed[used:] = jnp.zeros((2 * size - used, LANES), F32)
    for at, lane, source, column, depth, total in blocks:
        packed[at : at + depth, lane : lane + total] = acc[source : source + depth, column : column + total]
    half_0[...] = packed[:size].astype(half_0.dtype)
    half_1[...] = packed[size:].astype(half_1.dtype)


def others_kernel(dims, *refs):
    frames, rows, channels, width, mid, own_c, rank_count, axial_count, group = dims
    xp, up, sw, tw, hid_out, grad_out, wf, twf = refs
    w_taps, w_act = prepare(sw, tw, wf, twf)
    for h in range(rows):
        for first in range(0, frames, group):
            picked = range(first, first + group)
            field, cot = gathered(xp, up, h, picked)
            for f, hid, grad in zip(picked, *activations(w_taps, w_act, field, cot, width)):
                hid_out[h, f] = with_rows(hid, padded(mid)).astype(BF16)
                grad_out[h, f] = with_rows(grad, padded(mid)).astype(BF16)


def fields_kernel(dims, fast, *refs):
    frames, rows, channels, width, mid, own_c, rank_count, axial_count, group = dims
    hid_in, grad_in, hid_other, grad_other, sw, tw, sw_other, tw_other = refs[:8]
    out, out_a, out_b, ig, ig_a, ig_b, twt, wg, ig_acc, out_edges = refs[8:]
    own = pl.ds(pl.multiple_of(lax.axis_index("chan") * own_c, own_c), own_c)
    blank = jnp.zeros((own_c, padded(mid) - mid), F32)

    def both(a, b):
        return jnp.concatenate([a.astype(F32), blank, b.astype(F32), blank], 1).astype(BF16)

    for k in range(3):
        twt[k * own_c : (k + 1) * own_c] = both(tw[k, own], tw_other[k, own])
    for i in range(3):
        for j in range(3):
            at = (i * 3 + j) * own_c
            wg[at : at + own_c] = both(sw[i, j, own], sw_other[i, j, own])
    w_out, w_in = twt[...], wg[...]

    for h in range(rows):
        out_terms = {}
        for first in range(0, frames, group):
            picked = range(first, first + group)
            hid = jnp.concatenate([jnp.concatenate([hid_in[h, f], hid_other[h, f]], 0) for f in picked], 1)
            grad = jnp.concatenate([jnp.concatenate([grad_in[h, f], grad_other[h, f]], 0) for f in picked], 1)
            y_out = dot(w_out, hid)
            y_in = dot(w_in, grad)
            for g, f in enumerate(picked):
                cols = slice(g * width, (g + 1) * width)
                for k in range(3):
                    out_terms.setdefault(f - k + 1, []).append(y_out[k * own_c : (k + 1) * own_c, cols])
                for i in range(3):
                    at = i * 3 * own_c
                    total = (
                        y_in[at + own_c : at + 2 * own_c, cols]
                        + moved(y_in[at : at + own_c, cols], -1)
                        + moved(y_in[at + 2 * own_c : at + 3 * own_c, cols], 1)
                    )
                    if h == 0 or i == 2:
                        ig_acc[f, h + i] = total
                    else:
                        ig_acc[f, h + i] += total
        for f, terms in out_terms.items():
            total = functools.reduce(lambda a, b: a + b, terms)
            if f < 0:
                out_edges[0, h] = total.astype(BF16)
            elif f >= frames:
                out_edges[1, h] = total.astype(BF16)
            else:
                out[f, h] = total

    odd = lax.rem(lax.axis_index("tm"), 2) if fast else 1
    high = jnp.where(lax.axis_index("axial") == 0, rows + 1, 0) if fast else 0
    out_a[...] = out_edges[1 - odd]
    out_b[...] = out_edges[odd]
    for f in range(frames):
        ig_a[f] = ig_acc[f, high].astype(BF16)
        ig_b[f] = ig_acc[f, rows + 1].astype(BF16)
        for h in range(rows):
            ig[f, h] = ig_acc[f, h + 1]


def unpack(packed, acc, sg, tg):
    channels, mid = tg.shape[1:]
    for at, lane, source, column, depth, total in pieces(*acc.shape)[0]:
        acc[source : source + depth, column : column + total] = packed[at : at + depth, lane : lane + total]
    for i in range(3):
        rows = slice(i * channels, (i + 1) * channels)
        for j in range(3):
            sg[i, j] = acc[rows, j * mid : (j + 1) * mid]
        tg[2 - i] = acc[rows, 3 * mid :]


def add_edges(axial_count, own, from_lo, from_hi, ig_own, ig_from_lo, ig_from_hi, out, ig):
    frames, rows = own.shape[:2]
    axial = lax.axis_index("axial")
    has_lo = (axial > 0).astype(F32)
    has_hi = (axial < axial_count - 1).astype(F32)
    for f in range(frames):
        for h in range(rows):
            total = own[f, h]
            if f == 0:
                total = total + from_lo(h).astype(F32)
            if f == frames - 1:
                total = total + from_hi(h).astype(F32)
            out[f, h] = total.astype(BF16)
            total = ig_own[f, h]
            if h == 0:
                total = total + ig_from_lo(f).astype(F32) * has_lo
            if h == rows - 1:
                total = total + ig_from_hi(f).astype(F32) * has_hi
            ig[f, h] = total.astype(BF16)


def last_kernel(own, ig_own, half_0, got_0, half_1, got_1, got_a, got_b, out, ig, sg, tg, packed, acc, edges):
    frames, rows, own_c, width = own.shape
    size = half_0.shape[0]
    odd = lax.rem(lax.axis_index("tm"), 2)
    edges[1 - odd] = got_a[...].reshape(rows, own_c, width)
    edges[odd] = got_b[...].reshape(rows, own_c, width)
    add_edges(
        2,
        own,
        lambda h: edges[0, h],
        lambda h: edges[1, h],
        ig_own,
        lambda f: got_0[size + f * own_c : size + (f + 1) * own_c],
        lambda f: got_0[size + f * own_c : size + (f + 1) * own_c],
        out,
        ig,
    )
    packed[:size] = half_0[...].astype(F32) + got_0[:size].astype(F32)
    packed[size:] = half_1[...].astype(F32) + got_1[...].astype(F32)
    unpack(packed, acc, sg, tg)


def last_kernel_general(axial_count, *refs):
    own, ig_own, half_0, half_1, from_lo, from_hi, ig_from_lo, ig_from_hi, out, ig, sg, tg, packed, acc, edges = refs
    add_edges(
        axial_count,
        own,
        lambda h: from_lo[h],
        lambda h: from_hi[h],
        ig_own,
        lambda f: ig_from_lo[f],
        lambda f: ig_from_hi[f],
        out,
        ig,
    )
    size = half_0.shape[0]
    packed[:size] = half_0[...]
    packed[size:] = half_1[...]
    unpack(packed, acc, sg, tg)


def call(kernel, name, out_shape, count, limit, scratch=(), in_specs=None, flops=0):
    return pl.pallas_call(
        kernel,
        out_shape=out_shape,
        in_specs=in_specs or [VMEM] * count,
        out_specs=[VMEM] * len(out_shape),
        scratch_shapes=list(scratch),
        compiler_params=pltpu.CompilerParams(vmem_limit_bytes=int(limit * 1024 * 1024)),
        cost_estimate=pl.CostEstimate(flops=flops, bytes_accessed=1 << 20, transcendentals=0) if flops else None,
        name=name,
    )


def shards(frames_in, spatial_weight, temporal_weight, upstream):
    frames, rows, channels, width = frames_in.shape
    mid = temporal_weight.shape[1]
    axial_count = lax.axis_size("axial")
    tm_count = lax.axis_size("tm")
    core_count = lax.axis_size("chan")
    rank_count = tm_count * axial_count
    axial = lax.axis_index("axial")
    own_c = channels // core_count
    group = 2 if frames % 2 == 0 else 1
    dims = (frames, rows, channels, width, mid, own_c, rank_count, axial_count, group)
    size = half_rows(3 * channels, 4 * mid)
    sds = jax.ShapeDtypeStruct

    split = axial_count == 2 and frames % 2 == 0
    edge_count = frames // 2 if split else frames
    turned = jnp.swapaxes(temporal_weight, 1, 2)
    edge, frame = call(
        functools.partial(stage_kernel, split),
        "stage",
        [sds((edge_count, channels, width), BF16), sds((rows, channels, width), BF16)],
        2,
        60,
        [pltpu.SemaphoreType.DMA((2,))],
        [HBM] * 2,
    )(frames_in, upstream)
    frame = lax.ppermute(frame, ("tm", "chan"), facing(tm_count))
    if split:
        edge = lax.ppermute(edge, "axial", ring(2, 1))
    else:
        edge = lax.ppermute(edge, ("axial", "chan"), facing(axial_count))
    sw_other = lax.ppermute(spatial_weight, "chan", ring(2, 1))
    tw_other = lax.ppermute(turned, "chan", ring(2, 1))

    own_shape = (frames, rows, own_c, width)
    inner = (inner_rows(axial_count, rows)[1], frames - 2, padded(mid), width)
    cells = (rows, frames, padded(mid), width)
    xp_shape = (frames, rows + 2, channels, width)
    up_shape = (frames + 2, rows, channels, width)
    total = (3 * channels, 4 * mid)
    forms = [pltpu.VMEM((3 * mid, 3 * channels), F32), pltpu.VMEM((mid, 3 * channels), F32)]
    fast = axial_count == 2 and tm_count == 4
    hid, grad, acc, xp, up, w_taps, w_act = call(
        functools.partial(inner_kernel, dims),
        "inner_cells",
        [
            sds(inner, BF16),
            sds(inner, BF16),
            sds(total, F32),
            sds(xp_shape, BF16),
            sds(up_shape, BF16),
            sds((3 * mid, 3 * channels), BF16),
            sds((mid, 3 * channels), BF16),
        ],
        4,
        16,
        forms,
        flops=1 << 31,
    )(frames_in, upstream, spatial_weight, turned)
    edge, frame, acc = lax.optimization_barrier((edge, frame, acc))
    swapped = lax.ppermute(jnp.concatenate([edge, frame], 0), "chan", ring(2, 1))
    half_type = BF16 if fast else F32
    hid, grad, xp, up, half_0, half_1 = call(
        functools.partial(grads_kernel, dims),
        "weight_grads",
        [
            sds(cells, BF16),
            sds(cells, BF16),
            sds(xp_shape, BF16),
            sds(up_shape, BF16),
            sds((size, LANES), half_type),
            sds((size, LANES), half_type),
        ],
        10,
        16,
        [
            pltpu.VMEM((2 * edge_count, channels, width), BF16),
            pltpu.VMEM(total, F32),
            pltpu.VMEM((2 * size, LANES), F32),
        ],
    )(hid, grad, acc, xp, up, edge, frame, swapped, w_taps, w_act)

    if fast:
        near, far = pairs(4, 1), [(0, 3), (1, 2), (2, 1), (3, 0)]
        got_0 = lax.ppermute(half_0, "tm", near)
        got_1 = lax.ppermute(half_1, "axial", ring(2, 1))

    hid_other, grad_other = call(
        functools.partial(others_kernel, dims),
        "other_cells",
        [sds(cells, BF16), sds(cells, BF16)],
        4,
        16,
        forms,
        flops=1 << 31,
    )(xp, up, sw_other, tw_other)

    own_shape = (frames, rows, own_c, width)
    out_edge, ig_edge = sds((rows, own_c, width), BF16), sds((frames, own_c, width), BF16)
    out_own, out_a, out_b, ig_own, ig_a, ig_b = call(
        functools.partial(fields_kernel, dims, fast),
        "field_products",
        [sds(own_shape, F32), out_edge, out_edge, sds(own_shape, F32), ig_edge, ig_edge],
        8,
        16,
        [
            pltpu.VMEM((3 * own_c, 2 * padded(mid)), BF16),
            pltpu.VMEM((9 * own_c, 2 * padded(mid)), BF16),
            pltpu.VMEM((frames, rows + 2, own_c, width), F32),
            pltpu.VMEM((2, rows, own_c, width), BF16),
        ],
        flops=1 << 31,
    )(hid, grad, hid_other, grad_other, spatial_weight, turned, sw_other, tw_other)

    outs = [
        sds(own_shape, BF16),
        sds(own_shape, BF16),
        sds((3, 3, channels, mid), F32),
        sds((3, channels, mid), F32),
    ]
    scratch = [
        pltpu.VMEM((2 * size, LANES), F32),
        pltpu.VMEM(total, F32),
        pltpu.VMEM((2, rows, own_c, width), BF16),
    ]
    if fast:
        got_0, got_1, out_a, out_b, ig_a = lax.optimization_barrier((got_0, got_1, out_a, out_b, ig_a))
        half_0, half_1 = lax.optimization_barrier((half_0 + got_0, half_1 + got_1))
        got_0 = lax.ppermute(jnp.concatenate([half_0, out_b.reshape(-1, width)], 0), "tm", far)
        got_1 = lax.ppermute(jnp.concatenate([half_1, out_a.reshape(-1, width)], 0), "tm", near)
        got_a, got_b = got_1[size:], got_0[size:]
        half_0, half_1 = lax.optimization_barrier((half_0 + got_0[:size], half_1 + got_1[:size]))
        got_1 = lax.ppermute(half_1, "tm", pairs(4, 2))
        got_0 = lax.ppermute(jnp.concatenate([half_0, ig_a.reshape(-1, width)], 0), "axial", ring(2, 1))
        results = call(last_kernel, "last", outs, 8, 8, scratch)(
            out_own, ig_own, half_0, got_0, half_1, got_1, got_a, got_b
        )
    else:
        half_0, half_1 = lax.psum((half_0, half_1), ("tm", "axial"))
        from_hi = lax.ppermute(out_a, "tm", ring(tm_count, -1))
        from_lo = lax.ppermute(out_b, "tm", ring(tm_count, 1))
        ig_from_hi = lax.ppermute(ig_a, "axial", ring(axial_count, -1))
        ig_from_lo = lax.ppermute(ig_b, "axial", ring(axial_count, 1))
        results = call(functools.partial(last_kernel_general, axial_count), "last", outs, 8, 8, scratch)(
            out_own, ig_own, half_0, half_1, from_lo, from_hi, ig_from_lo, ig_from_hi
        )
    output, input_grad, spatial_grad, temporal_grad = results
    return output, input_grad, spatial_grad, jnp.swapaxes(temporal_grad, 1, 2)


def solution(mesh):
    placed = (
        P(("parts", "tm"), "axial", None, None),
        P("parts", None, None, "chan"),
        P("parts", "chan", None),
        P(("parts", "tm"), "axial", None, None),
    )
    return jax.shard_map(
        shards,
        mesh=mesh,
        in_specs=placed,
        out_specs=(
            P(("parts", "tm"), "axial", "chan", None),
            P(("parts", "tm"), "axial", "chan", None),
            P("parts", None, None, "chan"),
            P("parts", "chan", None),
        ),
        check_vma=False,
    )
```

```python
import functools
import math

import jax
import jax.numpy as jnp
from jax import lax
from jax.experimental import pallas as pl
from jax.experimental.pallas import tpu as pltpu
from jax.sharding import PartitionSpec as P

F32 = jnp.float32
BF16 = jnp.bfloat16
LANES = 128
HBM = pl.BlockSpec(memory_space=pltpu.HBM)
VMEM = pl.BlockSpec(memory_space=pltpu.VMEM)


def ring(count, step):
    return [(i, (i + step) % count) for i in range(count)]


def pairs(count, stride):
    return [(i, i ^ stride) for i in range(count)]


def facing(count):
    order = []
    for i in range(count):
        order += [(2 * i, 2 * ((i - 1) % count) + 1), (2 * i + 1, 2 * ((i + 1) % count))]
    return order


def dot(a, b):
    return jnp.dot(a, b, preferred_element_type=F32)


def dot_nt(a, b):
    return lax.dot_general(a, b, (((1,), (1,)), ((), ())), preferred_element_type=F32)


def moved(value, step):
    width = value.shape[1]
    column = lax.broadcasted_iota(jnp.int32, value.shape, 1)
    edge = 0 if step > 0 else width - 1
    return jnp.where(column == edge, 0.0, pltpu.roll(value, step % width, 1))


def pieces(depth, total):
    blocks, row = [], 0
    for first in range(0, total - total % LANES, LANES):
        blocks.append((row, 0, 0, first, depth, LANES))
        row += depth
    rest = total % LANES
    if rest:
        fold = LANES // rest
        if LANES % rest or depth % (8 * fold):
            fold = 1
        part = depth // fold
        for g in range(fold):
            blocks.append((row, g * rest, g * part, total - rest, part, rest))
        row += part
    return blocks, row


def padded(count):
    return -(-count // 16) * 16


def with_rows(value, count):
    if value.shape[0] == count:
        return value
    return jnp.concatenate([value, jnp.zeros((count - value.shape[0], value.shape[1]), value.dtype)], 0)


def half_rows(depth, total):
    return -(-pieces(depth, total)[1] // 32) * 16


def stage_kernel(split, x, u, sw, tw, edge, frame, sems):
    frames, rows = x.shape[:2]
    core = lax.axis_index("chan")
    if split:
        row = jnp.where(lax.axis_index("axial") == 0, rows - 1, 0)
        picked = pl.ds(core * (frames // 2), frames // 2)
    else:
        row = core * (rows - 1)
        picked = pl.ds(0, frames)
    copies = [
        pltpu.make_async_copy(u.at[core * (frames - 1)], frame, sems.at[0]),
        pltpu.make_async_copy(x.at[picked, row], edge, sems.at[1]),
    ]
    for copy in copies:
        copy.start()
    for copy in copies:
        copy.wait()


def prepare(sw, tw, wf, twf):
    channels, mid = tw.shape[1:]
    for j in range(3):
        wf[j * mid : (j + 1) * mid] = sw[:, j].reshape(3 * channels, mid).astype(F32).T
    twf[...] = jnp.concatenate([tw[k].astype(F32) for k in (2, 1, 0)], 0).T
    return wf[...].astype(BF16), twf[...].astype(BF16)


def activations(w_taps, w_act, field, cot, width):
    mid = w_act.shape[0]
    taps = dot(w_taps, field)
    act = dot(w_act, cot)
    hids, grads = [], []
    for first in range(0, field.shape[1], width):
        cols = slice(first, first + width)
        pre = taps[mid : 2 * mid, cols] + moved(taps[:mid, cols], 1) + moved(taps[2 * mid :, cols], -1)
        s = 0.5 * jnp.tanh(0.5 * pre) + 0.5
        hids.append(pre * s)
        grads.append(act[:, cols] * s * (1.0 + pre * (1.0 - s)))
    return hids, grads


def gathered(xp, up, h, picked):
    depth = 3 * xp.shape[2]
    width = xp.shape[3]
    field = jnp.concatenate([xp[f, pl.ds(h, 3)].reshape(depth, width) for f in picked], 1)
    cot = jnp.concatenate([jnp.concatenate([up[f + d, h] for d in range(3)], 0) for f in picked], 1)
    return field, cot


def inner_rows(axial_count, rows):
    if axial_count == 2:
        low = lax.axis_index("axial") == 0
        return jnp.where(low, 0, 1), rows - 1, [jnp.where(low, rows - 1, 0)]
    return 1, rows - 2, [0, rows - 1]


def cell_grads(xp, up, w_taps, w_act, groups, store):
    fields, cots, shifts, owns = [], [], [], []
    width = xp.shape[3]
    for h, picked in groups:
        field, cot = gathered(xp, up, h, picked)
        hids, grads = activations(w_taps, w_act, field, cot, width)
        shifts.append(
            jnp.concatenate(
                [
                    jnp.concatenate([moved(v, -1) for v in grads], 1),
                    jnp.concatenate(grads, 1),
                    jnp.concatenate([moved(v, 1) for v in grads], 1),
                ],
                0,
            ).astype(BF16)
        )
        hids = [with_rows(v, padded(v.shape[0])).astype(BF16) for v in hids]
        owns.append(jnp.concatenate(hids, 1))
        for f, hid, grad in zip(picked, hids, grads):
            store(h, f, hid, with_rows(grad, padded(grad.shape[0])).astype(BF16))
        fields.append(field)
        cots.append(cot)
    return (
        dot_nt(jnp.concatenate(fields, 1), jnp.concatenate(shifts, 1)),
        dot_nt(jnp.concatenate(cots, 1), jnp.concatenate(owns, 1))[:, : w_act.shape[0]],
    )


def inner_kernel(dims, *refs):
    frames, rows, channels, width, mid, own_c, rank_count, axial_count, group = dims
    x, u, sw, tw = refs[:4]
    hid_out, grad_out, acc_out, xp, up, taps_out, act_out, wf, twf = refs[4:]
    for f in range(frames):
        for at in (0, rows + 1):
            xp[f, at] = jnp.zeros((channels, width), BF16)
        for h in range(rows):
            xp[f, h + 1] = x[f, h]
            up[f + 1, h] = u[f, h]
    for at in (0, frames + 1):
        up[at] = jnp.zeros(up.shape[1:], BF16)
    w_taps, w_act = prepare(sw, tw, wf, twf)
    taps_out[...] = w_taps
    act_out[...] = w_act

    first, count, _ = inner_rows(axial_count, rows)

    def store(h, f, hid, grad):
        hid_out[h - first, f - 1] = hid
        grad_out[h - first, f - 1] = grad

    groups = [(first + i, (f, f + 1)) for i in range(count) for f in range(1, frames - 1, 2)]
    w_part, t_part = cell_grads(xp, up, w_taps, w_act, groups, store)
    acc_out[:, : 3 * mid] = w_part
    acc_out[:, 3 * mid :] = t_part


def grads_kernel(dims, *refs):
    frames, rows, channels, width, mid, own_c, rank_count, axial_count, group = dims
    hid_in, grad_in, acc_in, x, u, edge, frame, swapped, taps_in, act_in = refs[:10]
    hid_out, grad_out, xp, up, kept, sent, edges, acc, packed = refs[10:]
    axial = lax.axis_index("axial")
    core = lax.axis_index("chan")
    w_taps, w_act = taps_in[...], act_in[...]

    has_lo = (axial > 0).astype(BF16)
    has_hi = (axial < axial_count - 1).astype(BF16)
    part = edge.shape[0]
    edges[pl.ds(core * part, part)] = edge[...]
    edges[pl.ds((1 - core) * part, part)] = swapped[0:part]
    at_hi = 2 * part - frames
    for f in range(frames):
        xp[f, 0] = edges[f] * has_lo
        xp[f, rows + 1] = edges[at_hi + f] * has_hi
        for h in range(rows):
            xp[f, h + 1] = x[f, h + 1]
            up[f + 1, h] = u[f + 1, h]
    up[core * (frames + 1)] = frame[...]
    up[(1 - core) * (frames + 1)] = swapped[part:]

    first, count, others = inner_rows(axial_count, rows)

    def store(h, f, hid, grad):
        hid_out[h, f] = hid
        grad_out[h, f] = grad

    for i in range(count):
        for f in range(1, frames - 1):
            store(first + i, f, hid_in[i, f - 1], grad_in[i, f - 1])
    groups = [(first + i, (0, frames - 1)) for i in range(count)]
    groups += [(h, (f, f + 1)) for h in others for f in range(0, frames, 2)]
    w_part, t_part = cell_grads(xp, up, w_taps, w_act, groups, store)
    factor = 1.0 / math.sqrt(frames * rows * width * rank_count)
    acc[:, : 3 * mid] = (acc_in[:, : 3 * mid] + w_part) * factor
    acc[:, 3 * mid :] = (acc_in[:, 3 * mid :] + t_part) * factor

    blocks, used = pieces(*acc.shape)
    size = packed.shape[0] // 2
    packed[used:] = jnp.zeros((2 * size - used, LANES), F32)
    for at, lane, source, column, depth, total in blocks:
        packed[at : at + depth, lane : lane + total] = acc[source : source + depth, column : column + total]
    mine = lax.rem(axial, 2)
    kept[...] = packed[pl.ds(pl.multiple_of(mine * size, 16), size)]
    sent[...] = packed[pl.ds(pl.multiple_of((1 - mine) * size, 16), size)].astype(sent.dtype)


def others_kernel(dims, *refs):
    frames, rows, channels, width, mid, own_c, rank_count, axial_count, group = dims
    xp, up, sw, tw, hid_out, grad_out, wf, twf = refs
    w_taps, w_act = prepare(sw, tw, wf, twf)
    for h in range(rows):
        for first in range(0, frames, group):
            picked = range(first, first + group)
            field, cot = gathered(xp, up, h, picked)
            for f, hid, grad in zip(picked, *activations(w_taps, w_act, field, cot, width)):
                hid_out[h, f] = with_rows(hid, padded(mid)).astype(BF16)
                grad_out[h, f] = with_rows(grad, padded(mid)).astype(BF16)


def fields_kernel(dims, fast, *refs):
    frames, rows, channels, width, mid, own_c, rank_count, axial_count, group = dims
    hid_in, grad_in, hid_other, grad_other, sw, tw, sw_other, tw_other = refs[:8]
    out, out_a, out_b, ig, ig_a, ig_b, twt, wg, ig_acc, out_edges = refs[8:]
    own = pl.ds(pl.multiple_of(lax.axis_index("chan") * own_c, own_c), own_c)
    blank = jnp.zeros((own_c, padded(mid) - mid), F32)

    def both(a, b):
        return jnp.concatenate([a.astype(F32), blank, b.astype(F32), blank], 1).astype(BF16)

    for k in range(3):
        twt[k * own_c : (k + 1) * own_c] = both(tw[k, own], tw_other[k, own])
    for i in range(3):
        for j in range(3):
            at = (i * 3 + j) * own_c
            wg[at : at + own_c] = both(sw[i, j, own], sw_other[i, j, own])
    w_out, w_in = twt[...], wg[...]

    for h in range(rows):
        out_terms = {}
        for first in range(0, frames, group):
            picked = range(first, first + group)
            hid = jnp.concatenate([jnp.concatenate([hid_in[h, f], hid_other[h, f]], 0) for f in picked], 1)
            grad = jnp.concatenate([jnp.concatenate([grad_in[h, f], grad_other[h, f]], 0) for f in picked], 1)
            y_out = dot(w_out, hid)
            y_in = dot(w_in, grad)
            for g, f in enumerate(picked):
                cols = slice(g * width, (g + 1) * width)
                for k in range(3):
                    out_terms.setdefault(f - k + 1, []).append(y_out[k * own_c : (k + 1) * own_c, cols])
                for i in range(3):
                    at = i * 3 * own_c
                    total = (
                        y_in[at + own_c : at + 2 * own_c, cols]
                        + moved(y_in[at : at + own_c, cols], -1)
                        + moved(y_in[at + 2 * own_c : at + 3 * own_c, cols], 1)
                    )
                    if h == 0 or i == 2:
                        ig_acc[f, h + i] = total
                    else:
                        ig_acc[f, h + i] += total
        for f, terms in out_terms.items():
            total = functools.reduce(lambda a, b: a + b, terms)
            if f < 0:
                out_edges[0, h] = total.astype(BF16)
            elif f >= frames:
                out_edges[1, h] = total.astype(BF16)
            else:
                out[f, h] = total

    odd = lax.rem(lax.axis_index("tm"), 2) if fast else 1
    high = jnp.where(lax.axis_index("axial") == 0, rows + 1, 0) if fast else 0
    out_a[...] = out_edges[1 - odd]
    out_b[...] = out_edges[odd]
    for f in range(frames):
        ig_a[f] = ig_acc[f, high].astype(BF16)
        ig_b[f] = ig_acc[f, rows + 1].astype(BF16)
        for h in range(rows):
            ig[f, h] = ig_acc[f, h + 1]


def unpack(packed, acc, sg, tg):
    channels, mid = tg.shape[1:]
    for at, lane, source, column, depth, total in pieces(*acc.shape)[0]:
        acc[source : source + depth, column : column + total] = packed[at : at + depth, lane : lane + total]
    for i in range(3):
        rows = slice(i * channels, (i + 1) * channels)
        for j in range(3):
            sg[i, j] = acc[rows, j * mid : (j + 1) * mid]
        tg[2 - i] = acc[rows, 3 * mid :]


def add_edges(axial_count, own, from_lo, from_hi, ig_own, ig_from_lo, ig_from_hi, out, ig):
    frames, rows = own.shape[:2]
    axial = lax.axis_index("axial")
    has_lo = (axial > 0).astype(F32)
    has_hi = (axial < axial_count - 1).astype(F32)
    for f in range(frames):
        for h in range(rows):
            total = own[f, h]
            if f == 0:
                total = total + from_lo(h).astype(F32)
            if f == frames - 1:
                total = total + from_hi(h).astype(F32)
            out[f, h] = total.astype(BF16)
            total = ig_own[f, h]
            if h == 0:
                total = total + ig_from_lo(f).astype(F32) * has_lo
            if h == rows - 1:
                total = total + ig_from_hi(f).astype(F32) * has_hi
            ig[f, h] = total.astype(BF16)


def last_kernel(fast, *refs):
    own, ig_own, kept, other, from_a, from_b, ig_from_a, ig_from_b, out, ig, sg, tg, packed, acc, edges = refs
    edge_shape = edges.shape[1:]
    odd = lax.rem(lax.axis_index("tm"), 2) if fast else 1
    edges[1 - odd] = from_a[...].reshape(edge_shape)
    edges[odd] = from_b[...].reshape(edge_shape)
    add_edges(
        lax.axis_size("axial"),
        own,
        lambda h: edges[0, h],
        lambda h: edges[1, h],
        ig_own,
        lambda f: ig_from_a[f],
        lambda f: ig_from_b[f],
        out,
        ig,
    )
    size = kept.shape[0]
    mine = lax.rem(lax.axis_index("axial"), 2)
    packed[pl.ds(pl.multiple_of(mine * size, 16), size)] = kept[...].astype(F32)
    packed[pl.ds(pl.multiple_of((1 - mine) * size, 16), size)] = other[...].astype(F32)
    unpack(packed, acc, sg, tg)


def call(kernel, name, out_shape, count, limit, scratch=(), in_specs=None, flops=0):
    return pl.pallas_call(
        kernel,
        out_shape=out_shape,
        in_specs=in_specs or [VMEM] * count,
        out_specs=[VMEM] * len(out_shape),
        scratch_shapes=list(scratch),
        compiler_params=pltpu.CompilerParams(vmem_limit_bytes=int(limit * 1024 * 1024)),
        cost_estimate=pl.CostEstimate(flops=flops, bytes_accessed=1 << 20, transcendentals=0) if flops else None,
        name=name,
    )


def shards(frames_in, spatial_weight, temporal_weight, upstream):
    frames, rows, channels, width = frames_in.shape
    mid = temporal_weight.shape[1]
    axial_count = lax.axis_size("axial")
    tm_count = lax.axis_size("tm")
    core_count = lax.axis_size("chan")
    rank_count = tm_count * axial_count
    axial = lax.axis_index("axial")
    own_c = channels // core_count
    group = 2 if frames % 2 == 0 else 1
    dims = (frames, rows, channels, width, mid, own_c, rank_count, axial_count, group)
    size = half_rows(3 * channels, 4 * mid)
    sds = jax.ShapeDtypeStruct

    split = axial_count == 2 and frames % 2 == 0
    edge_count = frames // 2 if split else frames
    turned = jnp.swapaxes(temporal_weight, 1, 2)
    edge, frame = call(
        functools.partial(stage_kernel, split),
        "stage",
        [sds((edge_count, channels, width), BF16), sds((rows, channels, width), BF16)],
        4,
        60,
        [pltpu.SemaphoreType.DMA((2,))],
        [HBM] * 4,
    )(frames_in, upstream, spatial_weight, turned)
    frame = lax.ppermute(frame, ("tm", "chan"), facing(tm_count))
    if split:
        edge = lax.ppermute(edge, "axial", ring(2, 1))
    else:
        edge = lax.ppermute(edge, ("axial", "chan"), facing(axial_count))
    sw_other = lax.ppermute(spatial_weight, "chan", ring(2, 1))
    tw_other = lax.ppermute(turned, "chan", ring(2, 1))

    own_shape = (frames, rows, own_c, width)
    inner = (inner_rows(axial_count, rows)[1], frames - 2, padded(mid), width)
    cells = (rows, frames, padded(mid), width)
    xp_shape = (frames, rows + 2, channels, width)
    up_shape = (frames + 2, rows, channels, width)
    total = (3 * channels, 4 * mid)
    forms = [pltpu.VMEM((3 * mid, 3 * channels), F32), pltpu.VMEM((mid, 3 * channels), F32)]
    fast = axial_count == 2 and tm_count == 4
    hid, grad, acc, xp, up, w_taps, w_act = call(
        functools.partial(inner_kernel, dims),
        "inner_cells",
        [
            sds(inner, BF16),
            sds(inner, BF16),
            sds(total, F32),
            sds(xp_shape, BF16),
            sds(up_shape, BF16),
            sds((3 * mid, 3 * channels), BF16),
            sds((mid, 3 * channels), BF16),
        ],
        4,
        16,
        forms,
        flops=1 << 31,
    )(frames_in, upstream, spatial_weight, turned)
    edge, frame, acc, sw_other, tw_other = lax.optimization_barrier((edge, frame, acc, sw_other, tw_other))
    swapped = lax.ppermute(jnp.concatenate([edge, frame], 0), "chan", ring(2, 1))
    hid, grad, xp, up, kept, sent = call(
        functools.partial(grads_kernel, dims),
        "weight_grads",
        [
            sds(cells, BF16),
            sds(cells, BF16),
            sds(xp_shape, BF16),
            sds(up_shape, BF16),
            sds((size, LANES), F32),
            sds((size, LANES), BF16 if fast else F32),
        ],
        10,
        16,
        [
            pltpu.VMEM((2 * edge_count, channels, width), BF16),
            pltpu.VMEM(total, F32),
            pltpu.VMEM((2 * size, LANES), F32),
        ],
    )(hid, grad, acc, xp, up, edge, frame, swapped, w_taps, w_act)

    if fast:
        near, far = pairs(4, 1), [(0, 3), (1, 2), (2, 1), (3, 0)]
        got = lax.ppermute(sent, "axial", ring(2, 1))

    hid_other, grad_other = call(
        functools.partial(others_kernel, dims),
        "other_cells",
        [sds(cells, BF16), sds(cells, BF16)],
        4,
        16,
        forms,
        flops=1 << 31,
    )(xp, up, sw_other, tw_other)

    own_shape = (frames, rows, own_c, width)
    out_edge, ig_edge = sds((rows, own_c, width), BF16), sds((frames, own_c, width), BF16)
    out_own, out_a, out_b, ig_own, ig_a, ig_b = call(
        functools.partial(fields_kernel, dims, fast),
        "field_products",
        [sds(own_shape, F32), out_edge, out_edge, sds(own_shape, F32), ig_edge, ig_edge],
        8,
        16,
        [
            pltpu.VMEM((3 * own_c, 2 * padded(mid)), BF16),
            pltpu.VMEM((9 * own_c, 2 * padded(mid)), BF16),
            pltpu.VMEM((frames, rows + 2, own_c, width), F32),
            pltpu.VMEM((2, rows, own_c, width), BF16),
        ],
        flops=1 << 31,
    )(hid, grad, hid_other, grad_other, spatial_weight, turned, sw_other, tw_other)

    outs = [
        sds(own_shape, BF16),
        sds(own_shape, BF16),
        sds((3, 3, channels, mid), F32),
        sds((3, channels, mid), F32),
    ]
    scratch = [
        pltpu.VMEM((2 * size, LANES), F32),
        pltpu.VMEM(total, F32),
        pltpu.VMEM((2, rows, own_c, width), BF16),
    ]
    if fast:
        got, out_a, out_b, ig_a = lax.optimization_barrier((got, out_a, out_b, ig_a))
        kept = lax.optimization_barrier((kept + got.astype(F32)).astype(BF16))
        got = lax.ppermute(jnp.concatenate([kept, out_a.reshape(-1, width)], 0), "tm", near)
        from_b = lax.ppermute(out_b, "tm", far)
        got, from_b = lax.optimization_barrier((got, from_b))
        from_a = got[size:]
        kept = lax.optimization_barrier(kept + got[:size])
        got = lax.ppermute(kept, "tm", pairs(4, 2))
        ig_from_a = ig_from_b = lax.ppermute(ig_a, "axial", ring(2, 1))
        got, ig_from_a = lax.optimization_barrier((got, ig_from_a))
        kept = lax.optimization_barrier(kept + got)
        other = lax.ppermute(kept, "axial", ring(2, 1))
    else:
        odd = lax.rem(axial, 2) == 1
        low, high = jnp.where(odd, sent, kept), jnp.where(odd, kept, sent)
        low, high = lax.psum((low, high), ("tm", "axial"))
        kept, other = jnp.where(odd, high, low), jnp.where(odd, low, high)
        from_b = lax.ppermute(out_a, "tm", ring(tm_count, -1))
        from_a = lax.ppermute(out_b, "tm", ring(tm_count, 1))
        ig_from_b = lax.ppermute(ig_a, "axial", ring(axial_count, -1))
        ig_from_a = lax.ppermute(ig_b, "axial", ring(axial_count, 1))
    results = call(functools.partial(last_kernel, fast), "last", outs, 8, 8, scratch)(
        out_own, ig_own, kept, other, from_a, from_b, ig_from_a, ig_from_b
    )
    output, input_grad, spatial_grad, temporal_grad = results
    return output, input_grad, spatial_grad, jnp.swapaxes(temporal_grad, 1, 2)


def solution(mesh):
    placed = (
        P(("parts", "tm"), "axial", None, None),
        P("parts", None, None, "chan"),
        P("parts", "chan", None),
        P(("parts", "tm"), "axial", None, None),
    )
    return jax.shard_map(
        shards,
        mesh=mesh,
        in_specs=placed,
        out_specs=(
            P(("parts", "tm"), "axial", "chan", None),
            P(("parts", "tm"), "axial", "chan", None),
            P("parts", None, None, "chan"),
            P("parts", "chan", None),
        ),
        check_vma=False,
    )
```

```python
import functools
import math

import jax
import jax.numpy as jnp
from jax import lax
from jax.experimental import pallas as pl
from jax.experimental.pallas import tpu as pltpu
from jax.sharding import PartitionSpec as P

F32 = jnp.float32
BF16 = jnp.bfloat16
LANES = 128
HBM = pl.BlockSpec(memory_space=pltpu.HBM)
VMEM = pl.BlockSpec(memory_space=pltpu.VMEM)


def ring(count, step):
    return [(i, (i + step) % count) for i in range(count)]


def pairs(count, stride):
    return [(i, i ^ stride) for i in range(count)]


def facing(count):
    order = []
    for i in range(count):
        order += [(2 * i, 2 * ((i - 1) % count) + 1), (2 * i + 1, 2 * ((i + 1) % count))]
    return order


def dot(a, b):
    return jnp.dot(a, b, preferred_element_type=F32)


def dot_nt(a, b):
    return lax.dot_general(a, b, (((1,), (1,)), ((), ())), preferred_element_type=F32)


def moved(value, step):
    width = value.shape[1]
    column = lax.broadcasted_iota(jnp.int32, value.shape, 1)
    edge = 0 if step > 0 else width - 1
    return jnp.where(column == edge, 0.0, pltpu.roll(value, step % width, 1))


def pieces(depth, total):
    blocks, row = [], 0
    for first in range(0, total - total % LANES, LANES):
        blocks.append((row, 0, 0, first, depth, LANES))
        row += depth
    rest = total % LANES
    if rest:
        fold = LANES // rest
        if LANES % rest or depth % (8 * fold):
            fold = 1
        part = depth // fold
        for g in range(fold):
            blocks.append((row, g * rest, g * part, total - rest, part, rest))
        row += part
    return blocks, row


def padded(count):
    return -(-count // 16) * 16


def with_rows(value, count):
    if value.shape[0] == count:
        return value
    return jnp.concatenate([value, jnp.zeros((count - value.shape[0], value.shape[1]), value.dtype)], 0)


def half_rows(depth, total):
    return -(-pieces(depth, total)[1] // 32) * 16


def stage_kernel(split, x, u, sw, tw, edge, frame, sems):
    frames, rows = x.shape[:2]
    core = lax.axis_index("chan")
    if split:
        row = jnp.where(lax.axis_index("axial") == 0, rows - 1, 0)
        picked = pl.ds(core * (frames // 2), frames // 2)
    else:
        row = core * (rows - 1)
        picked = pl.ds(0, frames)
    copies = [
        pltpu.make_async_copy(u.at[core * (frames - 1)], frame, sems.at[0]),
        pltpu.make_async_copy(x.at[picked, row], edge, sems.at[1]),
    ]
    for copy in copies:
        copy.start()
    for copy in copies:
        copy.wait()


def prepare(sw, tw, wf, twf):
    channels, mid = tw.shape[1:]
    for j in range(3):
        wf[j * mid : (j + 1) * mid] = sw[:, j].reshape(3 * channels, mid).astype(F32).T
    twf[...] = jnp.concatenate([tw[k].astype(F32) for k in (2, 1, 0)], 0).T
    return wf[...].astype(BF16), twf[...].astype(BF16)


def activations(w_taps, w_act, field, cot, width):
    mid = w_act.shape[0]
    taps = dot(w_taps, field)
    act = dot(w_act, cot)
    hids, grads = [], []
    for first in range(0, field.shape[1], width):
        cols = slice(first, first + width)
        pre = taps[mid : 2 * mid, cols] + moved(taps[:mid, cols], 1) + moved(taps[2 * mid :, cols], -1)
        s = 0.5 * jnp.tanh(0.5 * pre) + 0.5
        hids.append(pre * s)
        grads.append(act[:, cols] * s * (1.0 + pre * (1.0 - s)))
    return hids, grads


def gathered(xp, up, h, picked):
    depth = 3 * xp.shape[2]
    width = xp.shape[3]
    field = jnp.concatenate([xp[f, pl.ds(h, 3)].reshape(depth, width) for f in picked], 1)
    cot = jnp.concatenate([jnp.concatenate([up[f + d, h] for d in range(3)], 0) for f in picked], 1)
    return field, cot


def inner_rows(axial_count, rows):
    if axial_count == 2:
        low = lax.axis_index("axial") == 0
        return jnp.where(low, 0, 1), rows - 1, [jnp.where(low, rows - 1, 0)]
    return 1, rows - 2, [0, rows - 1]


def cell_grads(xp, up, w_taps, w_act, groups, store):
    fields, cots, shifts, owns = [], [], [], []
    width = xp.shape[3]
    for h, picked in groups:
        field, cot = gathered(xp, up, h, picked)
        hids, grads = activations(w_taps, w_act, field, cot, width)
        shifts.append(
            jnp.concatenate(
                [
                    jnp.concatenate([moved(v, -1) for v in grads], 1),
                    jnp.concatenate(grads, 1),
                    jnp.concatenate([moved(v, 1) for v in grads], 1),
                ],
                0,
            ).astype(BF16)
        )
        hids = [with_rows(v, padded(v.shape[0])).astype(BF16) for v in hids]
        owns.append(jnp.concatenate(hids, 1))
        for f, hid, grad in zip(picked, hids, grads):
            store(h, f, hid, with_rows(grad, padded(grad.shape[0])).astype(BF16))
        fields.append(field)
        cots.append(cot)
    return (
        dot_nt(jnp.concatenate(fields, 1), jnp.concatenate(shifts, 1)),
        dot_nt(jnp.concatenate(cots, 1), jnp.concatenate(owns, 1))[:, : w_act.shape[0]],
    )


def inner_kernel(dims, *refs):
    frames, rows, channels, width, mid, own_c, rank_count, axial_count, group = dims
    x, u, sw, tw = refs[:4]
    hid_out, grad_out, acc_out, xp, up, taps_out, act_out, wf, twf = refs[4:]
    for f in range(frames):
        for at in (0, rows + 1):
            xp[f, at] = jnp.zeros((channels, width), BF16)
        for h in range(rows):
            xp[f, h + 1] = x[f, h]
            up[f + 1, h] = u[f, h]
    for at in (0, frames + 1):
        up[at] = jnp.zeros(up.shape[1:], BF16)
    w_taps, w_act = prepare(sw, tw, wf, twf)
    taps_out[...] = w_taps
    act_out[...] = w_act

    first, count, _ = inner_rows(axial_count, rows)

    def store(h, f, hid, grad):
        hid_out[h - first, f - 1] = hid
        grad_out[h - first, f - 1] = grad

    groups = [(first + i, (f, f + 1)) for i in range(count) for f in range(1, frames - 1, 2)]
    w_part, t_part = cell_grads(xp, up, w_taps, w_act, groups, store)
    acc_out[:, : 3 * mid] = w_part
    acc_out[:, 3 * mid :] = t_part


def grads_kernel(dims, *refs):
    frames, rows, channels, width, mid, own_c, rank_count, axial_count, group = dims
    hid_in, grad_in, acc_in, x, u, edge, frame, swapped, taps_in, act_in = refs[:10]
    hid_out, grad_out, xp, up, half_0, half_1, edges, acc, packed = refs[10:]
    axial = lax.axis_index("axial")
    core = lax.axis_index("chan")
    w_taps, w_act = taps_in[...], act_in[...]

    has_lo = (axial > 0).astype(BF16)
    has_hi = (axial < axial_count - 1).astype(BF16)
    part = edge.shape[0]
    edges[pl.ds(core * part, part)] = edge[...]
    edges[pl.ds((1 - core) * part, part)] = swapped[0:part]
    at_hi = 2 * part - frames
    for f in range(frames):
        xp[f, 0] = edges[f] * has_lo
        xp[f, rows + 1] = edges[at_hi + f] * has_hi
        for h in range(rows):
            xp[f, h + 1] = x[f, h + 1]
            up[f + 1, h] = u[f + 1, h]
    up[core * (frames + 1)] = frame[...]
    up[(1 - core) * (frames + 1)] = swapped[part:]

    first, count, others = inner_rows(axial_count, rows)

    def store(h, f, hid, grad):
        hid_out[h, f] = hid
        grad_out[h, f] = grad

    for i in range(count):
        for f in range(1, frames - 1):
            store(first + i, f, hid_in[i, f - 1], grad_in[i, f - 1])
    groups = [(first + i, (0, frames - 1)) for i in range(count)]
    groups += [(h, (f, f + 1)) for h in others for f in range(0, frames, 2)]
    w_part, t_part = cell_grads(xp, up, w_taps, w_act, groups, store)
    factor = 1.0 / math.sqrt(frames * rows * width * rank_count)
    acc[:, : 3 * mid] = (acc_in[:, : 3 * mid] + w_part) * factor
    acc[:, 3 * mid :] = (acc_in[:, 3 * mid :] + t_part) * factor

    blocks, used = pieces(*acc.shape)
    size = packed.shape[0] // 2
    packed[used:] = jnp.zeros((2 * size - used, LANES), F32)
    for at, lane, source, column, depth, total in blocks:
        packed[at : at + depth, lane : lane + total] = acc[source : source + depth, column : column + total]
    half_0[...] = packed[:size].astype(half_0.dtype)
    half_1[...] = packed[size:].astype(half_1.dtype)


def inner_others_kernel(dims, *refs):
    frames, rows, channels, width, mid, own_c, rank_count, axial_count, group = dims
    xp, up, sw, tw, hid_out, grad_out, taps_out, act_out, wf, twf = refs
    w_taps, w_act = prepare(sw, tw, wf, twf)
    taps_out[...] = w_taps
    act_out[...] = w_act
    first, count, _ = inner_rows(axial_count, rows)
    for i in range(count):
        for f in range(1, frames - 1, 2):
            picked = (f, f + 1)
            field, cot = gathered(xp, up, first + i, picked)
            for f, hid, grad in zip(picked, *activations(w_taps, w_act, field, cot, width)):
                hid_out[i, f - 1] = with_rows(hid, padded(mid)).astype(BF16)
                grad_out[i, f - 1] = with_rows(grad, padded(mid)).astype(BF16)


def others_kernel(dims, *refs):
    frames, rows, channels, width, mid, own_c, rank_count, axial_count, group = dims
    hid_in, grad_in, xp, up, taps_in, act_in, hid_out, grad_out = refs
    w_taps, w_act = taps_in[...], act_in[...]
    first, count, others = inner_rows(axial_count, rows)
    groups = [(first + i, (0, frames - 1)) for i in range(count)]
    groups += [(h, (f, f + 1)) for h in others for f in range(0, frames, 2)]
    for h, picked in groups:
        field, cot = gathered(xp, up, h, picked)
        for f, hid, grad in zip(picked, *activations(w_taps, w_act, field, cot, width)):
            hid_out[h, f] = with_rows(hid, padded(mid)).astype(BF16)
            grad_out[h, f] = with_rows(grad, padded(mid)).astype(BF16)
    for i in range(count):
        for f in range(1, frames - 1):
            hid_out[first + i, f] = hid_in[i, f - 1]
            grad_out[first + i, f] = grad_in[i, f - 1]


def fields_kernel(dims, fast, *refs):
    frames, rows, channels, width, mid, own_c, rank_count, axial_count, group = dims
    hid_in, grad_in, hid_other, grad_other, sw, tw, sw_other, tw_other = refs[:8]
    out, out_a, out_b, ig, ig_a, ig_b, twt, wg, ig_acc, out_edges = refs[8:]
    own = pl.ds(pl.multiple_of(lax.axis_index("chan") * own_c, own_c), own_c)
    blank = jnp.zeros((own_c, padded(mid) - mid), F32)

    def both(a, b):
        return jnp.concatenate([a.astype(F32), blank, b.astype(F32), blank], 1).astype(BF16)

    for k in range(3):
        twt[k * own_c : (k + 1) * own_c] = both(tw[k, own], tw_other[k, own])
    for i in range(3):
        for j in range(3):
            at = (i * 3 + j) * own_c
            wg[at : at + own_c] = both(sw[i, j, own], sw_other[i, j, own])
    w_out, w_in = twt[...], wg[...]

    for h in range(rows):
        out_terms = {}
        for first in range(0, frames, group):
            picked = range(first, first + group)
            hid = jnp.concatenate([jnp.concatenate([hid_in[h, f], hid_other[h, f]], 0) for f in picked], 1)
            grad = jnp.concatenate([jnp.concatenate([grad_in[h, f], grad_other[h, f]], 0) for f in picked], 1)
            y_out = dot(w_out, hid)
            y_in = dot(w_in, grad)
            for g, f in enumerate(picked):
                cols = slice(g * width, (g + 1) * width)
                for k in range(3):
                    out_terms.setdefault(f - k + 1, []).append(y_out[k * own_c : (k + 1) * own_c, cols])
                for i in range(3):
                    at = i * 3 * own_c
                    total = (
                        y_in[at + own_c : at + 2 * own_c, cols]
                        + moved(y_in[at : at + own_c, cols], -1)
                        + moved(y_in[at + 2 * own_c : at + 3 * own_c, cols], 1)
                    )
                    if h == 0 or i == 2:
                        ig_acc[f, h + i] = total
                    else:
                        ig_acc[f, h + i] += total
        for f, terms in out_terms.items():
            total = functools.reduce(lambda a, b: a + b, terms)
            if f < 0:
                out_edges[0, h] = total.astype(BF16)
            elif f >= frames:
                out_edges[1, h] = total.astype(BF16)
            else:
                out[f, h] = total

    odd = lax.rem(lax.axis_index("tm"), 2) if fast else 1
    high = jnp.where(lax.axis_index("axial") == 0, rows + 1, 0) if fast else 0
    out_a[...] = out_edges[1 - odd]
    out_b[...] = out_edges[odd]
    for f in range(frames):
        ig_a[f] = ig_acc[f, high].astype(BF16)
        ig_b[f] = ig_acc[f, rows + 1].astype(BF16)
        for h in range(rows):
            ig[f, h] = ig_acc[f, h + 1]


def unpack(packed, acc, sg, tg):
    channels, mid = tg.shape[1:]
    for at, lane, source, column, depth, total in pieces(*acc.shape)[0]:
        acc[source : source + depth, column : column + total] = packed[at : at + depth, lane : lane + total]
    for i in range(3):
        rows = slice(i * channels, (i + 1) * channels)
        for j in range(3):
            sg[i, j] = acc[rows, j * mid : (j + 1) * mid]
        tg[2 - i] = acc[rows, 3 * mid :]


def add_edges(axial_count, own, from_lo, from_hi, ig_own, ig_from_lo, ig_from_hi, out, ig):
    frames, rows = own.shape[:2]
    axial = lax.axis_index("axial")
    has_lo = (axial > 0).astype(F32)
    has_hi = (axial < axial_count - 1).astype(F32)
    for f in range(frames):
        for h in range(rows):
            total = own[f, h]
            if f == 0:
                total = total + from_lo(h).astype(F32)
            if f == frames - 1:
                total = total + from_hi(h).astype(F32)
            out[f, h] = total.astype(BF16)
            total = ig_own[f, h]
            if h == 0:
                total = total + ig_from_lo(f).astype(F32) * has_lo
            if h == rows - 1:
                total = total + ig_from_hi(f).astype(F32) * has_hi
            ig[f, h] = total.astype(BF16)


def last_kernel(own, ig_own, half_0, half_1, got_0, near, apart, far, out, ig, sg, tg, packed, acc, edges):
    frames, rows, own_c, width = own.shape
    size = half_0.shape[0]
    odd = lax.rem(lax.axis_index("tm"), 2)
    edges[1 - odd] = near[size:].reshape(rows, own_c, width)
    edges[odd] = far[size:].reshape(rows, own_c, width)
    add_edges(
        2,
        own,
        lambda h: edges[0, h],
        lambda h: edges[1, h],
        ig_own,
        lambda f: got_0[size + f * own_c : size + (f + 1) * own_c],
        lambda f: got_0[size + f * own_c : size + (f + 1) * own_c],
        out,
        ig,
    )
    packed[:size] = half_0[...].astype(F32) + got_0[:size].astype(F32)
    packed[size:] = (half_1[...].astype(F32) + near[:size].astype(F32)) + (
        apart[...].astype(F32) + far[:size].astype(F32)
    )
    unpack(packed, acc, sg, tg)


def last_kernel_general(axial_count, *refs):
    own, ig_own, half_0, half_1, from_lo, from_hi, ig_from_lo, ig_from_hi, out, ig, sg, tg, packed, acc, edges = refs
    add_edges(
        axial_count,
        own,
        lambda h: from_lo[h],
        lambda h: from_hi[h],
        ig_own,
        lambda f: ig_from_lo[f],
        lambda f: ig_from_hi[f],
        out,
        ig,
    )
    size = half_0.shape[0]
    packed[:size] = half_0[...]
    packed[size:] = half_1[...]
    unpack(packed, acc, sg, tg)


def call(kernel, name, out_shape, count, limit, scratch=(), in_specs=None, flops=0):
    return pl.pallas_call(
        kernel,
        out_shape=out_shape,
        in_specs=in_specs or [VMEM] * count,
        out_specs=[VMEM] * len(out_shape),
        scratch_shapes=list(scratch),
        compiler_params=pltpu.CompilerParams(vmem_limit_bytes=int(limit * 1024 * 1024)),
        cost_estimate=pl.CostEstimate(flops=flops, bytes_accessed=1 << 20, transcendentals=0) if flops else None,
        name=name,
    )


def shards(frames_in, spatial_weight, temporal_weight, upstream):
    frames, rows, channels, width = frames_in.shape
    mid = temporal_weight.shape[1]
    axial_count = lax.axis_size("axial")
    tm_count = lax.axis_size("tm")
    core_count = lax.axis_size("chan")
    rank_count = tm_count * axial_count
    axial = lax.axis_index("axial")
    own_c = channels // core_count
    group = 2 if frames % 2 == 0 else 1
    dims = (frames, rows, channels, width, mid, own_c, rank_count, axial_count, group)
    size = half_rows(3 * channels, 4 * mid)
    sds = jax.ShapeDtypeStruct

    split = axial_count == 2 and frames % 2 == 0
    edge_count = frames // 2 if split else frames
    turned = jnp.swapaxes(temporal_weight, 1, 2)
    edge, frame = call(
        functools.partial(stage_kernel, split),
        "stage",
        [sds((edge_count, channels, width), BF16), sds((rows, channels, width), BF16)],
        4,
        60,
        [pltpu.SemaphoreType.DMA((2,))],
        [HBM] * 4,
    )(frames_in, upstream, spatial_weight, turned)
    edge, frame, sw_sent, tw_sent = lax.optimization_barrier((edge, frame, spatial_weight, turned))
    frame = lax.ppermute(frame, ("tm", "chan"), facing(tm_count))
    if split:
        edge = lax.ppermute(edge, "axial", ring(2, 1))
    else:
        edge = lax.ppermute(edge, ("axial", "chan"), facing(axial_count))
    sw_other = lax.ppermute(sw_sent, "chan", ring(2, 1))
    tw_other = lax.ppermute(tw_sent, "chan", ring(2, 1))

    own_shape = (frames, rows, own_c, width)
    inner = (inner_rows(axial_count, rows)[1], frames - 2, padded(mid), width)
    cells = (rows, frames, padded(mid), width)
    xp_shape = (frames, rows + 2, channels, width)
    up_shape = (frames + 2, rows, channels, width)
    total = (3 * channels, 4 * mid)
    forms = [pltpu.VMEM((3 * mid, 3 * channels), F32), pltpu.VMEM((mid, 3 * channels), F32)]
    fast = axial_count == 2 and tm_count == 4
    hid, grad, acc, xp, up, w_taps, w_act = call(
        functools.partial(inner_kernel, dims),
        "inner_cells",
        [
            sds(inner, BF16),
            sds(inner, BF16),
            sds(total, F32),
            sds(xp_shape, BF16),
            sds(up_shape, BF16),
            sds((3 * mid, 3 * channels), BF16),
            sds((mid, 3 * channels), BF16),
        ],
        4,
        16,
        forms,
        flops=1 << 31,
    )(frames_in, upstream, spatial_weight, turned)
    hid_other, grad_other, taps_other, act_other = call(
        functools.partial(inner_others_kernel, dims),
        "inner_others",
        [sds(inner, BF16), sds(inner, BF16), sds((3 * mid, 3 * channels), BF16), sds((mid, 3 * channels), BF16)],
        4,
        16,
        forms,
        flops=1 << 30,
    )(xp, up, sw_other, tw_other)
    edge, frame, acc, hid_other = lax.optimization_barrier((edge, frame, acc, hid_other))
    swapped = lax.ppermute(jnp.concatenate([edge, frame], 0), "chan", ring(2, 1))
    hid, grad, xp, up, half_0, half_1 = call(
        functools.partial(grads_kernel, dims),
        "weight_grads",
        [
            sds(cells, BF16),
            sds(cells, BF16),
            sds(xp_shape, BF16),
            sds(up_shape, BF16),
            sds((size, LANES), BF16 if fast else F32),
            sds((size, LANES), BF16 if fast else F32),
        ],
        10,
        16,
        [
            pltpu.VMEM((2 * edge_count, channels, width), BF16),
            pltpu.VMEM(total, F32),
            pltpu.VMEM((2 * size, LANES), F32),
        ],
    )(hid, grad, acc, xp, up, edge, frame, swapped, w_taps, w_act)

    if fast:
        far_0 = lax.ppermute(half_0, "tm", pairs(4, 3))
        apart_0 = lax.ppermute(half_0, "tm", pairs(4, 2))
        near_0 = lax.ppermute(half_0, "tm", pairs(4, 1))
        got_1 = lax.ppermute(half_1, "axial", ring(2, 1))

    hid_other, grad_other = call(
        functools.partial(others_kernel, dims),
        "other_cells",
        [sds(cells, BF16), sds(cells, BF16)],
        6,
        16,
        flops=1 << 31,
    )(hid_other, grad_other, xp, up, taps_other, act_other)

    own_shape = (frames, rows, own_c, width)
    out_edge, ig_edge = sds((rows, own_c, width), BF16), sds((frames, own_c, width), BF16)
    out_own, out_a, out_b, ig_own, ig_a, ig_b = call(
        functools.partial(fields_kernel, dims, fast),
        "field_products",
        [sds(own_shape, F32), out_edge, out_edge, sds(own_shape, F32), ig_edge, ig_edge],
        8,
        16,
        [
            pltpu.VMEM((3 * own_c, 2 * padded(mid)), BF16),
            pltpu.VMEM((9 * own_c, 2 * padded(mid)), BF16),
            pltpu.VMEM((frames, rows + 2, own_c, width), F32),
            pltpu.VMEM((2, rows, own_c, width), BF16),
        ],
        flops=1 << 31,
    )(hid, grad, hid_other, grad_other, spatial_weight, turned, sw_other, tw_other)

    outs = [
        sds(own_shape, BF16),
        sds(own_shape, BF16),
        sds((3, 3, channels, mid), F32),
        sds((3, channels, mid), F32),
    ]
    scratch = [
        pltpu.VMEM((2 * size, LANES), F32),
        pltpu.VMEM(total, F32),
        pltpu.VMEM((2, rows, own_c, width), BF16),
    ]
    if fast:
        far_0, apart_0, near_0, got_1, out_a, out_b, ig_a = lax.optimization_barrier(
            (far_0, apart_0, near_0, got_1, out_a, out_b, ig_a)
        )
        half_0 = (half_0.astype(F32) + near_0.astype(F32)) + (apart_0.astype(F32) + far_0.astype(F32))
        half_1 = half_1.astype(F32) + got_1.astype(F32)
        half_0, half_1 = lax.optimization_barrier((half_0.astype(BF16), half_1.astype(BF16)))
        far_1 = lax.ppermute(jnp.concatenate([half_1, out_b.reshape(-1, width)], 0), "tm", pairs(4, 3))
        apart_1 = lax.ppermute(half_1, "tm", pairs(4, 2))
        near_1 = lax.ppermute(jnp.concatenate([half_1, out_a.reshape(-1, width)], 0), "tm", pairs(4, 1))
        got_0 = lax.ppermute(jnp.concatenate([half_0, ig_a.reshape(-1, width)], 0), "axial", ring(2, 1))
        results = call(last_kernel, "last", outs, 8, 8, scratch)(
            out_own, ig_own, half_0, half_1, got_0, near_1, apart_1, far_1
        )
    else:
        half_0, half_1 = lax.psum((half_0, half_1), ("tm", "axial"))
        from_hi = lax.ppermute(out_a, "tm", ring(tm_count, -1))
        from_lo = lax.ppermute(out_b, "tm", ring(tm_count, 1))
        ig_from_hi = lax.ppermute(ig_a, "axial", ring(axial_count, -1))
        ig_from_lo = lax.ppermute(ig_b, "axial", ring(axial_count, 1))
        results = call(functools.partial(last_kernel_general, axial_count), "last", outs, 8, 8, scratch)(
            out_own, ig_own, half_0, half_1, from_lo, from_hi, ig_from_lo, ig_from_hi
        )
    output, input_grad, spatial_grad, temporal_grad = results
    return output, input_grad, spatial_grad, jnp.swapaxes(temporal_grad, 1, 2)


def solution(mesh):
    placed = (
        P(("parts", "tm"), "axial", None, None),
        P("parts", None, None, "chan"),
        P("parts", "chan", None),
        P(("parts", "tm"), "axial", None, None),
    )
    return jax.shard_map(
        shards,
        mesh=mesh,
        in_specs=placed,
        out_specs=(
            P(("parts", "tm"), "axial", "chan", None),
            P(("parts", "tm"), "axial", "chan", None),
            P("parts", None, None, "chan"),
            P("parts", "chan", None),
        ),
        check_vma=False,
    )
```

```python
import functools
import math

import jax
import jax.numpy as jnp
from jax import lax
from jax.experimental import pallas as pl
from jax.experimental.pallas import tpu as pltpu
from jax.sharding import PartitionSpec as P

F32 = jnp.float32
BF16 = jnp.bfloat16
LANES = 128
HBM = pl.BlockSpec(memory_space=pltpu.HBM)
VMEM = pl.BlockSpec(memory_space=pltpu.VMEM)


def ring(count, step):
    return [(i, (i + step) % count) for i in range(count)]


def pairs(count, stride):
    return [(i, i ^ stride) for i in range(count)]


def facing(count):
    order = []
    for i in range(count):
        order += [(2 * i, 2 * ((i - 1) % count) + 1), (2 * i + 1, 2 * ((i + 1) % count))]
    return order


def dot(a, b):
    return jnp.dot(a, b, preferred_element_type=F32)


def dot_nt(a, b):
    return lax.dot_general(a, b, (((1,), (1,)), ((), ())), preferred_element_type=F32)


def moved(value, step):
    width = value.shape[1]
    column = lax.broadcasted_iota(jnp.int32, value.shape, 1)
    edge = 0 if step > 0 else width - 1
    return jnp.where(column == edge, 0.0, pltpu.roll(value, step % width, 1))


def pieces(depth, total):
    blocks, row = [], 0
    for first in range(0, total - total % LANES, LANES):
        blocks.append((row, 0, 0, first, depth, LANES))
        row += depth
    rest = total % LANES
    if rest:
        fold = LANES // rest
        if LANES % rest or depth % (8 * fold):
            fold = 1
        part = depth // fold
        for g in range(fold):
            blocks.append((row, g * rest, g * part, total - rest, part, rest))
        row += part
    return blocks, row


def padded(count):
    return -(-count // 16) * 16


def with_rows(value, count):
    if value.shape[0] == count:
        return value
    return jnp.concatenate([value, jnp.zeros((count - value.shape[0], value.shape[1]), value.dtype)], 0)


def half_rows(depth, total):
    return -(-pieces(depth, total)[1] // 32) * 16


def stage_kernel(split, x, u, sw, tw, edge, frame, sems):
    frames, rows = x.shape[:2]
    core = lax.axis_index("chan")
    if split:
        row = jnp.where(lax.axis_index("axial") == 0, rows - 1, 0)
        picked = pl.ds(core * (frames // 2), frames // 2)
    else:
        row = core * (rows - 1)
        picked = pl.ds(0, frames)
    copies = [
        pltpu.make_async_copy(u.at[core * (frames - 1)], frame, sems.at[0]),
        pltpu.make_async_copy(x.at[picked, row], edge, sems.at[1]),
    ]
    for copy in copies:
        copy.start()
    for copy in copies:
        copy.wait()


def prepare(sw, tw, wf, twf):
    channels, mid = tw.shape[1:]
    for j in range(3):
        wf[j * mid : (j + 1) * mid] = sw[:, j].reshape(3 * channels, mid).astype(F32).T
    twf[...] = jnp.concatenate([tw[k].astype(F32) for k in (2, 1, 0)], 0).T
    return wf[...].astype(BF16), twf[...].astype(BF16)


def activations(w_taps, w_act, field, cot, width):
    mid = w_act.shape[0]
    taps = dot(w_taps, field)
    act = dot(w_act, cot)
    hids, grads = [], []
    for first in range(0, field.shape[1], width):
        cols = slice(first, first + width)
        pre = taps[mid : 2 * mid, cols] + moved(taps[:mid, cols], 1) + moved(taps[2 * mid :, cols], -1)
        s = 0.5 * jnp.tanh(0.5 * pre) + 0.5
        hids.append(pre * s)
        grads.append(act[:, cols] * s * (1.0 + pre * (1.0 - s)))
    return hids, grads


def gathered(xp, up, h, picked):
    depth = 3 * xp.shape[2]
    width = xp.shape[3]
    field = jnp.concatenate([xp[f, pl.ds(h, 3)].reshape(depth, width) for f in picked], 1)
    cot = jnp.concatenate([jnp.concatenate([up[f + d, h] for d in range(3)], 0) for f in picked], 1)
    return field, cot


def inner_rows(axial_count, rows):
    if axial_count == 2:
        low = lax.axis_index("axial") == 0
        return jnp.where(low, 0, 1), rows - 1, [jnp.where(low, rows - 1, 0)]
    return 1, rows - 2, [0, rows - 1]


def cell_grads(xp, up, w_taps, w_act, groups, store):
    fields, cots, shifts, owns = [], [], [], []
    width = xp.shape[3]
    for h, picked in groups:
        field, cot = gathered(xp, up, h, picked)
        hids, grads = activations(w_taps, w_act, field, cot, width)
        shifts.append(
            jnp.concatenate(
                [
                    jnp.concatenate([moved(v, -1) for v in grads], 1),
                    jnp.concatenate(grads, 1),
                    jnp.concatenate([moved(v, 1) for v in grads], 1),
                ],
                0,
            ).astype(BF16)
        )
        hids = [with_rows(v, padded(v.shape[0])).astype(BF16) for v in hids]
        owns.append(jnp.concatenate(hids, 1))
        for f, hid, grad in zip(picked, hids, grads):
            store(h, f, hid, with_rows(grad, padded(grad.shape[0])).astype(BF16))
        fields.append(field)
        cots.append(cot)
    return (
        dot_nt(jnp.concatenate(fields, 1), jnp.concatenate(shifts, 1)),
        dot_nt(jnp.concatenate(cots, 1), jnp.concatenate(owns, 1))[:, : w_act.shape[0]],
    )


def inner_kernel(dims, *refs):
    frames, rows, channels, width, mid, own_c, rank_count, axial_count, group = dims
    x, u, sw, tw = refs[:4]
    hid_out, grad_out, acc_out, xp, up, taps_out, act_out, wf, twf = refs[4:]
    for f in range(frames):
        for at in (0, rows + 1):
            xp[f, at] = jnp.zeros((channels, width), BF16)
        for h in range(rows):
            xp[f, h + 1] = x[f, h]
            up[f + 1, h] = u[f, h]
    for at in (0, frames + 1):
        up[at] = jnp.zeros(up.shape[1:], BF16)
    w_taps, w_act = prepare(sw, tw, wf, twf)
    taps_out[...] = w_taps
    act_out[...] = w_act

    first, count, _ = inner_rows(axial_count, rows)

    def store(h, f, hid, grad):
        hid_out[h - first, f - 1] = hid
        grad_out[h - first, f - 1] = grad

    groups = [(first + i, (f, f + 1)) for i in range(count) for f in range(1, frames - 1, 2)]
    w_part, t_part = cell_grads(xp, up, w_taps, w_act, groups, store)
    acc_out[:, : 3 * mid] = w_part
    acc_out[:, 3 * mid :] = t_part


def grads_kernel(dims, *refs):
    frames, rows, channels, width, mid, own_c, rank_count, axial_count, group = dims
    hid_in, grad_in, acc_in, x, u, edge, frame, swapped, taps_in, act_in = refs[:10]
    hid_out, grad_out, xp, up, kept, sent, edges, acc, packed = refs[10:]
    axial = lax.axis_index("axial")
    core = lax.axis_index("chan")
    w_taps, w_act = taps_in[...], act_in[...]

    has_lo = (axial > 0).astype(BF16)
    has_hi = (axial < axial_count - 1).astype(BF16)
    part = edge.shape[0]
    edges[pl.ds(core * part, part)] = edge[...]
    edges[pl.ds((1 - core) * part, part)] = swapped[0:part]
    at_hi = 2 * part - frames
    for f in range(frames):
        xp[f, 0] = edges[f] * has_lo
        xp[f, rows + 1] = edges[at_hi + f] * has_hi
        for h in range(rows):
            xp[f, h + 1] = x[f, h + 1]
            up[f + 1, h] = u[f + 1, h]
    up[core * (frames + 1)] = frame[...]
    up[(1 - core) * (frames + 1)] = swapped[part:]

    first, count, others = inner_rows(axial_count, rows)

    def store(h, f, hid, grad):
        hid_out[h, f] = hid
        grad_out[h, f] = grad

    for i in range(count):
        for f in range(1, frames - 1):
            store(first + i, f, hid_in[i, f - 1], grad_in[i, f - 1])
    groups = [(first + i, (0, frames - 1)) for i in range(count)]
    groups += [(h, (f, f + 1)) for h in others for f in range(0, frames, 2)]
    w_part, t_part = cell_grads(xp, up, w_taps, w_act, groups, store)
    factor = 1.0 / math.sqrt(frames * rows * width * rank_count)
    acc[:, : 3 * mid] = (acc_in[:, : 3 * mid] + w_part) * factor
    acc[:, 3 * mid :] = (acc_in[:, 3 * mid :] + t_part) * factor

    blocks, used = pieces(*acc.shape)
    size = packed.shape[0] // 2
    packed[used:] = jnp.zeros((2 * size - used, LANES), F32)
    for at, lane, source, column, depth, total in blocks:
        packed[at : at + depth, lane : lane + total] = acc[source : source + depth, column : column + total]
    mine = lax.rem(axial, 2)
    kept[...] = packed[pl.ds(pl.multiple_of(mine * size, 16), size)]
    sent[...] = packed[pl.ds(pl.multiple_of((1 - mine) * size, 16), size)].astype(sent.dtype)


def inner_others_kernel(dims, *refs):
    frames, rows, channels, width, mid, own_c, rank_count, axial_count, group = dims
    xp, up, sw, tw, hid_out, grad_out, taps_out, act_out, wf, twf = refs
    w_taps, w_act = prepare(sw, tw, wf, twf)
    taps_out[...] = w_taps
    act_out[...] = w_act
    first, count, _ = inner_rows(axial_count, rows)
    for i in range(count):
        for f in range(1, frames - 1, 2):
            picked = (f, f + 1)
            field, cot = gathered(xp, up, first + i, picked)
            for f, hid, grad in zip(picked, *activations(w_taps, w_act, field, cot, width)):
                hid_out[i, f - 1] = with_rows(hid, padded(mid)).astype(BF16)
                grad_out[i, f - 1] = with_rows(grad, padded(mid)).astype(BF16)


def others_kernel(dims, *refs):
    frames, rows, channels, width, mid, own_c, rank_count, axial_count, group = dims
    hid_in, grad_in, xp, up, taps_in, act_in, hid_out, grad_out = refs
    w_taps, w_act = taps_in[...], act_in[...]
    first, count, others = inner_rows(axial_count, rows)
    groups = [(first + i, (0, frames - 1)) for i in range(count)]
    groups += [(h, (f, f + 1)) for h in others for f in range(0, frames, 2)]
    for h, picked in groups:
        field, cot = gathered(xp, up, h, picked)
        for f, hid, grad in zip(picked, *activations(w_taps, w_act, field, cot, width)):
            hid_out[h, f] = with_rows(hid, padded(mid)).astype(BF16)
            grad_out[h, f] = with_rows(grad, padded(mid)).astype(BF16)
    for i in range(count):
        for f in range(1, frames - 1):
            hid_out[first + i, f] = hid_in[i, f - 1]
            grad_out[first + i, f] = grad_in[i, f - 1]


def fields_kernel(dims, fast, *refs):
    frames, rows, channels, width, mid, own_c, rank_count, axial_count, group = dims
    hid_in, grad_in, hid_other, grad_other, sw, tw, sw_other, tw_other = refs[:8]
    out, out_lo, out_hi, ig, ig_a, ig_b, twt, wg, ig_acc = refs[8:]
    own = pl.ds(pl.multiple_of(lax.axis_index("chan") * own_c, own_c), own_c)
    blank = jnp.zeros((own_c, padded(mid) - mid), F32)

    def both(a, b):
        return jnp.concatenate([a.astype(F32), blank, b.astype(F32), blank], 1).astype(BF16)

    for k in range(3):
        twt[k * own_c : (k + 1) * own_c] = both(tw[k, own], tw_other[k, own])
    for i in range(3):
        for j in range(3):
            at = (i * 3 + j) * own_c
            wg[at : at + own_c] = both(sw[i, j, own], sw_other[i, j, own])
    w_out, w_in = twt[...], wg[...]

    for h in range(rows):
        out_terms = {}
        for first in range(0, frames, group):
            picked = range(first, first + group)
            hid = jnp.concatenate([jnp.concatenate([hid_in[h, f], hid_other[h, f]], 0) for f in picked], 1)
            grad = jnp.concatenate([jnp.concatenate([grad_in[h, f], grad_other[h, f]], 0) for f in picked], 1)
            y_out = dot(w_out, hid)
            y_in = dot(w_in, grad)
            for g, f in enumerate(picked):
                cols = slice(g * width, (g + 1) * width)
                for k in range(3):
                    out_terms.setdefault(f - k + 1, []).append(y_out[k * own_c : (k + 1) * own_c, cols])
                for i in range(3):
                    at = i * 3 * own_c
                    total = (
                        y_in[at + own_c : at + 2 * own_c, cols]
                        + moved(y_in[at : at + own_c, cols], -1)
                        + moved(y_in[at + 2 * own_c : at + 3 * own_c, cols], 1)
                    )
                    if h == 0 or i == 2:
                        ig_acc[f, h + i] = total
                    else:
                        ig_acc[f, h + i] += total
        for f, terms in out_terms.items():
            total = functools.reduce(lambda a, b: a + b, terms)
            if f < 0:
                out_lo[h] = total.astype(BF16)
            elif f >= frames:
                out_hi[h] = total.astype(BF16)
            else:
                out[f, h] = total

    high = jnp.where(lax.axis_index("axial") == 0, rows + 1, 0) if fast else 0
    for f in range(frames):
        ig_a[f] = ig_acc[f, high].astype(BF16)
        ig_b[f] = ig_acc[f, rows + 1].astype(BF16)
        for h in range(rows):
            ig[f, h] = ig_acc[f, h + 1]


def outputs_kernel(axial_count, own, from_lo, from_hi, ig_own, ig_from_lo, ig_from_hi, out, ig):
    frames, rows = own.shape[:2]
    axial = lax.axis_index("axial")
    has_lo = (axial > 0).astype(F32)
    has_hi = (axial < axial_count - 1).astype(F32)
    for f in range(frames):
        for h in range(rows):
            total = own[f, h]
            if f == 0:
                total = total + from_lo[h].astype(F32)
            if f == frames - 1:
                total = total + from_hi[h].astype(F32)
            out[f, h] = total.astype(BF16)
            total = ig_own[f, h]
            if h == 0:
                total = total + ig_from_lo[f].astype(F32) * has_lo
            if h == rows - 1:
                total = total + ig_from_hi[f].astype(F32) * has_hi
            ig[f, h] = total.astype(BF16)


def unpack_kernel(mine, other, sg, tg, packed, acc):
    channels, mid = tg.shape[1:]
    size = mine.shape[0]
    half = lax.rem(lax.axis_index("axial"), 2)
    packed[pl.ds(pl.multiple_of(half * size, 16), size)] = mine[...].astype(F32)
    packed[pl.ds(pl.multiple_of((1 - half) * size, 16), size)] = other[...].astype(F32)
    for at, lane, source, column, depth, total in pieces(*acc.shape)[0]:
        acc[source : source + depth, column : column + total] = packed[at : at + depth, lane : lane + total]
    for i in range(3):
        rows = slice(i * channels, (i + 1) * channels)
        for j in range(3):
            sg[i, j] = acc[rows, j * mid : (j + 1) * mid]
        tg[2 - i] = acc[rows, 3 * mid :]


def call(kernel, name, out_shape, count, limit, scratch=(), in_specs=None, flops=0):
    return pl.pallas_call(
        kernel,
        out_shape=out_shape,
        in_specs=in_specs or [VMEM] * count,
        out_specs=[VMEM] * len(out_shape),
        scratch_shapes=list(scratch),
        compiler_params=pltpu.CompilerParams(vmem_limit_bytes=int(limit * 1024 * 1024)),
        cost_estimate=pl.CostEstimate(flops=flops, bytes_accessed=1 << 20, transcendentals=0) if flops else None,
        name=name,
    )


def shards(frames_in, spatial_weight, temporal_weight, upstream):
    frames, rows, channels, width = frames_in.shape
    mid = temporal_weight.shape[1]
    axial_count = lax.axis_size("axial")
    tm_count = lax.axis_size("tm")
    core_count = lax.axis_size("chan")
    rank_count = tm_count * axial_count
    axial = lax.axis_index("axial")
    own_c = channels // core_count
    group = 2 if frames % 2 == 0 else 1
    dims = (frames, rows, channels, width, mid, own_c, rank_count, axial_count, group)
    size = half_rows(3 * channels, 4 * mid)
    sds = jax.ShapeDtypeStruct

    split = axial_count == 2 and frames % 2 == 0
    edge_count = frames // 2 if split else frames
    turned = jnp.swapaxes(temporal_weight, 1, 2)
    edge, frame = call(
        functools.partial(stage_kernel, split),
        "stage",
        [sds((edge_count, channels, width), BF16), sds((rows, channels, width), BF16)],
        4,
        60,
        [pltpu.SemaphoreType.DMA((2,))],
        [HBM] * 4,
    )(frames_in, upstream, spatial_weight, turned)
    edge, frame, sw_sent, tw_sent = lax.optimization_barrier((edge, frame, spatial_weight, turned))
    frame = lax.ppermute(frame, ("tm", "chan"), facing(tm_count))
    if split:
        edge = lax.ppermute(edge, "axial", ring(2, 1))
    else:
        edge = lax.ppermute(edge, ("axial", "chan"), facing(axial_count))
    sw_other = lax.ppermute(sw_sent, "chan", ring(2, 1))
    tw_other = lax.ppermute(tw_sent, "chan", ring(2, 1))

    own_shape = (frames, rows, own_c, width)
    inner = (inner_rows(axial_count, rows)[1], frames - 2, padded(mid), width)
    cells = (rows, frames, padded(mid), width)
    xp_shape = (frames, rows + 2, channels, width)
    up_shape = (frames + 2, rows, channels, width)
    total = (3 * channels, 4 * mid)
    forms = [pltpu.VMEM((3 * mid, 3 * channels), F32), pltpu.VMEM((mid, 3 * channels), F32)]
    fast = axial_count == 2 and tm_count == 4
    hid, grad, acc, xp, up, w_taps, w_act = call(
        functools.partial(inner_kernel, dims),
        "inner_cells",
        [
            sds(inner, BF16),
            sds(inner, BF16),
            sds(total, F32),
            sds(xp_shape, BF16),
            sds(up_shape, BF16),
            sds((3 * mid, 3 * channels), BF16),
            sds((mid, 3 * channels), BF16),
        ],
        4,
        16,
        forms,
        flops=1 << 31,
    )(frames_in, upstream, spatial_weight, turned)
    hid_other, grad_other, taps_other, act_other = call(
        functools.partial(inner_others_kernel, dims),
        "inner_others",
        [sds(inner, BF16), sds(inner, BF16), sds((3 * mid, 3 * channels), BF16), sds((mid, 3 * channels), BF16)],
        4,
        16,
        forms,
        flops=1 << 30,
    )(xp, up, sw_other, tw_other)
    edge, frame, acc, hid_other = lax.optimization_barrier((edge, frame, acc, hid_other))
    swapped = lax.ppermute(jnp.concatenate([edge, frame], 0), "chan", ring(2, 1))
    hid, grad, xp, up, kept, sent = call(
        functools.partial(grads_kernel, dims),
        "weight_grads",
        [
            sds(cells, BF16),
            sds(cells, BF16),
            sds(xp_shape, BF16),
            sds(up_shape, BF16),
            sds((size, LANES), F32),
            sds((size, LANES), BF16 if fast else F32),
        ],
        10,
        16,
        [
            pltpu.VMEM((2 * edge_count, channels, width), BF16),
            pltpu.VMEM(total, F32),
            pltpu.VMEM((2 * size, LANES), F32),
        ],
    )(hid, grad, acc, xp, up, edge, frame, swapped, w_taps, w_act)

    if fast:
        got = lax.ppermute(sent, "axial", ring(2, 1))

    hid_other, grad_other = call(
        functools.partial(others_kernel, dims),
        "other_cells",
        [sds(cells, BF16), sds(cells, BF16)],
        6,
        16,
        flops=1 << 31,
    )(hid_other, grad_other, xp, up, taps_other, act_other)

    own_shape = (frames, rows, own_c, width)
    out_edge, ig_edge = sds((rows, own_c, width), BF16), sds((frames, own_c, width), BF16)
    out_own, out_lo, out_hi, ig_own, ig_a, ig_b = call(
        functools.partial(fields_kernel, dims, fast),
        "field_products",
        [sds(own_shape, F32), out_edge, out_edge, sds(own_shape, F32), ig_edge, ig_edge],
        8,
        16,
        [
            pltpu.VMEM((3 * own_c, 2 * padded(mid)), BF16),
            pltpu.VMEM((9 * own_c, 2 * padded(mid)), BF16),
            pltpu.VMEM((frames, rows + 2, own_c, width), F32),
        ],
        flops=1 << 31,
    )(hid, grad, hid_other, grad_other, spatial_weight, turned, sw_other, tw_other)

    if fast:
        got, out_lo, out_hi, ig_a = lax.optimization_barrier((got, out_lo, out_hi, ig_a))
    from_hi = lax.ppermute(out_lo, "tm", ring(tm_count, -1))
    from_lo = lax.ppermute(out_hi, "tm", ring(tm_count, 1))
    if fast:
        ig_from_lo = ig_from_hi = lax.ppermute(ig_a, "axial", ring(2, 1))
        mine = lax.optimization_barrier((kept + got.astype(F32)).astype(BF16))
        for stride in (1, 2):
            mine = lax.optimization_barrier(mine + lax.ppermute(mine, "tm", pairs(tm_count, stride)))
        other = lax.ppermute(mine, "axial", ring(2, 1))
    else:
        ig_from_hi = lax.ppermute(ig_a, "axial", ring(axial_count, -1))
        ig_from_lo = lax.ppermute(ig_b, "axial", ring(axial_count, 1))
        odd = lax.rem(axial, 2) == 1
        low, high = jnp.where(odd, sent, kept), jnp.where(odd, kept, sent)
        low, high = lax.psum((low, high), ("tm", "axial"))
        mine, other = jnp.where(odd, high, low), jnp.where(odd, low, high)

    output, input_grad = call(
        functools.partial(outputs_kernel, axial_count),
        "outputs",
        [sds(own_shape, BF16), sds(own_shape, BF16)],
        6,
        4,
        flops=1 << 29,
    )(out_own, from_lo, from_hi, ig_own, ig_from_lo, ig_from_hi)
    spatial_grad, temporal_grad = call(
        unpack_kernel,
        "unpack",
        [sds((3, 3, channels, mid), F32), sds((3, channels, mid), F32)],
        2,
        4,
        [pltpu.VMEM((2 * size, LANES), F32), pltpu.VMEM(total, F32)],
    )(mine, other)
    return output, input_grad, spatial_grad, jnp.swapaxes(temporal_grad, 1, 2)


def solution(mesh):
    placed = (
        P(("parts", "tm"), "axial", None, None),
        P("parts", None, None, "chan"),
        P("parts", "chan", None),
        P(("parts", "tm"), "axial", None, None),
    )
    return jax.shard_map(
        shards,
        mesh=mesh,
        in_specs=placed,
        out_specs=(
            P(("parts", "tm"), "axial", "chan", None),
            P(("parts", "tm"), "axial", "chan", None),
            P("parts", None, None, "chan"),
            P("parts", "chan", None),
        ),
        check_vma=False,
    )
```

```python
import functools
import math

import jax
import jax.numpy as jnp
from jax import lax
from jax.experimental import pallas as pl
from jax.experimental.pallas import tpu as pltpu
from jax.sharding import PartitionSpec as P

F32 = jnp.float32
BF16 = jnp.bfloat16
LANES = 128
HBM = pl.BlockSpec(memory_space=pltpu.HBM)
VMEM = pl.BlockSpec(memory_space=pltpu.VMEM)


def ring(count, step):
    return [(i, (i + step) % count) for i in range(count)]


def pairs(count, stride):
    return [(i, i ^ stride) for i in range(count)]


def facing(count):
    order = []
    for i in range(count):
        order += [(2 * i, 2 * ((i - 1) % count) + 1), (2 * i + 1, 2 * ((i + 1) % count))]
    return order


def dot(a, b):
    return jnp.dot(a, b, preferred_element_type=F32)


def dot_nt(a, b):
    return lax.dot_general(a, b, (((1,), (1,)), ((), ())), preferred_element_type=F32)


def moved(value, step):
    width = value.shape[1]
    column = lax.broadcasted_iota(jnp.int32, value.shape, 1)
    edge = 0 if step > 0 else width - 1
    return jnp.where(column == edge, 0.0, pltpu.roll(value, step % width, 1))


def pieces(depth, total):
    blocks, row = [], 0
    for first in range(0, total - total % LANES, LANES):
        blocks.append((row, 0, 0, first, depth, LANES))
        row += depth
    rest = total % LANES
    if rest:
        fold = LANES // rest
        if LANES % rest or depth % (8 * fold):
            fold = 1
        part = depth // fold
        for g in range(fold):
            blocks.append((row, g * rest, g * part, total - rest, part, rest))
        row += part
    return blocks, row


def padded(count):
    return -(-count // 16) * 16


def with_rows(value, count):
    if value.shape[0] == count:
        return value
    return jnp.concatenate([value, jnp.zeros((count - value.shape[0], value.shape[1]), value.dtype)], 0)


def half_rows(depth, total):
    return -(-pieces(depth, total)[1] // 32) * 16


def stage_kernel(split, x, u, sw, tw, edge, frame, sems):
    frames, rows = x.shape[:2]
    core = lax.axis_index("chan")
    if split:
        row = jnp.where(lax.axis_index("axial") == 0, rows - 1, 0)
        picked = pl.ds(core * (frames // 2), frames // 2)
    else:
        row = core * (rows - 1)
        picked = pl.ds(0, frames)
    copies = [
        pltpu.make_async_copy(u.at[core * (frames - 1)], frame, sems.at[0]),
        pltpu.make_async_copy(x.at[picked, row], edge, sems.at[1]),
    ]
    for copy in copies:
        copy.start()
    for copy in copies:
        copy.wait()


def prepare(sw, tw, wf, twf):
    channels, mid = tw.shape[1:]
    for j in range(3):
        wf[j * mid : (j + 1) * mid] = sw[:, j].reshape(3 * channels, mid).astype(F32).T
    twf[...] = jnp.concatenate([tw[k].astype(F32) for k in (2, 1, 0)], 0).T
    return wf[...].astype(BF16), twf[...].astype(BF16)


def activations(w_taps, w_act, field, cot, width):
    mid = w_act.shape[0]
    taps = dot(w_taps, field)
    act = dot(w_act, cot)
    hids, grads = [], []
    for first in range(0, field.shape[1], width):
        cols = slice(first, first + width)
        pre = taps[mid : 2 * mid, cols] + moved(taps[:mid, cols], 1) + moved(taps[2 * mid :, cols], -1)
        s = 0.5 * jnp.tanh(0.5 * pre) + 0.5
        hids.append(pre * s)
        grads.append(act[:, cols] * s * (1.0 + pre * (1.0 - s)))
    return hids, grads


def gathered(xp, up, h, picked):
    depth = 3 * xp.shape[2]
    width = xp.shape[3]
    field = jnp.concatenate([xp[f, pl.ds(h, 3)].reshape(depth, width) for f in picked], 1)
    cot = jnp.concatenate([jnp.concatenate([up[f + d, h] for d in range(3)], 0) for f in picked], 1)
    return field, cot


def inner_rows(axial_count, rows):
    if axial_count == 2:
        low = lax.axis_index("axial") == 0
        return jnp.where(low, 0, 1), rows - 1, [jnp.where(low, rows - 1, 0)]
    return 1, rows - 2, [0, rows - 1]


def cell_grads(xp, up, w_taps, w_act, groups, store):
    fields, cots, shifts, owns = [], [], [], []
    width = xp.shape[3]
    for h, picked in groups:
        field, cot = gathered(xp, up, h, picked)
        hids, grads = activations(w_taps, w_act, field, cot, width)
        shifts.append(
            jnp.concatenate(
                [
                    jnp.concatenate([moved(v, -1) for v in grads], 1),
                    jnp.concatenate(grads, 1),
                    jnp.concatenate([moved(v, 1) for v in grads], 1),
                ],
                0,
            ).astype(BF16)
        )
        hids = [with_rows(v, padded(v.shape[0])).astype(BF16) for v in hids]
        owns.append(jnp.concatenate(hids, 1))
        for f, hid, grad in zip(picked, hids, grads):
            store(h, f, hid, with_rows(grad, padded(grad.shape[0])).astype(BF16))
        fields.append(field)
        cots.append(cot)
    return (
        dot_nt(jnp.concatenate(fields, 1), jnp.concatenate(shifts, 1)),
        dot_nt(jnp.concatenate(cots, 1), jnp.concatenate(owns, 1))[:, : w_act.shape[0]],
    )


def inner_kernel(dims, *refs):
    frames, rows, channels, width, mid, own_c, rank_count, axial_count, group = dims
    x, u, sw, tw, _ = refs[:5]
    hid_out, grad_out, acc_out, xp, up, taps_out, act_out, wf, twf = refs[5:]
    for f in range(frames):
        for at in (0, rows + 1):
            xp[f, at] = jnp.zeros((channels, width), BF16)
        for h in range(rows):
            xp[f, h + 1] = x[f, h]
            up[f + 1, h] = u[f, h]
    for at in (0, frames + 1):
        up[at] = jnp.zeros(up.shape[1:], BF16)
    w_taps, w_act = prepare(sw, tw, wf, twf)
    taps_out[...] = w_taps
    act_out[...] = w_act

    first, count, _ = inner_rows(axial_count, rows)

    def store(h, f, hid, grad):
        hid_out[h - first, f - 1] = hid
        grad_out[h - first, f - 1] = grad

    groups = [(first + i, (f, f + 1)) for i in range(count) for f in range(1, frames - 1, 2)]
    w_part, t_part = cell_grads(xp, up, w_taps, w_act, groups, store)
    acc_out[:, : 3 * mid] = w_part
    acc_out[:, 3 * mid :] = t_part


def grads_kernel(dims, *refs):
    frames, rows, channels, width, mid, own_c, rank_count, axial_count, group = dims
    hid_in, grad_in, acc_in, x, u, edge, frame, swapped, taps_in, act_in = refs[:10]
    hid_out, grad_out, xp, up, half_0, half_1, edges, acc, packed = refs[10:]
    axial = lax.axis_index("axial")
    core = lax.axis_index("chan")
    w_taps, w_act = taps_in[...], act_in[...]

    has_lo = (axial > 0).astype(BF16)
    has_hi = (axial < axial_count - 1).astype(BF16)
    part = edge.shape[0]
    edges[pl.ds(core * part, part)] = edge[...]
    edges[pl.ds((1 - core) * part, part)] = swapped[0:part]
    at_hi = 2 * part - frames
    for f in range(frames):
        xp[f, 0] = edges[f] * has_lo
        xp[f, rows + 1] = edges[at_hi + f] * has_hi
        for h in range(rows):
            xp[f, h + 1] = x[f, h + 1]
            up[f + 1, h] = u[f + 1, h]
    up[core * (frames + 1)] = frame[...]
    up[(1 - core) * (frames + 1)] = swapped[part:]

    first, count, others = inner_rows(axial_count, rows)

    def store(h, f, hid, grad):
        hid_out[h, f] = hid
        grad_out[h, f] = grad

    for i in range(count):
        for f in range(1, frames - 1):
            store(first + i, f, hid_in[i, f - 1], grad_in[i, f - 1])
    groups = [(first + i, (0, frames - 1)) for i in range(count)]
    groups += [(h, (f, f + 1)) for h in others for f in range(0, frames, 2)]
    w_part, t_part = cell_grads(xp, up, w_taps, w_act, groups, store)
    factor = 1.0 / math.sqrt(frames * rows * width * rank_count)
    acc[:, : 3 * mid] = (acc_in[:, : 3 * mid] + w_part) * factor
    acc[:, 3 * mid :] = (acc_in[:, 3 * mid :] + t_part) * factor

    blocks, used = pieces(*acc.shape)
    size = packed.shape[0] // 2
    packed[used:] = jnp.zeros((2 * size - used, LANES), F32)
    for at, lane, source, column, depth, total in blocks:
        packed[at : at + depth, lane : lane + total] = acc[source : source + depth, column : column + total]
    half_0[...] = packed[:size].astype(half_0.dtype)
    half_1[...] = packed[size:].astype(half_1.dtype)


def inner_others_kernel(dims, *refs):
    frames, rows, channels, width, mid, own_c, rank_count, axial_count, group = dims
    xp, up, sw, tw, hid_out, grad_out, taps_out, act_out, wf, twf = refs
    w_taps, w_act = prepare(sw, tw, wf, twf)
    taps_out[...] = w_taps
    act_out[...] = w_act
    first, count, _ = inner_rows(axial_count, rows)
    for i in range(count):
        for f in range(1, frames - 1, 2):
            picked = (f, f + 1)
            field, cot = gathered(xp, up, first + i, picked)
            for f, hid, grad in zip(picked, *activations(w_taps, w_act, field, cot, width)):
                hid_out[i, f - 1] = with_rows(hid, padded(mid)).astype(BF16)
                grad_out[i, f - 1] = with_rows(grad, padded(mid)).astype(BF16)


def others_kernel(dims, *refs):
    frames, rows, channels, width, mid, own_c, rank_count, axial_count, group = dims
    hid_in, grad_in, xp, up, taps_in, act_in, hid_out, grad_out = refs
    w_taps, w_act = taps_in[...], act_in[...]
    first, count, others = inner_rows(axial_count, rows)
    groups = [(first + i, (0, frames - 1)) for i in range(count)]
    groups += [(h, (f, f + 1)) for h in others for f in range(0, frames, 2)]
    for h, picked in groups:
        field, cot = gathered(xp, up, h, picked)
        for f, hid, grad in zip(picked, *activations(w_taps, w_act, field, cot, width)):
            hid_out[h, f] = with_rows(hid, padded(mid)).astype(BF16)
            grad_out[h, f] = with_rows(grad, padded(mid)).astype(BF16)
    for i in range(count):
        for f in range(1, frames - 1):
            hid_out[first + i, f] = hid_in[i, f - 1]
            grad_out[first + i, f] = grad_in[i, f - 1]


def fields_kernel(dims, fast, *refs):
    frames, rows, channels, width, mid, own_c, rank_count, axial_count, group = dims
    hid_in, grad_in, hid_other, grad_other, sw, tw, sw_other, tw_other = refs[:8]
    out, out_a, out_b, ig, ig_a, ig_b, twt, wg, ig_acc, out_edges = refs[8:]
    own = pl.ds(pl.multiple_of(lax.axis_index("chan") * own_c, own_c), own_c)
    blank = jnp.zeros((own_c, padded(mid) - mid), F32)

    def both(a, b):
        return jnp.concatenate([a.astype(F32), blank, b.astype(F32), blank], 1).astype(BF16)

    for k in range(3):
        twt[k * own_c : (k + 1) * own_c] = both(tw[k, own], tw_other[k, own])
    for i in range(3):
        for j in range(3):
            at = (i * 3 + j) * own_c
            wg[at : at + own_c] = both(sw[i, j, own], sw_other[i, j, own])
    w_out, w_in = twt[...], wg[...]

    for h in range(rows):
        out_terms = {}
        for first in range(0, frames, group):
            picked = range(first, first + group)
            hid = jnp.concatenate([jnp.concatenate([hid_in[h, f], hid_other[h, f]], 0) for f in picked], 1)
            grad = jnp.concatenate([jnp.concatenate([grad_in[h, f], grad_other[h, f]], 0) for f in picked], 1)
            y_out = dot(w_out, hid)
            y_in = dot(w_in, grad)
            for g, f in enumerate(picked):
                cols = slice(g * width, (g + 1) * width)
                for k in range(3):
                    out_terms.setdefault(f - k + 1, []).append(y_out[k * own_c : (k + 1) * own_c, cols])
                for i in range(3):
                    at = i * 3 * own_c
                    total = (
                        y_in[at + own_c : at + 2 * own_c, cols]
                        + moved(y_in[at : at + own_c, cols], -1)
                        + moved(y_in[at + 2 * own_c : at + 3 * own_c, cols], 1)
                    )
                    if h == 0 or i == 2:
                        ig_acc[f, h + i] = total
                    else:
                        ig_acc[f, h + i] += total
        for f, terms in out_terms.items():
            total = functools.reduce(lambda a, b: a + b, terms)
            if f < 0:
                out_edges[0, h] = total.astype(BF16)
            elif f >= frames:
                out_edges[1, h] = total.astype(BF16)
            else:
                out[f, h] = total

    odd = lax.rem(lax.axis_index("tm"), 2) if fast else 1
    high = jnp.where(lax.axis_index("axial") == 0, rows + 1, 0) if fast else 0
    out_a[...] = out_edges[1 - odd]
    out_b[...] = out_edges[odd]
    for f in range(frames):
        ig_a[f] = ig_acc[f, high].astype(BF16)
        ig_b[f] = ig_acc[f, rows + 1].astype(BF16)
        for h in range(rows):
            ig[f, h] = ig_acc[f, h + 1]


def unpack(packed, acc, sg, tg):
    channels, mid = tg.shape[1:]
    for at, lane, source, column, depth, total in pieces(*acc.shape)[0]:
        acc[source : source + depth, column : column + total] = packed[at : at + depth, lane : lane + total]
    for i in range(3):
        rows = slice(i * channels, (i + 1) * channels)
        for j in range(3):
            sg[i, j] = acc[rows, j * mid : (j + 1) * mid]
        tg[2 - i] = acc[rows, 3 * mid :]


def add_edges(axial_count, own, from_lo, from_hi, ig_own, ig_from_lo, ig_from_hi, out, ig):
    frames, rows = own.shape[:2]
    axial = lax.axis_index("axial")
    has_lo = (axial > 0).astype(F32)
    has_hi = (axial < axial_count - 1).astype(F32)
    for f in range(frames):
        for h in range(rows):
            total = own[f, h]
            if f == 0:
                total = total + from_lo(h).astype(F32)
            if f == frames - 1:
                total = total + from_hi(h).astype(F32)
            out[f, h] = total.astype(BF16)
            total = ig_own[f, h]
            if h == 0:
                total = total + ig_from_lo(f).astype(F32) * has_lo
            if h == rows - 1:
                total = total + ig_from_hi(f).astype(F32) * has_hi
            ig[f, h] = total.astype(BF16)


def last_kernel(own, ig_own, half_0, half_1, across, near, far, out, ig, sg, tg, packed, acc, edges):
    frames, rows, own_c, width = own.shape
    size = half_0.shape[0]
    odd = lax.rem(lax.axis_index("tm"), 2)
    edges[1 - odd] = near[size:].reshape(rows, own_c, width)
    edges[odd] = far[size:].reshape(rows, own_c, width)
    add_edges(
        2,
        own,
        lambda h: edges[0, h],
        lambda h: edges[1, h],
        ig_own,
        lambda f: across[size + f * own_c : size + (f + 1) * own_c],
        lambda f: across[size + f * own_c : size + (f + 1) * own_c],
        out,
        ig,
    )
    packed[:size] = half_0[...].astype(F32) + across[:size].astype(F32)
    packed[size:] = half_1[...].astype(F32) + far[:size].astype(F32)
    unpack(packed, acc, sg, tg)


def last_kernel_general(axial_count, *refs):
    own, ig_own, half_0, half_1, from_lo, from_hi, ig_from_lo, ig_from_hi, out, ig, sg, tg, packed, acc, edges = refs
    add_edges(
        axial_count,
        own,
        lambda h: from_lo[h],
        lambda h: from_hi[h],
        ig_own,
        lambda f: ig_from_lo[f],
        lambda f: ig_from_hi[f],
        out,
        ig,
    )
    size = half_0.shape[0]
    packed[:size] = half_0[...]
    packed[size:] = half_1[...]
    unpack(packed, acc, sg, tg)


def call(kernel, name, out_shape, count, limit, scratch=(), in_specs=None, flops=0):
    return pl.pallas_call(
        kernel,
        out_shape=out_shape,
        in_specs=in_specs or [VMEM] * count,
        out_specs=[VMEM] * len(out_shape),
        scratch_shapes=list(scratch),
        compiler_params=pltpu.CompilerParams(vmem_limit_bytes=int(limit * 1024 * 1024)),
        cost_estimate=pl.CostEstimate(flops=flops, bytes_accessed=1 << 20, transcendentals=0) if flops else None,
        name=name,
    )


def shards(frames_in, spatial_weight, temporal_weight, upstream):
    frames, rows, channels, width = frames_in.shape
    mid = temporal_weight.shape[1]
    axial_count = lax.axis_size("axial")
    tm_count = lax.axis_size("tm")
    core_count = lax.axis_size("chan")
    rank_count = tm_count * axial_count
    axial = lax.axis_index("axial")
    own_c = channels // core_count
    group = 2 if frames % 2 == 0 else 1
    dims = (frames, rows, channels, width, mid, own_c, rank_count, axial_count, group)
    size = half_rows(3 * channels, 4 * mid)
    sds = jax.ShapeDtypeStruct

    split = axial_count == 2 and frames % 2 == 0
    edge_count = frames // 2 if split else frames
    turned = jnp.swapaxes(temporal_weight, 1, 2)
    edge, frame = call(
        functools.partial(stage_kernel, split),
        "stage",
        [sds((edge_count, channels, width), BF16), sds((rows, channels, width), BF16)],
        4,
        60,
        [pltpu.SemaphoreType.DMA((2,))],
        [HBM] * 4,
    )(frames_in, upstream, spatial_weight, turned)
    edge, frame, sw_sent, tw_sent = lax.optimization_barrier((edge, frame, spatial_weight, turned))
    frame = lax.ppermute(frame, ("tm", "chan"), facing(tm_count))
    tw_other = lax.ppermute(tw_sent, "chan", ring(2, 1))
    edge, tw_other = lax.optimization_barrier((edge, tw_other))
    if split:
        edge = lax.ppermute(edge, "axial", ring(2, 1))
    else:
        edge = lax.ppermute(edge, ("axial", "chan"), facing(axial_count))
    sw_other = lax.ppermute(sw_sent, "chan", ring(2, 1))

    own_shape = (frames, rows, own_c, width)
    inner = (inner_rows(axial_count, rows)[1], frames - 2, padded(mid), width)
    cells = (rows, frames, padded(mid), width)
    xp_shape = (frames, rows + 2, channels, width)
    up_shape = (frames + 2, rows, channels, width)
    total = (3 * channels, 4 * mid)
    forms = [pltpu.VMEM((3 * mid, 3 * channels), F32), pltpu.VMEM((mid, 3 * channels), F32)]
    fast = axial_count == 2 and tm_count == 4
    hid, grad, acc, xp, up, w_taps, w_act = call(
        functools.partial(inner_kernel, dims),
        "inner_cells",
        [
            sds(inner, BF16),
            sds(inner, BF16),
            sds(total, F32),
            sds(xp_shape, BF16),
            sds(up_shape, BF16),
            sds((3 * mid, 3 * channels), BF16),
            sds((mid, 3 * channels), BF16),
        ],
        5,
        16,
        forms,
        flops=1 << 31,
    )(frames_in, upstream, spatial_weight, turned, tw_other)
    hid_other, grad_other, taps_other, act_other = call(
        functools.partial(inner_others_kernel, dims),
        "inner_others",
        [sds(inner, BF16), sds(inner, BF16), sds((3 * mid, 3 * channels), BF16), sds((mid, 3 * channels), BF16)],
        4,
        16,
        forms,
        flops=1 << 30,
    )(xp, up, sw_other, tw_other)
    edge, frame, acc, hid_other = lax.optimization_barrier((edge, frame, acc, hid_other))
    swapped = lax.ppermute(jnp.concatenate([edge, frame], 0), "chan", ring(2, 1))
    hid, grad, xp, up, half_0, half_1 = call(
        functools.partial(grads_kernel, dims),
        "weight_grads",
        [
            sds(cells, BF16),
            sds(cells, BF16),
            sds(xp_shape, BF16),
            sds(up_shape, BF16),
            sds((size, LANES), BF16 if fast else F32),
            sds((size, LANES), BF16 if fast else F32),
        ],
        10,
        16,
        [
            pltpu.VMEM((2 * edge_count, channels, width), BF16),
            pltpu.VMEM(total, F32),
            pltpu.VMEM((2 * size, LANES), F32),
        ],
    )(hid, grad, acc, xp, up, edge, frame, swapped, w_taps, w_act)

    if fast:
        got_0 = lax.ppermute(half_0, "tm", pairs(4, 1))
        got_1 = lax.ppermute(half_1, "axial", ring(2, 1))

    hid_other, grad_other = call(
        functools.partial(others_kernel, dims),
        "other_cells",
        [sds(cells, BF16), sds(cells, BF16)],
        6,
        16,
        flops=1 << 31,
    )(hid_other, grad_other, xp, up, taps_other, act_other)

    own_shape = (frames, rows, own_c, width)
    out_edge, ig_edge = sds((rows, own_c, width), BF16), sds((frames, own_c, width), BF16)
    out_own, out_a, out_b, ig_own, ig_a, ig_b = call(
        functools.partial(fields_kernel, dims, fast),
        "field_products",
        [sds(own_shape, F32), out_edge, out_edge, sds(own_shape, F32), ig_edge, ig_edge],
        8,
        16,
        [
            pltpu.VMEM((3 * own_c, 2 * padded(mid)), BF16),
            pltpu.VMEM((9 * own_c, 2 * padded(mid)), BF16),
            pltpu.VMEM((frames, rows + 2, own_c, width), F32),
            pltpu.VMEM((2, rows, own_c, width), BF16),
        ],
        flops=1 << 31,
    )(hid, grad, hid_other, grad_other, spatial_weight, turned, sw_other, tw_other)

    outs = [
        sds(own_shape, BF16),
        sds(own_shape, BF16),
        sds((3, 3, channels, mid), F32),
        sds((3, channels, mid), F32),
    ]
    scratch = [
        pltpu.VMEM((2 * size, LANES), F32),
        pltpu.VMEM(total, F32),
        pltpu.VMEM((2, rows, own_c, width), BF16),
    ]
    if fast:
        got_0, out_a, out_b, ig_a = lax.optimization_barrier((got_0, out_a, out_b, ig_a))
        half_0 = lax.optimization_barrier(half_0 + got_0)
        apart = lax.ppermute(half_0, "tm", pairs(4, 2))
        half_1 = lax.optimization_barrier(half_1 + got_1)
        near = lax.ppermute(jnp.concatenate([half_1, out_a.reshape(-1, width)], 0), "tm", pairs(4, 1))
        half_1 = lax.optimization_barrier(half_1 + near[:size])
        far = lax.ppermute(jnp.concatenate([half_1, out_b.reshape(-1, width)], 0), "tm", pairs(4, 3))
        half_0 = lax.optimization_barrier(half_0 + apart)
        across = lax.ppermute(jnp.concatenate([half_0, ig_a.reshape(-1, width)], 0), "axial", ring(2, 1))
        results = call(last_kernel, "last", outs, 7, 8, scratch)(
            out_own, ig_own, half_0, half_1, across, near, far
        )
    else:
        half_0, half_1 = lax.psum((half_0, half_1), ("tm", "axial"))
        from_hi = lax.ppermute(out_a, "tm", ring(tm_count, -1))
        from_lo = lax.ppermute(out_b, "tm", ring(tm_count, 1))
        ig_from_hi = lax.ppermute(ig_a, "axial", ring(axial_count, -1))
        ig_from_lo = lax.ppermute(ig_b, "axial", ring(axial_count, 1))
        results = call(functools.partial(last_kernel_general, axial_count), "last", outs, 8, 8, scratch)(
            out_own, ig_own, half_0, half_1, from_lo, from_hi, ig_from_lo, ig_from_hi
        )
    output, input_grad, spatial_grad, temporal_grad = results
    return output, input_grad, spatial_grad, jnp.swapaxes(temporal_grad, 1, 2)


def solution(mesh):
    placed = (
        P(("parts", "tm"), "axial", None, None),
        P("parts", None, None, "chan"),
        P("parts", "chan", None),
        P(("parts", "tm"), "axial", None, None),
    )
    return jax.shard_map(
        shards,
        mesh=mesh,
        in_specs=placed,
        out_specs=(
            P(("parts", "tm"), "axial", "chan", None),
            P(("parts", "tm"), "axial", "chan", None),
            P("parts", None, None, "chan"),
            P("parts", "chan", None),
        ),
        check_vma=False,
    )
```

```python
import functools
import math

import jax
import jax.numpy as jnp
from jax import lax
from jax.experimental import pallas as pl
from jax.experimental.pallas import tpu as pltpu
from jax.sharding import PartitionSpec as P

F32 = jnp.float32
BF16 = jnp.bfloat16
LANES = 128
HBM = pl.BlockSpec(memory_space=pltpu.HBM)
VMEM = pl.BlockSpec(memory_space=pltpu.VMEM)


def ring(count, step):
    return [(i, (i + step) % count) for i in range(count)]


def pairs(count, stride):
    return [(i, i ^ stride) for i in range(count)]


def facing(count):
    order = []
    for i in range(count):
        order += [(2 * i, 2 * ((i - 1) % count) + 1), (2 * i + 1, 2 * ((i + 1) % count))]
    return order


def dot(a, b):
    return jnp.dot(a, b, preferred_element_type=F32)


def dot_nt(a, b):
    return lax.dot_general(a, b, (((1,), (1,)), ((), ())), preferred_element_type=F32)


def moved(value, step):
    width = value.shape[1]
    column = lax.broadcasted_iota(jnp.int32, value.shape, 1)
    edge = 0 if step > 0 else width - 1
    return jnp.where(column == edge, 0.0, pltpu.roll(value, step % width, 1))


def pieces(depth, total):
    blocks, row = [], 0
    for first in range(0, total - total % LANES, LANES):
        blocks.append((row, 0, 0, first, depth, LANES))
        row += depth
    rest = total % LANES
    if rest:
        fold = LANES // rest
        if LANES % rest or depth % (8 * fold):
            fold = 1
        part = depth // fold
        for g in range(fold):
            blocks.append((row, g * rest, g * part, total - rest, part, rest))
        row += part
    return blocks, row


def padded(count):
    return -(-count // 16) * 16


def with_rows(value, count):
    if value.shape[0] == count:
        return value
    return jnp.concatenate([value, jnp.zeros((count - value.shape[0], value.shape[1]), value.dtype)], 0)


def half_rows(depth, total):
    return -(-pieces(depth, total)[1] // 32) * 16


def stage_kernel(split, x, u, sw, tw, edge, frame, sems):
    frames, rows = x.shape[:2]
    core = lax.axis_index("chan")
    if split:
        row = jnp.where(lax.axis_index("axial") == 0, rows - 1, 0)
        picked = pl.ds(core * (frames // 2), frames // 2)
    else:
        row = core * (rows - 1)
        picked = pl.ds(0, frames)
    copies = [
        pltpu.make_async_copy(u.at[core * (frames - 1)], frame, sems.at[0]),
        pltpu.make_async_copy(x.at[picked, row], edge, sems.at[1]),
    ]
    for copy in copies:
        copy.start()
    for copy in copies:
        copy.wait()


def prepare(sw, tw, wf, twf):
    channels, mid = tw.shape[1:]
    for j in range(3):
        wf[j * mid : (j + 1) * mid] = sw[:, j].reshape(3 * channels, mid).astype(F32).T
    twf[...] = jnp.concatenate([tw[k].astype(F32) for k in (2, 1, 0)], 0).T
    return wf[...].astype(BF16), twf[...].astype(BF16)


def activations(w_taps, w_act, field, cot, width):
    mid = w_act.shape[0]
    taps = dot(w_taps, field)
    act = dot(w_act, cot)
    hids, grads = [], []
    for first in range(0, field.shape[1], width):
        cols = slice(first, first + width)
        pre = taps[mid : 2 * mid, cols] + moved(taps[:mid, cols], 1) + moved(taps[2 * mid :, cols], -1)
        s = 0.5 * jnp.tanh(0.5 * pre) + 0.5
        hids.append(pre * s)
        grads.append(act[:, cols] * s * (1.0 + pre * (1.0 - s)))
    return hids, grads


def gathered(xp, up, h, picked):
    depth = 3 * xp.shape[2]
    width = xp.shape[3]
    field = jnp.concatenate([xp[f, pl.ds(h, 3)].reshape(depth, width) for f in picked], 1)
    cot = jnp.concatenate([jnp.concatenate([up[f + d, h] for d in range(3)], 0) for f in picked], 1)
    return field, cot


def inner_rows(axial_count, rows):
    if axial_count == 2:
        low = lax.axis_index("axial") == 0
        return jnp.where(low, 0, 1), rows - 1, [jnp.where(low, rows - 1, 0)]
    return 1, rows - 2, [0, rows - 1]


def cell_grads(xp, up, w_taps, w_act, groups, store):
    fields, cots, shifts, owns = [], [], [], []
    width = xp.shape[3]
    for h, picked in groups:
        field, cot = gathered(xp, up, h, picked)
        hids, grads = activations(w_taps, w_act, field, cot, width)
        shifts.append(
            jnp.concatenate(
                [
                    jnp.concatenate([moved(v, -1) for v in grads], 1),
                    jnp.concatenate(grads, 1),
                    jnp.concatenate([moved(v, 1) for v in grads], 1),
                ],
                0,
            ).astype(BF16)
        )
        hids = [with_rows(v, padded(v.shape[0])).astype(BF16) for v in hids]
        owns.append(jnp.concatenate(hids, 1))
        for f, hid, grad in zip(picked, hids, grads):
            store(h, f, hid, with_rows(grad, padded(grad.shape[0])).astype(BF16))
        fields.append(field)
        cots.append(cot)
    return (
        dot_nt(jnp.concatenate(fields, 1), jnp.concatenate(shifts, 1)),
        dot_nt(jnp.concatenate(cots, 1), jnp.concatenate(owns, 1))[:, : w_act.shape[0]],
    )


def inner_kernel(dims, *refs):
    frames, rows, channels, width, mid, own_c, rank_count, axial_count, group = dims
    x, u, sw, tw = refs[:4]
    hid_out, grad_out, acc_out, xp, up, taps_out, act_out, wf, twf = refs[4:]
    for f in range(frames):
        for at in (0, rows + 1):
            xp[f, at] = jnp.zeros((channels, width), BF16)
        for h in range(rows):
            xp[f, h + 1] = x[f, h]
            up[f + 1, h] = u[f, h]
    for at in (0, frames + 1):
        up[at] = jnp.zeros(up.shape[1:], BF16)
    w_taps, w_act = prepare(sw, tw, wf, twf)
    taps_out[...] = w_taps
    act_out[...] = w_act

    first, count, _ = inner_rows(axial_count, rows)

    def store(h, f, hid, grad):
        hid_out[h - first, f - 1] = hid
        grad_out[h - first, f - 1] = grad

    groups = [(first + i, (f, f + 1)) for i in range(count) for f in range(1, frames - 1, 2)]
    w_part, t_part = cell_grads(xp, up, w_taps, w_act, groups, store)
    acc_out[:, : 3 * mid] = w_part
    acc_out[:, 3 * mid :] = t_part


def grads_kernel(dims, *refs):
    frames, rows, channels, width, mid, own_c, rank_count, axial_count, group = dims
    hid_in, grad_in, acc_in, x, u, edge, frame, swapped, taps_in, act_in = refs[:10]
    hid_out, grad_out, xp, up, half_0, half_1, edges, acc, packed = refs[10:]
    axial = lax.axis_index("axial")
    core = lax.axis_index("chan")
    w_taps, w_act = taps_in[...], act_in[...]

    has_lo = (axial > 0).astype(BF16)
    has_hi = (axial < axial_count - 1).astype(BF16)
    part = edge.shape[0]
    edges[pl.ds(core * part, part)] = edge[...]
    edges[pl.ds((1 - core) * part, part)] = swapped[0:part]
    at_hi = 2 * part - frames
    for f in range(frames):
        xp[f, 0] = edges[f] * has_lo
        xp[f, rows + 1] = edges[at_hi + f] * has_hi
        for h in range(rows):
            xp[f, h + 1] = x[f, h + 1]
            up[f + 1, h] = u[f + 1, h]
    up[core * (frames + 1)] = frame[...]
    up[(1 - core) * (frames + 1)] = swapped[part:]

    first, count, others = inner_rows(axial_count, rows)

    def store(h, f, hid, grad):
        hid_out[h, f] = hid
        grad_out[h, f] = grad

    for i in range(count):
        for f in range(1, frames - 1):
            store(first + i, f, hid_in[i, f - 1], grad_in[i, f - 1])
    groups = [(first + i, (0, frames - 1)) for i in range(count)]
    groups += [(h, (f, f + 1)) for h in others for f in range(0, frames, 2)]
    w_part, t_part = cell_grads(xp, up, w_taps, w_act, groups, store)
    factor = 1.0 / math.sqrt(frames * rows * width * rank_count)
    acc[:, : 3 * mid] = (acc_in[:, : 3 * mid] + w_part) * factor
    acc[:, 3 * mid :] = (acc_in[:, 3 * mid :] + t_part) * factor

    blocks, used = pieces(*acc.shape)
    size = packed.shape[0] // 2
    packed[used:] = jnp.zeros((2 * size - used, LANES), F32)
    for at, lane, source, column, depth, total in blocks:
        packed[at : at + depth, lane : lane + total] = acc[source : source + depth, column : column + total]
    half_0[...] = packed[:size].astype(half_0.dtype)
    half_1[...] = packed[size:].astype(half_1.dtype)


def others_kernel(dims, *refs):
    frames, rows, channels, width, mid, own_c, rank_count, axial_count, group = dims
    xp, up, sw, tw, hid_out, grad_out, wf, twf = refs
    w_taps, w_act = prepare(sw, tw, wf, twf)
    for h in range(rows):
        for first in range(0, frames, group):
            picked = range(first, first + group)
            field, cot = gathered(xp, up, h, picked)
            for f, hid, grad in zip(picked, *activations(w_taps, w_act, field, cot, width)):
                hid_out[h, f] = with_rows(hid, padded(mid)).astype(BF16)
                grad_out[h, f] = with_rows(grad, padded(mid)).astype(BF16)


def fields_kernel(dims, fast, *refs):
    frames, rows, channels, width, mid, own_c, rank_count, axial_count, group = dims
    hid_in, grad_in, hid_other, grad_other, sw, tw, sw_other, tw_other = refs[:8]
    out, out_a, out_b, ig, ig_a, ig_b, twt, wg, ig_acc, out_edges = refs[8:]
    own = pl.ds(pl.multiple_of(lax.axis_index("chan") * own_c, own_c), own_c)
    blank = jnp.zeros((own_c, padded(mid) - mid), F32)

    def both(a, b):
        return jnp.concatenate([a.astype(F32), blank, b.astype(F32), blank], 1).astype(BF16)

    for k in range(3):
        twt[k * own_c : (k + 1) * own_c] = both(tw[k, own], tw_other[k, own])
    for i in range(3):
        for j in range(3):
            at = (i * 3 + j) * own_c
            wg[at : at + own_c] = both(sw[i, j, own], sw_other[i, j, own])
    w_out, w_in = twt[...], wg[...]

    for h in range(rows):
        out_terms = {}
        for first in range(0, frames, group):
            picked = range(first, first + group)
            hid = jnp.concatenate([jnp.concatenate([hid_in[h, f], hid_other[h, f]], 0) for f in picked], 1)
            grad = jnp.concatenate([jnp.concatenate([grad_in[h, f], grad_other[h, f]], 0) for f in picked], 1)
            y_out = dot(w_out, hid)
            y_in = dot(w_in, grad)
            for g, f in enumerate(picked):
                cols = slice(g * width, (g + 1) * width)
                for k in range(3):
                    out_terms.setdefault(f - k + 1, []).append(y_out[k * own_c : (k + 1) * own_c, cols])
                for i in range(3):
                    at = i * 3 * own_c
                    total = (
                        y_in[at + own_c : at + 2 * own_c, cols]
                        + moved(y_in[at : at + own_c, cols], -1)
                        + moved(y_in[at + 2 * own_c : at + 3 * own_c, cols], 1)
                    )
                    if h == 0 or i == 2:
                        ig_acc[f, h + i] = total
                    else:
                        ig_acc[f, h + i] += total
        for f, terms in out_terms.items():
            total = functools.reduce(lambda a, b: a + b, terms)
            if f < 0:
                out_edges[0, h] = total.astype(BF16)
            elif f >= frames:
                out_edges[1, h] = total.astype(BF16)
            else:
                out[f, h] = total

    odd = lax.rem(lax.axis_index("tm"), 2) if fast else 1
    high = jnp.where(lax.axis_index("axial") == 0, rows + 1, 0) if fast else 0
    out_a[...] = out_edges[1 - odd]
    out_b[...] = out_edges[odd]
    for f in range(frames):
        ig_a[f] = ig_acc[f, high].astype(BF16)
        ig_b[f] = ig_acc[f, rows + 1].astype(BF16)
        for h in range(rows):
            ig[f, h] = ig_acc[f, h + 1]


def unpack(packed, acc, sg, tg):
    channels, mid = tg.shape[1:]
    for at, lane, source, column, depth, total in pieces(*acc.shape)[0]:
        acc[source : source + depth, column : column + total] = packed[at : at + depth, lane : lane + total]
    for i in range(3):
        rows = slice(i * channels, (i + 1) * channels)
        for j in range(3):
            sg[i, j] = acc[rows, j * mid : (j + 1) * mid]
        tg[2 - i] = acc[rows, 3 * mid :]


def add_edges(axial_count, own, from_lo, from_hi, ig_own, ig_from_lo, ig_from_hi, out, ig):
    frames, rows = own.shape[:2]
    axial = lax.axis_index("axial")
    has_lo = (axial > 0).astype(F32)
    has_hi = (axial < axial_count - 1).astype(F32)
    for f in range(frames):
        for h in range(rows):
            total = own[f, h]
            if f == 0:
                total = total + from_lo(h).astype(F32)
            if f == frames - 1:
                total = total + from_hi(h).astype(F32)
            out[f, h] = total.astype(BF16)
            total = ig_own[f, h]
            if h == 0:
                total = total + ig_from_lo(f).astype(F32) * has_lo
            if h == rows - 1:
                total = total + ig_from_hi(f).astype(F32) * has_hi
            ig[f, h] = total.astype(BF16)


def last_kernel(own, ig_own, half_0, half_1, across, near, far, out, ig, sg, tg, packed, acc, edges):
    frames, rows, own_c, width = own.shape
    size = half_0.shape[0]
    odd = lax.rem(lax.axis_index("tm"), 2)
    edges[1 - odd] = near[size:].reshape(rows, own_c, width)
    edges[odd] = far[size:].reshape(rows, own_c, width)
    add_edges(
        2,
        own,
        lambda h: edges[0, h],
        lambda h: edges[1, h],
        ig_own,
        lambda f: across[size + f * own_c : size + (f + 1) * own_c],
        lambda f: across[size + f * own_c : size + (f + 1) * own_c],
        out,
        ig,
    )
    packed[:size] = half_0[...].astype(F32) + across[:size].astype(F32)
    packed[size:] = half_1[...].astype(F32) + far[:size].astype(F32)
    unpack(packed, acc, sg, tg)


def last_kernel_general(axial_count, *refs):
    own, ig_own, half_0, half_1, from_lo, from_hi, ig_from_lo, ig_from_hi, out, ig, sg, tg, packed, acc, edges = refs
    add_edges(
        axial_count,
        own,
        lambda h: from_lo[h],
        lambda h: from_hi[h],
        ig_own,
        lambda f: ig_from_lo[f],
        lambda f: ig_from_hi[f],
        out,
        ig,
    )
    size = half_0.shape[0]
    packed[:size] = half_0[...]
    packed[size:] = half_1[...]
    unpack(packed, acc, sg, tg)


def call(kernel, name, out_shape, count, limit, scratch=(), in_specs=None, flops=0):
    return pl.pallas_call(
        kernel,
        out_shape=out_shape,
        in_specs=in_specs or [VMEM] * count,
        out_specs=[VMEM] * len(out_shape),
        scratch_shapes=list(scratch),
        compiler_params=pltpu.CompilerParams(vmem_limit_bytes=int(limit * 1024 * 1024)),
        cost_estimate=pl.CostEstimate(flops=flops, bytes_accessed=1 << 20, transcendentals=0) if flops else None,
        name=name,
    )


def shards(frames_in, spatial_weight, temporal_weight, upstream):
    frames, rows, channels, width = frames_in.shape
    mid = temporal_weight.shape[1]
    axial_count = lax.axis_size("axial")
    tm_count = lax.axis_size("tm")
    core_count = lax.axis_size("chan")
    rank_count = tm_count * axial_count
    axial = lax.axis_index("axial")
    own_c = channels // core_count
    group = 2 if frames % 2 == 0 else 1
    dims = (frames, rows, channels, width, mid, own_c, rank_count, axial_count, group)
    size = half_rows(3 * channels, 4 * mid)
    sds = jax.ShapeDtypeStruct

    split = axial_count == 2 and frames % 2 == 0
    edge_count = frames // 2 if split else frames
    turned = jnp.swapaxes(temporal_weight, 1, 2)
    edge, frame = call(
        functools.partial(stage_kernel, split),
        "stage",
        [sds((edge_count, channels, width), BF16), sds((rows, channels, width), BF16)],
        4,
        60,
        [pltpu.SemaphoreType.DMA((2,))],
        [HBM] * 4,
    )(frames_in, upstream, spatial_weight, turned)
    frame = lax.ppermute(frame, ("tm", "chan"), facing(tm_count))
    tw_other = lax.ppermute(turned, "chan", ring(2, 1))
    if split:
        edge = lax.ppermute(edge, "axial", ring(2, 1))
    else:
        edge = lax.ppermute(edge, ("axial", "chan"), facing(axial_count))
    sw_other = lax.ppermute(spatial_weight, "chan", ring(2, 1))

    own_shape = (frames, rows, own_c, width)
    inner = (inner_rows(axial_count, rows)[1], frames - 2, padded(mid), width)
    cells = (rows, frames, padded(mid), width)
    xp_shape = (frames, rows + 2, channels, width)
    up_shape = (frames + 2, rows, channels, width)
    total = (3 * channels, 4 * mid)
    forms = [pltpu.VMEM((3 * mid, 3 * channels), F32), pltpu.VMEM((mid, 3 * channels), F32)]
    fast = axial_count == 2 and tm_count == 4
    hid, grad, acc, xp, up, w_taps, w_act = call(
        functools.partial(inner_kernel, dims),
        "inner_cells",
        [
            sds(inner, BF16),
            sds(inner, BF16),
            sds(total, F32),
            sds(xp_shape, BF16),
            sds(up_shape, BF16),
            sds((3 * mid, 3 * channels), BF16),
            sds((mid, 3 * channels), BF16),
        ],
        4,
        16,
        forms,
        flops=1 << 31,
    )(frames_in, upstream, spatial_weight, turned)
    edge, frame, acc = lax.optimization_barrier((edge, frame, acc))
    swapped = lax.ppermute(jnp.concatenate([edge, frame], 0), "chan", ring(2, 1))
    hid, grad, xp, up, half_0, half_1 = call(
        functools.partial(grads_kernel, dims),
        "weight_grads",
        [
            sds(cells, BF16),
            sds(cells, BF16),
            sds(xp_shape, BF16),
            sds(up_shape, BF16),
            sds((size, LANES), BF16 if fast else F32),
            sds((size, LANES), BF16 if fast else F32),
        ],
        10,
        16,
        [
            pltpu.VMEM((2 * edge_count, channels, width), BF16),
            pltpu.VMEM(total, F32),
            pltpu.VMEM((2 * size, LANES), F32),
        ],
    )(hid, grad, acc, xp, up, edge, frame, swapped, w_taps, w_act)

    if fast:
        got_0 = lax.ppermute(half_0, "tm", pairs(4, 1))
        got_1 = lax.ppermute(half_1, "axial", ring(2, 1))

    hid_other, grad_other = call(
        functools.partial(others_kernel, dims),
        "other_cells",
        [sds(cells, BF16), sds(cells, BF16)],
        4,
        16,
        forms,
        flops=1 << 31,
    )(xp, up, sw_other, tw_other)

    own_shape = (frames, rows, own_c, width)
    out_edge, ig_edge = sds((rows, own_c, width), BF16), sds((frames, own_c, width), BF16)
    out_own, out_a, out_b, ig_own, ig_a, ig_b = call(
        functools.partial(fields_kernel, dims, fast),
        "field_products",
        [sds(own_shape, F32), out_edge, out_edge, sds(own_shape, F32), ig_edge, ig_edge],
        8,
        16,
        [
            pltpu.VMEM((3 * own_c, 2 * padded(mid)), BF16),
            pltpu.VMEM((9 * own_c, 2 * padded(mid)), BF16),
            pltpu.VMEM((frames, rows + 2, own_c, width), F32),
            pltpu.VMEM((2, rows, own_c, width), BF16),
        ],
        flops=1 << 31,
    )(hid, grad, hid_other, grad_other, spatial_weight, turned, sw_other, tw_other)

    outs = [
        sds(own_shape, BF16),
        sds(own_shape, BF16),
        sds((3, 3, channels, mid), F32),
        sds((3, channels, mid), F32),
    ]
    scratch = [
        pltpu.VMEM((2 * size, LANES), F32),
        pltpu.VMEM(total, F32),
        pltpu.VMEM((2, rows, own_c, width), BF16),
    ]
    if fast:
        got_0, out_a, out_b, ig_a = lax.optimization_barrier((got_0, out_a, out_b, ig_a))
        half_0 = lax.optimization_barrier(half_0 + got_0)
        apart = lax.ppermute(half_0, "tm", pairs(4, 2))
        half_1 = lax.optimization_barrier(half_1 + got_1)
        near = lax.ppermute(jnp.concatenate([half_1, out_a.reshape(-1, width)], 0), "tm", pairs(4, 1))
        half_1 = lax.optimization_barrier(half_1 + near[:size])
        far = lax.ppermute(jnp.concatenate([half_1, out_b.reshape(-1, width)], 0), "tm", pairs(4, 3))
        half_0 = lax.optimization_barrier(half_0 + apart)
        across = lax.ppermute(jnp.concatenate([half_0, ig_a.reshape(-1, width)], 0), "axial", ring(2, 1))
        results = call(last_kernel, "last", outs, 7, 8, scratch)(
            out_own, ig_own, half_0, half_1, across, near, far
        )
    else:
        half_0, half_1 = lax.psum((half_0, half_1), ("tm", "axial"))
        from_hi = lax.ppermute(out_a, "tm", ring(tm_count, -1))
        from_lo = lax.ppermute(out_b, "tm", ring(tm_count, 1))
        ig_from_hi = lax.ppermute(ig_a, "axial", ring(axial_count, -1))
        ig_from_lo = lax.ppermute(ig_b, "axial", ring(axial_count, 1))
        results = call(functools.partial(last_kernel_general, axial_count), "last", outs, 8, 8, scratch)(
            out_own, ig_own, half_0, half_1, from_lo, from_hi, ig_from_lo, ig_from_hi
        )
    output, input_grad, spatial_grad, temporal_grad = results
    return output, input_grad, spatial_grad, jnp.swapaxes(temporal_grad, 1, 2)


def solution(mesh):
    placed = (
        P(("parts", "tm"), "axial", None, None),
        P("parts", None, None, "chan"),
        P("parts", "chan", None),
        P(("parts", "tm"), "axial", None, None),
    )
    return jax.shard_map(
        shards,
        mesh=mesh,
        in_specs=placed,
        out_specs=(
            P(("parts", "tm"), "axial", "chan", None),
            P(("parts", "tm"), "axial", "chan", None),
            P("parts", None, None, "chan"),
            P("parts", "chan", None),
        ),
        check_vma=False,
    )
```

```python
import functools
import math

import jax
import jax.numpy as jnp
from jax import lax
from jax.experimental import pallas as pl
from jax.experimental.pallas import tpu as pltpu
from jax.sharding import PartitionSpec as P

F32 = jnp.float32
BF16 = jnp.bfloat16
LANES = 128
HBM = pl.BlockSpec(memory_space=pltpu.HBM)
VMEM = pl.BlockSpec(memory_space=pltpu.VMEM)


def ring(count, step):
    return [(i, (i + step) % count) for i in range(count)]


def pairs(count, stride):
    return [(i, i ^ stride) for i in range(count)]


def facing(count):
    order = []
    for i in range(count):
        order += [(2 * i, 2 * ((i - 1) % count) + 1), (2 * i + 1, 2 * ((i + 1) % count))]
    return order


def dot(a, b):
    return jnp.dot(a, b, preferred_element_type=F32)


def dot_nt(a, b):
    return lax.dot_general(a, b, (((1,), (1,)), ((), ())), preferred_element_type=F32)


def moved(value, step):
    width = value.shape[1]
    column = lax.broadcasted_iota(jnp.int32, value.shape, 1)
    edge = 0 if step > 0 else width - 1
    return jnp.where(column == edge, 0.0, pltpu.roll(value, step % width, 1))


def pieces(depth, total):
    blocks, row = [], 0
    for first in range(0, total - total % LANES, LANES):
        blocks.append((row, 0, 0, first, depth, LANES))
        row += depth
    rest = total % LANES
    if rest:
        fold = LANES // rest
        if LANES % rest or depth % (8 * fold):
            fold = 1
        part = depth // fold
        for g in range(fold):
            blocks.append((row, g * rest, g * part, total - rest, part, rest))
        row += part
    return blocks, row


def padded(count):
    return -(-count // 16) * 16


def with_rows(value, count):
    if value.shape[0] == count:
        return value
    return jnp.concatenate([value, jnp.zeros((count - value.shape[0], value.shape[1]), value.dtype)], 0)


def half_rows(depth, total):
    return -(-pieces(depth, total)[1] // 32) * 16


def stage_kernel(split, x, u, sw, tw, edge, frame, sems):
    frames, rows = x.shape[:2]
    core = lax.axis_index("chan")
    if split:
        row = jnp.where(lax.axis_index("axial") == 0, rows - 1, 0)
        picked = pl.ds(core * (frames // 2), frames // 2)
    else:
        row = core * (rows - 1)
        picked = pl.ds(0, frames)
    copies = [
        pltpu.make_async_copy(u.at[core * (frames - 1)], frame, sems.at[0]),
        pltpu.make_async_copy(x.at[picked, row], edge, sems.at[1]),
    ]
    for copy in copies:
        copy.start()
    for copy in copies:
        copy.wait()


def prepare(sw, tw, wf, twf):
    channels, mid = tw.shape[1:]
    for j in range(3):
        wf[j * mid : (j + 1) * mid] = sw[:, j].reshape(3 * channels, mid).astype(F32).T
    twf[...] = jnp.concatenate([tw[k].astype(F32) for k in (2, 1, 0)], 0).T
    return wf[...].astype(BF16), twf[...].astype(BF16)


def activations(w_taps, w_act, field, cot, width):
    mid = w_act.shape[0]
    taps = dot(w_taps, field)
    act = dot(w_act, cot)
    hids, grads = [], []
    for first in range(0, field.shape[1], width):
        cols = slice(first, first + width)
        pre = taps[mid : 2 * mid, cols] + moved(taps[:mid, cols], 1) + moved(taps[2 * mid :, cols], -1)
        s = 0.5 * jnp.tanh(0.5 * pre) + 0.5
        hids.append(pre * s)
        grads.append(act[:, cols] * s * (1.0 + pre * (1.0 - s)))
    return hids, grads


def gathered(xp, up, h, picked):
    depth = 3 * xp.shape[2]
    width = xp.shape[3]
    field = jnp.concatenate([xp[f, pl.ds(h, 3)].reshape(depth, width) for f in picked], 1)
    cot = jnp.concatenate([jnp.concatenate([up[f + d, h] for d in range(3)], 0) for f in picked], 1)
    return field, cot


def inner_rows(axial_count, rows):
    if axial_count == 2:
        low = lax.axis_index("axial") == 0
        return jnp.where(low, 0, 1), rows - 1, [jnp.where(low, rows - 1, 0)]
    return 1, rows - 2, [0, rows - 1]


def cell_grads(xp, up, w_taps, w_act, groups, store):
    fields, cots, shifts, owns = [], [], [], []
    width = xp.shape[3]
    for h, picked in groups:
        field, cot = gathered(xp, up, h, picked)
        hids, grads = activations(w_taps, w_act, field, cot, width)
        shifts.append(
            jnp.concatenate(
                [
                    jnp.concatenate([moved(v, -1) for v in grads], 1),
                    jnp.concatenate(grads, 1),
                    jnp.concatenate([moved(v, 1) for v in grads], 1),
                ],
                0,
            ).astype(BF16)
        )
        hids = [with_rows(v, padded(v.shape[0])).astype(BF16) for v in hids]
        owns.append(jnp.concatenate(hids, 1))
        for f, hid, grad in zip(picked, hids, grads):
            store(h, f, hid, with_rows(grad, padded(grad.shape[0])).astype(BF16))
        fields.append(field)
        cots.append(cot)
    return (
        dot_nt(jnp.concatenate(fields, 1), jnp.concatenate(shifts, 1)),
        dot_nt(jnp.concatenate(cots, 1), jnp.concatenate(owns, 1))[:, : w_act.shape[0]],
    )


def inner_kernel(dims, *refs):
    frames, rows, channels, width, mid, own_c, rank_count, axial_count, group = dims
    x, u, sw, tw = refs[:4]
    hid_out, grad_out, acc_out, xp, up, taps_out, act_out, wf, twf = refs[4:]
    for f in range(frames):
        for at in (0, rows + 1):
            xp[f, at] = jnp.zeros((channels, width), BF16)
        for h in range(rows):
            xp[f, h + 1] = x[f, h]
            up[f + 1, h] = u[f, h]
    for at in (0, frames + 1):
        up[at] = jnp.zeros(up.shape[1:], BF16)
    w_taps, w_act = prepare(sw, tw, wf, twf)
    taps_out[...] = w_taps
    act_out[...] = w_act

    first, count, _ = inner_rows(axial_count, rows)

    def store(h, f, hid, grad):
        hid_out[h - first, f - 1] = hid
        grad_out[h - first, f - 1] = grad

    groups = [(first + i, (f, f + 1)) for i in range(count) for f in range(1, frames - 1, 2)]
    w_part, t_part = cell_grads(xp, up, w_taps, w_act, groups, store)
    acc_out[:, : 3 * mid] = w_part
    acc_out[:, 3 * mid :] = t_part


def grads_kernel(dims, *refs):
    frames, rows, channels, width, mid, own_c, rank_count, axial_count, group = dims
    hid_in, grad_in, acc_in, x, u, edge, frame, swapped, taps_in, act_in = refs[:10]
    hid_out, grad_out, xp, up, half_0, half_1, edges, acc, packed = refs[10:]
    axial = lax.axis_index("axial")
    core = lax.axis_index("chan")
    w_taps, w_act = taps_in[...], act_in[...]

    has_lo = (axial > 0).astype(BF16)
    has_hi = (axial < axial_count - 1).astype(BF16)
    part = edge.shape[0]
    edges[pl.ds(core * part, part)] = edge[...]
    edges[pl.ds((1 - core) * part, part)] = swapped[0:part]
    at_hi = 2 * part - frames
    for f in range(frames):
        xp[f, 0] = edges[f] * has_lo
        xp[f, rows + 1] = edges[at_hi + f] * has_hi
        for h in range(rows):
            xp[f, h + 1] = x[f, h + 1]
            up[f + 1, h] = u[f + 1, h]
    up[core * (frames + 1)] = frame[...]
    up[(1 - core) * (frames + 1)] = swapped[part:]

    first, count, others = inner_rows(axial_count, rows)

    def store(h, f, hid, grad):
        hid_out[h, f] = hid
        grad_out[h, f] = grad

    for i in range(count):
        for f in range(1, frames - 1):
            store(first + i, f, hid_in[i, f - 1], grad_in[i, f - 1])
    groups = [(first + i, (0, frames - 1)) for i in range(count)]
    groups += [(h, (f, f + 1)) for h in others for f in range(0, frames, 2)]
    w_part, t_part = cell_grads(xp, up, w_taps, w_act, groups, store)
    factor = 1.0 / math.sqrt(frames * rows * width * rank_count)
    acc[:, : 3 * mid] = (acc_in[:, : 3 * mid] + w_part) * factor
    acc[:, 3 * mid :] = (acc_in[:, 3 * mid :] + t_part) * factor

    blocks, used = pieces(*acc.shape)
    size = packed.shape[0] // 2
    packed[used:] = jnp.zeros((2 * size - used, LANES), F32)
    for at, lane, source, column, depth, total in blocks:
        packed[at : at + depth, lane : lane + total] = acc[source : source + depth, column : column + total]
    half_0[...] = packed[:size].astype(half_0.dtype)
    half_1[...] = packed[size:].astype(half_1.dtype)


def others_kernel(dims, *refs):
    frames, rows, channels, width, mid, own_c, rank_count, axial_count, group = dims
    xp, up, sw, tw, hid_out, grad_out, wf, twf = refs
    w_taps, w_act = prepare(sw, tw, wf, twf)
    for h in range(rows):
        for first in range(0, frames, group):
            picked = range(first, first + group)
            field, cot = gathered(xp, up, h, picked)
            for f, hid, grad in zip(picked, *activations(w_taps, w_act, field, cot, width)):
                hid_out[h, f] = with_rows(hid, padded(mid)).astype(BF16)
                grad_out[h, f] = with_rows(grad, padded(mid)).astype(BF16)


def fields_kernel(dims, fast, *refs):
    frames, rows, channels, width, mid, own_c, rank_count, axial_count, group = dims
    hid_in, grad_in, hid_other, grad_other, sw, tw, sw_other, tw_other = refs[:8]
    out, out_a, out_b, ig, ig_a, ig_b, twt, wg, ig_acc, out_edges = refs[8:]
    own = pl.ds(pl.multiple_of(lax.axis_index("chan") * own_c, own_c), own_c)
    blank = jnp.zeros((own_c, padded(mid) - mid), F32)

    def both(a, b):
        return jnp.concatenate([a.astype(F32), blank, b.astype(F32), blank], 1).astype(BF16)

    for k in range(3):
        twt[k * own_c : (k + 1) * own_c] = both(tw[k, own], tw_other[k, own])
    for i in range(3):
        for j in range(3):
            at = (i * 3 + j) * own_c
            wg[at : at + own_c] = both(sw[i, j, own], sw_other[i, j, own])
    w_out, w_in = twt[...], wg[...]

    for h in range(rows):
        out_terms = {}
        for first in range(0, frames, group):
            picked = range(first, first + group)
            hid = jnp.concatenate([jnp.concatenate([hid_in[h, f], hid_other[h, f]], 0) for f in picked], 1)
            grad = jnp.concatenate([jnp.concatenate([grad_in[h, f], grad_other[h, f]], 0) for f in picked], 1)
            y_out = dot(w_out, hid)
            y_in = dot(w_in, grad)
            for g, f in enumerate(picked):
                cols = slice(g * width, (g + 1) * width)
                for k in range(3):
                    out_terms.setdefault(f - k + 1, []).append(y_out[k * own_c : (k + 1) * own_c, cols])
                for i in range(3):
                    at = i * 3 * own_c
                    total = (
                        y_in[at + own_c : at + 2 * own_c, cols]
                        + moved(y_in[at : at + own_c, cols], -1)
                        + moved(y_in[at + 2 * own_c : at + 3 * own_c, cols], 1)
                    )
                    if h == 0 or i == 2:
                        ig_acc[f, h + i] = total
                    else:
                        ig_acc[f, h + i] += total
        for f, terms in out_terms.items():
            total = functools.reduce(lambda a, b: a + b, terms)
            if f < 0:
                out_edges[0, h] = total.astype(BF16)
            elif f >= frames:
                out_edges[1, h] = total.astype(BF16)
            else:
                out[f, h] = total

    odd = lax.rem(lax.axis_index("tm"), 2) if fast else 1
    high = jnp.where(lax.axis_index("axial") == 0, rows + 1, 0) if fast else 0
    out_a[...] = out_edges[1 - odd]
    out_b[...] = out_edges[odd]
    for f in range(frames):
        ig_a[f] = ig_acc[f, high].astype(BF16)
        ig_b[f] = ig_acc[f, rows + 1].astype(BF16)
        for h in range(rows):
            ig[f, h] = ig_acc[f, h + 1]


def unpack(packed, acc, sg, tg):
    channels, mid = tg.shape[1:]
    for at, lane, source, column, depth, total in pieces(*acc.shape)[0]:
        acc[source : source + depth, column : column + total] = packed[at : at + depth, lane : lane + total]
    for i in range(3):
        rows = slice(i * channels, (i + 1) * channels)
        for j in range(3):
            sg[i, j] = acc[rows, j * mid : (j + 1) * mid]
        tg[2 - i] = acc[rows, 3 * mid :]


def add_edges(axial_count, own, from_lo, from_hi, ig_own, ig_from_lo, ig_from_hi, out, ig):
    frames, rows = own.shape[:2]
    axial = lax.axis_index("axial")
    has_lo = (axial > 0).astype(F32)
    has_hi = (axial < axial_count - 1).astype(F32)
    for f in range(frames):
        for h in range(rows):
            total = own[f, h]
            if f == 0:
                total = total + from_lo(h).astype(F32)
            if f == frames - 1:
                total = total + from_hi(h).astype(F32)
            out[f, h] = total.astype(BF16)
            total = ig_own[f, h]
            if h == 0:
                total = total + ig_from_lo(f).astype(F32) * has_lo
            if h == rows - 1:
                total = total + ig_from_hi(f).astype(F32) * has_hi
            ig[f, h] = total.astype(BF16)


def last_kernel(own, ig_own, half_0, half_1, across, near, far, ig_edge, out, ig, sg, tg, packed, acc, edges):
    frames, rows, own_c, width = own.shape
    size = half_0.shape[0]
    odd = lax.rem(lax.axis_index("tm"), 2)
    edges[1 - odd] = near[size:].reshape(rows, own_c, width)
    edges[odd] = far[size:].reshape(rows, own_c, width)
    add_edges(
        2,
        own,
        lambda h: edges[0, h],
        lambda h: edges[1, h],
        ig_own,
        lambda f: ig_edge[f],
        lambda f: ig_edge[f],
        out,
        ig,
    )
    packed[:size] = half_0[...].astype(F32) + across[...].astype(F32)
    packed[size:] = half_1[...].astype(F32) + far[:size].astype(F32)
    unpack(packed, acc, sg, tg)


def last_kernel_general(axial_count, *refs):
    own, ig_own, half_0, half_1, from_lo, from_hi, ig_from_lo, ig_from_hi, out, ig, sg, tg, packed, acc, edges = refs
    add_edges(
        axial_count,
        own,
        lambda h: from_lo[h],
        lambda h: from_hi[h],
        ig_own,
        lambda f: ig_from_lo[f],
        lambda f: ig_from_hi[f],
        out,
        ig,
    )
    size = half_0.shape[0]
    packed[:size] = half_0[...]
    packed[size:] = half_1[...]
    unpack(packed, acc, sg, tg)


def call(kernel, name, out_shape, count, limit, scratch=(), in_specs=None, flops=0):
    return pl.pallas_call(
        kernel,
        out_shape=out_shape,
        in_specs=in_specs or [VMEM] * count,
        out_specs=[VMEM] * len(out_shape),
        scratch_shapes=list(scratch),
        compiler_params=pltpu.CompilerParams(vmem_limit_bytes=int(limit * 1024 * 1024)),
        cost_estimate=pl.CostEstimate(flops=flops, bytes_accessed=1 << 20, transcendentals=0) if flops else None,
        name=name,
    )


def shards(frames_in, spatial_weight, temporal_weight, upstream):
    frames, rows, channels, width = frames_in.shape
    mid = temporal_weight.shape[1]
    axial_count = lax.axis_size("axial")
    tm_count = lax.axis_size("tm")
    core_count = lax.axis_size("chan")
    rank_count = tm_count * axial_count
    axial = lax.axis_index("axial")
    own_c = channels // core_count
    group = 2 if frames % 2 == 0 else 1
    dims = (frames, rows, channels, width, mid, own_c, rank_count, axial_count, group)
    size = half_rows(3 * channels, 4 * mid)
    sds = jax.ShapeDtypeStruct

    split = axial_count == 2 and frames % 2 == 0
    edge_count = frames // 2 if split else frames
    turned = jnp.swapaxes(temporal_weight, 1, 2)
    edge, frame = call(
        functools.partial(stage_kernel, split),
        "stage",
        [sds((edge_count, channels, width), BF16), sds((rows, channels, width), BF16)],
        4,
        60,
        [pltpu.SemaphoreType.DMA((2,))],
        [HBM] * 4,
    )(frames_in, upstream, spatial_weight, turned)
    frame = lax.ppermute(frame, ("tm", "chan"), facing(tm_count))
    tw_other = lax.ppermute(turned, "chan", ring(2, 1))
    if split:
        edge = lax.ppermute(edge, "axial", ring(2, 1))
    else:
        edge = lax.ppermute(edge, ("axial", "chan"), facing(axial_count))
    sw_other = lax.ppermute(spatial_weight, "chan", ring(2, 1))

    own_shape = (frames, rows, own_c, width)
    inner = (inner_rows(axial_count, rows)[1], frames - 2, padded(mid), width)
    cells = (rows, frames, padded(mid), width)
    xp_shape = (frames, rows + 2, channels, width)
    up_shape = (frames + 2, rows, channels, width)
    total = (3 * channels, 4 * mid)
    forms = [pltpu.VMEM((3 * mid, 3 * channels), F32), pltpu.VMEM((mid, 3 * channels), F32)]
    fast = axial_count == 2 and tm_count == 4
    hid, grad, acc, xp, up, w_taps, w_act = call(
        functools.partial(inner_kernel, dims),
        "inner_cells",
        [
            sds(inner, BF16),
            sds(inner, BF16),
            sds(total, F32),
            sds(xp_shape, BF16),
            sds(up_shape, BF16),
            sds((3 * mid, 3 * channels), BF16),
            sds((mid, 3 * channels), BF16),
        ],
        4,
        16,
        forms,
        flops=1 << 31,
    )(frames_in, upstream, spatial_weight, turned)
    edge, frame, acc = lax.optimization_barrier((edge, frame, acc))
    swapped = lax.ppermute(jnp.concatenate([edge, frame], 0), "chan", ring(2, 1))
    hid, grad, xp, up, half_0, half_1 = call(
        functools.partial(grads_kernel, dims),
        "weight_grads",
        [
            sds(cells, BF16),
            sds(cells, BF16),
            sds(xp_shape, BF16),
            sds(up_shape, BF16),
            sds((size, LANES), BF16 if fast else F32),
            sds((size, LANES), BF16 if fast else F32),
        ],
        10,
        16,
        [
            pltpu.VMEM((2 * edge_count, channels, width), BF16),
            pltpu.VMEM(total, F32),
            pltpu.VMEM((2 * size, LANES), F32),
        ],
    )(hid, grad, acc, xp, up, edge, frame, swapped, w_taps, w_act)

    if fast:
        got_0 = lax.ppermute(half_0, "tm", pairs(4, 1))
        got_1 = lax.ppermute(half_1, "axial", ring(2, 1))

    hid_other, grad_other = call(
        functools.partial(others_kernel, dims),
        "other_cells",
        [sds(cells, BF16), sds(cells, BF16)],
        4,
        16,
        forms,
        flops=1 << 31,
    )(xp, up, sw_other, tw_other)

    own_shape = (frames, rows, own_c, width)
    out_edge, ig_edge = sds((rows, own_c, width), BF16), sds((frames, own_c, width), BF16)
    out_own, out_a, out_b, ig_own, ig_a, ig_b = call(
        functools.partial(fields_kernel, dims, fast),
        "field_products",
        [sds(own_shape, F32), out_edge, out_edge, sds(own_shape, F32), ig_edge, ig_edge],
        8,
        16,
        [
            pltpu.VMEM((3 * own_c, 2 * padded(mid)), BF16),
            pltpu.VMEM((9 * own_c, 2 * padded(mid)), BF16),
            pltpu.VMEM((frames, rows + 2, own_c, width), F32),
            pltpu.VMEM((2, rows, own_c, width), BF16),
        ],
        flops=1 << 31,
    )(hid, grad, hid_other, grad_other, spatial_weight, turned, sw_other, tw_other)

    outs = [
        sds(own_shape, BF16),
        sds(own_shape, BF16),
        sds((3, 3, channels, mid), F32),
        sds((3, channels, mid), F32),
    ]
    scratch = [
        pltpu.VMEM((2 * size, LANES), F32),
        pltpu.VMEM(total, F32),
        pltpu.VMEM((2, rows, own_c, width), BF16),
    ]
    if fast:
        got_0, out_a, out_b, ig_a = lax.optimization_barrier((got_0, out_a, out_b, ig_a))
        half_0 = lax.optimization_barrier(half_0 + got_0)
        apart = lax.ppermute(half_0, "tm", pairs(4, 2))
        half_1 = lax.optimization_barrier(half_1 + got_1)
        near = lax.ppermute(jnp.concatenate([half_1, out_a.reshape(-1, width)], 0), "tm", pairs(4, 1))
        half_1 = lax.optimization_barrier(half_1 + near[:size])
        far = lax.ppermute(jnp.concatenate([half_1, out_b.reshape(-1, width)], 0), "tm", pairs(4, 3))
        apart, half_1 = lax.optimization_barrier((apart, half_1))
        half_0 = lax.optimization_barrier(half_0 + apart)
        across = lax.ppermute(half_0, "axial", ring(2, 1))
        ig_edge = lax.ppermute(ig_a, "axial", ring(2, 1))
        results = call(last_kernel, "last", outs, 8, 8, scratch)(
            out_own, ig_own, half_0, half_1, across, near, far, ig_edge
        )
    else:
        half_0, half_1 = lax.psum((half_0, half_1), ("tm", "axial"))
        from_hi = lax.ppermute(out_a, "tm", ring(tm_count, -1))
        from_lo = lax.ppermute(out_b, "tm", ring(tm_count, 1))
        ig_from_hi = lax.ppermute(ig_a, "axial", ring(axial_count, -1))
        ig_from_lo = lax.ppermute(ig_b, "axial", ring(axial_count, 1))
        results = call(functools.partial(last_kernel_general, axial_count), "last", outs, 8, 8, scratch)(
            out_own, ig_own, half_0, half_1, from_lo, from_hi, ig_from_lo, ig_from_hi
        )
    output, input_grad, spatial_grad, temporal_grad = results
    return output, input_grad, spatial_grad, jnp.swapaxes(temporal_grad, 1, 2)


def solution(mesh):
    placed = (
        P(("parts", "tm"), "axial", None, None),
        P("parts", None, None, "chan"),
        P("parts", "chan", None),
        P(("parts", "tm"), "axial", None, None),
    )
    return jax.shard_map(
        shards,
        mesh=mesh,
        in_specs=placed,
        out_specs=(
            P(("parts", "tm"), "axial", "chan", None),
            P(("parts", "tm"), "axial", "chan", None),
            P("parts", None, None, "chan"),
            P("parts", "chan", None),
        ),
        check_vma=False,
    )
```

```python
import functools
import math

import jax
import jax.numpy as jnp
from jax import lax
from jax.experimental import pallas as pl
from jax.experimental.pallas import tpu as pltpu
from jax.sharding import PartitionSpec as P

F32 = jnp.float32
BF16 = jnp.bfloat16
LANES = 128
HBM = pl.BlockSpec(memory_space=pltpu.HBM)
VMEM = pl.BlockSpec(memory_space=pltpu.VMEM)


def ring(count, step):
    return [(i, (i + step) % count) for i in range(count)]


def pairs(count, stride):
    return [(i, i ^ stride) for i in range(count)]


def facing(count):
    order = []
    for i in range(count):
        order += [(2 * i, 2 * ((i - 1) % count) + 1), (2 * i + 1, 2 * ((i + 1) % count))]
    return order


def dot(a, b):
    return jnp.dot(a, b, preferred_element_type=F32)


def dot_nt(a, b):
    return lax.dot_general(a, b, (((1,), (1,)), ((), ())), preferred_element_type=F32)


def moved(value, step):
    width = value.shape[1]
    column = lax.broadcasted_iota(jnp.int32, value.shape, 1)
    edge = 0 if step > 0 else width - 1
    return jnp.where(column == edge, 0.0, pltpu.roll(value, step % width, 1))


def pieces(depth, total):
    blocks, row = [], 0
    for first in range(0, total - total % LANES, LANES):
        blocks.append((row, 0, 0, first, depth, LANES))
        row += depth
    rest = total % LANES
    if rest:
        fold = LANES // rest
        if LANES % rest or depth % (8 * fold):
            fold = 1
        part = depth // fold
        for g in range(fold):
            blocks.append((row, g * rest, g * part, total - rest, part, rest))
        row += part
    return blocks, row


def padded(count):
    return -(-count // 16) * 16


def with_rows(value, count):
    if value.shape[0] == count:
        return value
    return jnp.concatenate([value, jnp.zeros((count - value.shape[0], value.shape[1]), value.dtype)], 0)


def half_rows(depth, total):
    return -(-pieces(depth, total)[1] // 32) * 16


def stage_kernel(split, x, u, sw, tw, edge, frame, sems):
    frames, rows = x.shape[:2]
    core = lax.axis_index("chan")
    if split:
        row = jnp.where(lax.axis_index("axial") == 0, rows - 1, 0)
        picked = pl.ds(core * (frames // 2), frames // 2)
    else:
        row = core * (rows - 1)
        picked = pl.ds(0, frames)
    copies = [
        pltpu.make_async_copy(u.at[core * (frames - 1)], frame, sems.at[0]),
        pltpu.make_async_copy(x.at[picked, row], edge, sems.at[1]),
    ]
    for copy in copies:
        copy.start()
    for copy in copies:
        copy.wait()


def prepare(sw, tw, wf, twf):
    channels, mid = tw.shape[1:]
    for j in range(3):
        wf[j * mid : (j + 1) * mid] = sw[:, j].reshape(3 * channels, mid).astype(F32).T
    twf[...] = jnp.concatenate([tw[k].astype(F32) for k in (2, 1, 0)], 0).T
    return wf[...].astype(BF16), twf[...].astype(BF16)


def activations(w_taps, w_act, field, cot, width):
    mid = w_act.shape[0]
    taps = dot(w_taps, field)
    act = dot(w_act, cot)
    hids, grads = [], []
    for first in range(0, field.shape[1], width):
        cols = slice(first, first + width)
        pre = taps[mid : 2 * mid, cols] + moved(taps[:mid, cols], 1) + moved(taps[2 * mid :, cols], -1)
        s = 0.5 * jnp.tanh(0.5 * pre) + 0.5
        hids.append(pre * s)
        grads.append(act[:, cols] * s * (1.0 + pre * (1.0 - s)))
    return hids, grads


def gathered(xp, up, h, picked):
    depth = 3 * xp.shape[2]
    width = xp.shape[3]
    field = jnp.concatenate([xp[f, pl.ds(h, 3)].reshape(depth, width) for f in picked], 1)
    cot = jnp.concatenate([jnp.concatenate([up[f + d, h] for d in range(3)], 0) for f in picked], 1)
    return field, cot


def inner_rows(axial_count, rows):
    if axial_count == 2:
        low = lax.axis_index("axial") == 0
        return jnp.where(low, 0, 1), rows - 1, [jnp.where(low, rows - 1, 0)]
    return 1, rows - 2, [0, rows - 1]


def cell_grads(xp, up, w_taps, w_act, groups, store):
    fields, cots, shifts, owns = [], [], [], []
    width = xp.shape[3]
    for h, picked in groups:
        field, cot = gathered(xp, up, h, picked)
        hids, grads = activations(w_taps, w_act, field, cot, width)
        shifts.append(
            jnp.concatenate(
                [
                    jnp.concatenate([moved(v, -1) for v in grads], 1),
                    jnp.concatenate(grads, 1),
                    jnp.concatenate([moved(v, 1) for v in grads], 1),
                ],
                0,
            ).astype(BF16)
        )
        hids = [with_rows(v, padded(v.shape[0])).astype(BF16) for v in hids]
        owns.append(jnp.concatenate(hids, 1))
        for f, hid, grad in zip(picked, hids, grads):
            store(h, f, hid, with_rows(grad, padded(grad.shape[0])).astype(BF16))
        fields.append(field)
        cots.append(cot)
    return (
        dot_nt(jnp.concatenate(fields, 1), jnp.concatenate(shifts, 1)),
        dot_nt(jnp.concatenate(cots, 1), jnp.concatenate(owns, 1))[:, : w_act.shape[0]],
    )


def inner_kernel(dims, *refs):
    frames, rows, channels, width, mid, own_c, rank_count, axial_count, group = dims
    x, u, sw, tw = refs[:4]
    hid_out, grad_out, acc_out, xp, up, taps_out, act_out, wf, twf = refs[4:]
    for f in range(frames):
        for at in (0, rows + 1):
            xp[f, at] = jnp.zeros((channels, width), BF16)
        for h in range(rows):
            xp[f, h + 1] = x[f, h]
            up[f + 1, h] = u[f, h]
    for at in (0, frames + 1):
        up[at] = jnp.zeros(up.shape[1:], BF16)
    w_taps, w_act = prepare(sw, tw, wf, twf)
    taps_out[...] = w_taps
    act_out[...] = w_act

    first, count, _ = inner_rows(axial_count, rows)

    def store(h, f, hid, grad):
        hid_out[h - first, f - 1] = hid
        grad_out[h - first, f - 1] = grad

    groups = [(first + i, (f, f + 1)) for i in range(count) for f in range(1, frames - 1, 2)]
    w_part, t_part = cell_grads(xp, up, w_taps, w_act, groups, store)
    acc_out[:, : 3 * mid] = w_part
    acc_out[:, 3 * mid :] = t_part


def grads_kernel(dims, *refs):
    frames, rows, channels, width, mid, own_c, rank_count, axial_count, group = dims
    hid_in, grad_in, acc_in, x, u, edge, frame, swapped, taps_in, act_in = refs[:10]
    hid_out, grad_out, xp, up, half_0, half_1, edges, acc, packed = refs[10:]
    axial = lax.axis_index("axial")
    core = lax.axis_index("chan")
    w_taps, w_act = taps_in[...], act_in[...]

    has_lo = (axial > 0).astype(BF16)
    has_hi = (axial < axial_count - 1).astype(BF16)
    part = edge.shape[0]
    edges[pl.ds(core * part, part)] = edge[...]
    edges[pl.ds((1 - core) * part, part)] = swapped[0:part]
    at_hi = 2 * part - frames
    for f in range(frames):
        xp[f, 0] = edges[f] * has_lo
        xp[f, rows + 1] = edges[at_hi + f] * has_hi
        for h in range(rows):
            xp[f, h + 1] = x[f, h + 1]
            up[f + 1, h] = u[f + 1, h]
    up[core * (frames + 1)] = frame[...]
    up[(1 - core) * (frames + 1)] = swapped[part:]

    first, count, others = inner_rows(axial_count, rows)

    def store(h, f, hid, grad):
        hid_out[h, f] = hid
        grad_out[h, f] = grad

    for i in range(count):
        for f in range(1, frames - 1):
            store(first + i, f, hid_in[i, f - 1], grad_in[i, f - 1])
    groups = [(first + i, (0, frames - 1)) for i in range(count)]
    groups += [(h, (f, f + 1)) for h in others for f in range(0, frames, 2)]
    w_part, t_part = cell_grads(xp, up, w_taps, w_act, groups, store)
    factor = 1.0 / math.sqrt(frames * rows * width * rank_count)
    acc[:, : 3 * mid] = (acc_in[:, : 3 * mid] + w_part) * factor
    acc[:, 3 * mid :] = (acc_in[:, 3 * mid :] + t_part) * factor

    blocks, used = pieces(*acc.shape)
    size = packed.shape[0] // 2
    packed[used:] = jnp.zeros((2 * size - used, LANES), F32)
    for at, lane, source, column, depth, total in blocks:
        packed[at : at + depth, lane : lane + total] = acc[source : source + depth, column : column + total]
    half_0[...] = packed[:size].astype(half_0.dtype)
    half_1[...] = packed[size:].astype(half_1.dtype)


def others_kernel(dims, *refs):
    frames, rows, channels, width, mid, own_c, rank_count, axial_count, group = dims
    xp, up, sw, tw, hid_out, grad_out, wf, twf = refs
    w_taps, w_act = prepare(sw, tw, wf, twf)
    for h in range(rows):
        for first in range(0, frames, group):
            picked = range(first, first + group)
            field, cot = gathered(xp, up, h, picked)
            for f, hid, grad in zip(picked, *activations(w_taps, w_act, field, cot, width)):
                hid_out[h, f] = with_rows(hid, padded(mid)).astype(BF16)
                grad_out[h, f] = with_rows(grad, padded(mid)).astype(BF16)


def fields_kernel(dims, fast, *refs):
    frames, rows, channels, width, mid, own_c, rank_count, axial_count, group = dims
    hid_in, grad_in, hid_other, grad_other, sw, tw, sw_other, tw_other = refs[:8]
    out, out_a, out_b, ig, ig_a, ig_b, twt, wg, ig_acc, out_edges = refs[8:]
    own = pl.ds(pl.multiple_of(lax.axis_index("chan") * own_c, own_c), own_c)
    blank = jnp.zeros((own_c, padded(mid) - mid), F32)

    def both(a, b):
        return jnp.concatenate([a.astype(F32), blank, b.astype(F32), blank], 1).astype(BF16)

    for k in range(3):
        twt[k * own_c : (k + 1) * own_c] = both(tw[k, own], tw_other[k, own])
    for i in range(3):
        for j in range(3):
            at = (i * 3 + j) * own_c
            wg[at : at + own_c] = both(sw[i, j, own], sw_other[i, j, own])
    w_out, w_in = twt[...], wg[...]

    for h in range(rows):
        out_terms = {}
        for first in range(0, frames, group):
            picked = range(first, first + group)
            hid = jnp.concatenate([jnp.concatenate([hid_in[h, f], hid_other[h, f]], 0) for f in picked], 1)
            grad = jnp.concatenate([jnp.concatenate([grad_in[h, f], grad_other[h, f]], 0) for f in picked], 1)
            y_out = dot(w_out, hid)
            y_in = dot(w_in, grad)
            for g, f in enumerate(picked):
                cols = slice(g * width, (g + 1) * width)
                for k in range(3):
                    out_terms.setdefault(f - k + 1, []).append(y_out[k * own_c : (k + 1) * own_c, cols])
                for i in range(3):
                    at = i * 3 * own_c
                    total = (
                        y_in[at + own_c : at + 2 * own_c, cols]
                        + moved(y_in[at : at + own_c, cols], -1)
                        + moved(y_in[at + 2 * own_c : at + 3 * own_c, cols], 1)
                    )
                    if h == 0 or i == 2:
                        ig_acc[f, h + i] = total
                    else:
                        ig_acc[f, h + i] += total
        for f, terms in out_terms.items():
            total = functools.reduce(lambda a, b: a + b, terms)
            if f < 0:
                out_edges[0, h] = total.astype(BF16)
            elif f >= frames:
                out_edges[1, h] = total.astype(BF16)
            else:
                out[f, h] = total

    odd = lax.rem(lax.axis_index("tm"), 2) if fast else 1
    high = jnp.where(lax.axis_index("axial") == 0, rows + 1, 0) if fast else 0
    out_a[...] = out_edges[1 - odd]
    out_b[...] = out_edges[odd]
    for f in range(frames):
        ig_a[f] = ig_acc[f, high].astype(BF16)
        ig_b[f] = ig_acc[f, rows + 1].astype(BF16)
        for h in range(rows):
            ig[f, h] = ig_acc[f, h + 1]


def unpack(packed, acc, sg, tg):
    channels, mid = tg.shape[1:]
    for at, lane, source, column, depth, total in pieces(*acc.shape)[0]:
        acc[source : source + depth, column : column + total] = packed[at : at + depth, lane : lane + total]
    for i in range(3):
        rows = slice(i * channels, (i + 1) * channels)
        for j in range(3):
            sg[i, j] = acc[rows, j * mid : (j + 1) * mid]
        tg[2 - i] = acc[rows, 3 * mid :]


def add_edges(axial_count, own, from_lo, from_hi, ig_own, ig_from_lo, ig_from_hi, out, ig):
    frames, rows = own.shape[:2]
    axial = lax.axis_index("axial")
    has_lo = (axial > 0).astype(F32)
    has_hi = (axial < axial_count - 1).astype(F32)
    for f in range(frames):
        for h in range(rows):
            total = own[f, h]
            if f == 0:
                total = total + from_lo(h).astype(F32)
            if f == frames - 1:
                total = total + from_hi(h).astype(F32)
            out[f, h] = total.astype(BF16)
            total = ig_own[f, h]
            if h == 0:
                total = total + ig_from_lo(f).astype(F32) * has_lo
            if h == rows - 1:
                total = total + ig_from_hi(f).astype(F32) * has_hi
            ig[f, h] = total.astype(BF16)


def last_kernel(own, ig_own, half_0, half_1, across, near, far, ig_edge, out, ig, sg, tg, packed, acc, edges):
    frames, rows, own_c, width = own.shape
    size = half_0.shape[0]
    odd = lax.rem(lax.axis_index("tm"), 2)
    edges[1 - odd] = near[size:].reshape(rows, own_c, width)
    edges[odd] = far[size:].reshape(rows, own_c, width)
    add_edges(
        2,
        own,
        lambda h: edges[0, h],
        lambda h: edges[1, h],
        ig_own,
        lambda f: ig_edge[f],
        lambda f: ig_edge[f],
        out,
        ig,
    )
    packed[:size] = half_0[...].astype(F32) + across[...].astype(F32)
    packed[size:] = half_1[...].astype(F32) + far[:size].astype(F32)
    unpack(packed, acc, sg, tg)


def last_kernel_general(axial_count, *refs):
    own, ig_own, half_0, half_1, from_lo, from_hi, ig_from_lo, ig_from_hi, out, ig, sg, tg, packed, acc, edges = refs
    add_edges(
        axial_count,
        own,
        lambda h: from_lo[h],
        lambda h: from_hi[h],
        ig_own,
        lambda f: ig_from_lo[f],
        lambda f: ig_from_hi[f],
        out,
        ig,
    )
    size = half_0.shape[0]
    packed[:size] = half_0[...]
    packed[size:] = half_1[...]
    unpack(packed, acc, sg, tg)


def call(kernel, name, out_shape, count, limit, scratch=(), in_specs=None, flops=0):
    return pl.pallas_call(
        kernel,
        out_shape=out_shape,
        in_specs=in_specs or [VMEM] * count,
        out_specs=[VMEM] * len(out_shape),
        scratch_shapes=list(scratch),
        compiler_params=pltpu.CompilerParams(vmem_limit_bytes=int(limit * 1024 * 1024)),
        cost_estimate=pl.CostEstimate(flops=flops, bytes_accessed=1 << 20, transcendentals=0) if flops else None,
        name=name,
    )


def shards(frames_in, spatial_weight, temporal_weight, upstream):
    frames, rows, channels, width = frames_in.shape
    mid = temporal_weight.shape[1]
    axial_count = lax.axis_size("axial")
    tm_count = lax.axis_size("tm")
    core_count = lax.axis_size("chan")
    rank_count = tm_count * axial_count
    axial = lax.axis_index("axial")
    own_c = channels // core_count
    group = 2 if frames % 2 == 0 else 1
    dims = (frames, rows, channels, width, mid, own_c, rank_count, axial_count, group)
    size = half_rows(3 * channels, 4 * mid)
    sds = jax.ShapeDtypeStruct

    split = axial_count == 2 and frames % 2 == 0
    edge_count = frames // 2 if split else frames
    turned = jnp.swapaxes(temporal_weight, 1, 2)
    edge, frame = call(
        functools.partial(stage_kernel, split),
        "stage",
        [sds((edge_count, channels, width), BF16), sds((rows, channels, width), BF16)],
        4,
        60,
        [pltpu.SemaphoreType.DMA((2,))],
        [HBM] * 4,
    )(frames_in, upstream, spatial_weight, turned)
    frame = lax.ppermute(frame, ("tm", "chan"), facing(tm_count))
    tw_other = lax.ppermute(turned, "chan", ring(2, 1))
    if split:
        edge = lax.ppermute(edge, "axial", ring(2, 1))
    else:
        edge = lax.ppermute(edge, ("axial", "chan"), facing(axial_count))
    sw_other = lax.ppermute(spatial_weight, "chan", ring(2, 1))

    own_shape = (frames, rows, own_c, width)
    inner = (inner_rows(axial_count, rows)[1], frames - 2, padded(mid), width)
    cells = (rows, frames, padded(mid), width)
    xp_shape = (frames, rows + 2, channels, width)
    up_shape = (frames + 2, rows, channels, width)
    total = (3 * channels, 4 * mid)
    forms = [pltpu.VMEM((3 * mid, 3 * channels), F32), pltpu.VMEM((mid, 3 * channels), F32)]
    fast = axial_count == 2 and tm_count == 4
    hid, grad, acc, xp, up, w_taps, w_act = call(
        functools.partial(inner_kernel, dims),
        "inner_cells",
        [
            sds(inner, BF16),
            sds(inner, BF16),
            sds(total, F32),
            sds(xp_shape, BF16),
            sds(up_shape, BF16),
            sds((3 * mid, 3 * channels), BF16),
            sds((mid, 3 * channels), BF16),
        ],
        4,
        16,
        forms,
        flops=1 << 31,
    )(frames_in, upstream, spatial_weight, turned)
    edge, frame, acc = lax.optimization_barrier((edge, frame, acc))
    swapped = lax.ppermute(jnp.concatenate([edge, frame], 0), "chan", ring(2, 1))
    hid, grad, xp, up, half_0, half_1 = call(
        functools.partial(grads_kernel, dims),
        "weight_grads",
        [
            sds(cells, BF16),
            sds(cells, BF16),
            sds(xp_shape, BF16),
            sds(up_shape, BF16),
            sds((size, LANES), BF16 if fast else F32),
            sds((size, LANES), BF16 if fast else F32),
        ],
        10,
        16,
        [
            pltpu.VMEM((2 * edge_count, channels, width), BF16),
            pltpu.VMEM(total, F32),
            pltpu.VMEM((2 * size, LANES), F32),
        ],
    )(hid, grad, acc, xp, up, edge, frame, swapped, w_taps, w_act)

    if fast:
        got_0 = lax.ppermute(half_0, "tm", pairs(4, 1))
        got_1 = lax.ppermute(half_1, "axial", ring(2, 1))

    hid_other, grad_other = call(
        functools.partial(others_kernel, dims),
        "other_cells",
        [sds(cells, BF16), sds(cells, BF16)],
        4,
        16,
        forms,
        flops=1 << 31,
    )(xp, up, sw_other, tw_other)

    own_shape = (frames, rows, own_c, width)
    out_edge, ig_edge = sds((rows, own_c, width), BF16), sds((frames, own_c, width), BF16)
    out_own, out_a, out_b, ig_own, ig_a, ig_b = call(
        functools.partial(fields_kernel, dims, fast),
        "field_products",
        [sds(own_shape, F32), out_edge, out_edge, sds(own_shape, F32), ig_edge, ig_edge],
        8,
        16,
        [
            pltpu.VMEM((3 * own_c, 2 * padded(mid)), BF16),
            pltpu.VMEM((9 * own_c, 2 * padded(mid)), BF16),
            pltpu.VMEM((frames, rows + 2, own_c, width), F32),
            pltpu.VMEM((2, rows, own_c, width), BF16),
        ],
        flops=1 << 31,
    )(hid, grad, hid_other, grad_other, spatial_weight, turned, sw_other, tw_other)

    outs = [
        sds(own_shape, BF16),
        sds(own_shape, BF16),
        sds((3, 3, channels, mid), F32),
        sds((3, channels, mid), F32),
    ]
    scratch = [
        pltpu.VMEM((2 * size, LANES), F32),
        pltpu.VMEM(total, F32),
        pltpu.VMEM((2, rows, own_c, width), BF16),
    ]
    if fast:
        got_0, out_a, out_b, ig_a = lax.optimization_barrier((got_0, out_a, out_b, ig_a))
        half_0 = lax.optimization_barrier(half_0 + got_0)
        apart = lax.ppermute(half_0, "tm", pairs(4, 2))
        half_1 = lax.optimization_barrier(half_1 + got_1)
        near = lax.ppermute(jnp.concatenate([half_1, out_a.reshape(-1, width)], 0), "tm", pairs(4, 1))
        half_1 = lax.optimization_barrier(half_1 + near[:size])
        far = lax.ppermute(jnp.concatenate([half_1, out_b.reshape(-1, width)], 0), "tm", pairs(4, 3))
        ig_edge = lax.ppermute(ig_a, "axial", ring(2, 1))
        apart, half_1, ig_edge = lax.optimization_barrier((apart, half_1, ig_edge))
        half_0 = lax.optimization_barrier(half_0 + apart)
        across = lax.ppermute(half_0, "axial", ring(2, 1))
        results = call(last_kernel, "last", outs, 8, 8, scratch)(
            out_own, ig_own, half_0, half_1, across, near, far, ig_edge
        )
    else:
        half_0, half_1 = lax.psum((half_0, half_1), ("tm", "axial"))
        from_hi = lax.ppermute(out_a, "tm", ring(tm_count, -1))
        from_lo = lax.ppermute(out_b, "tm", ring(tm_count, 1))
        ig_from_hi = lax.ppermute(ig_a, "axial", ring(axial_count, -1))
        ig_from_lo = lax.ppermute(ig_b, "axial", ring(axial_count, 1))
        results = call(functools.partial(last_kernel_general, axial_count), "last", outs, 8, 8, scratch)(
            out_own, ig_own, half_0, half_1, from_lo, from_hi, ig_from_lo, ig_from_hi
        )
    output, input_grad, spatial_grad, temporal_grad = results
    return output, input_grad, spatial_grad, jnp.swapaxes(temporal_grad, 1, 2)


def solution(mesh):
    placed = (
        P(("parts", "tm"), "axial", None, None),
        P("parts", None, None, "chan"),
        P("parts", "chan", None),
        P(("parts", "tm"), "axial", None, None),
    )
    return jax.shard_map(
        shards,
        mesh=mesh,
        in_specs=placed,
        out_specs=(
            P(("parts", "tm"), "axial", "chan", None),
            P(("parts", "tm"), "axial", "chan", None),
            P("parts", None, None, "chan"),
            P("parts", "chan", None),
        ),
        check_vma=False,
    )
```

```python
import functools
import math

import jax
import jax.numpy as jnp
from jax import lax
from jax.experimental import pallas as pl
from jax.experimental.pallas import tpu as pltpu
from jax.sharding import PartitionSpec as P

F32 = jnp.float32
BF16 = jnp.bfloat16
LANES = 128
HBM = pl.BlockSpec(memory_space=pltpu.HBM)
VMEM = pl.BlockSpec(memory_space=pltpu.VMEM)


def ring(count, step):
    return [(i, (i + step) % count) for i in range(count)]


def pairs(count, stride):
    return [(i, i ^ stride) for i in range(count)]


def facing(count):
    order = []
    for i in range(count):
        order += [(2 * i, 2 * ((i - 1) % count) + 1), (2 * i + 1, 2 * ((i + 1) % count))]
    return order


def dot(a, b):
    return jnp.dot(a, b, preferred_element_type=F32)


def dot_nt(a, b):
    return lax.dot_general(a, b, (((1,), (1,)), ((), ())), preferred_element_type=F32)


def moved(value, step):
    width = value.shape[1]
    column = lax.broadcasted_iota(jnp.int32, value.shape, 1)
    edge = 0 if step > 0 else width - 1
    return jnp.where(column == edge, 0.0, pltpu.roll(value, step % width, 1))


def pieces(depth, total):
    blocks, row = [], 0
    for first in range(0, total - total % LANES, LANES):
        blocks.append((row, 0, 0, first, depth, LANES))
        row += depth
    rest = total % LANES
    if rest:
        fold = LANES // rest
        if LANES % rest or depth % (8 * fold):
            fold = 1
        part = depth // fold
        for g in range(fold):
            blocks.append((row, g * rest, g * part, total - rest, part, rest))
        row += part
    return blocks, row


def padded(count):
    return -(-count // 16) * 16


def with_rows(value, count):
    if value.shape[0] == count:
        return value
    return jnp.concatenate([value, jnp.zeros((count - value.shape[0], value.shape[1]), value.dtype)], 0)


def half_rows(depth, total):
    return -(-pieces(depth, total)[1] // 32) * 16


def stage_kernel(split, x, u, sw, tw, edge, frame, sems):
    frames, rows = x.shape[:2]
    core = lax.axis_index("chan")
    if split:
        row = jnp.where(lax.axis_index("axial") == 0, rows - 1, 0)
        picked = pl.ds(core * (frames // 2), frames // 2)
    else:
        row = core * (rows - 1)
        picked = pl.ds(0, frames)
    copies = [
        pltpu.make_async_copy(u.at[core * (frames - 1)], frame, sems.at[0]),
        pltpu.make_async_copy(x.at[picked, row], edge, sems.at[1]),
    ]
    for copy in copies:
        copy.start()
    for copy in copies:
        copy.wait()


def prepare(sw, tw, wf, twf):
    channels, mid = tw.shape[1:]
    for j in range(3):
        wf[j * mid : (j + 1) * mid] = sw[:, j].reshape(3 * channels, mid).astype(F32).T
    twf[...] = jnp.concatenate([tw[k].astype(F32) for k in (2, 1, 0)], 0).T
    return wf[...].astype(BF16), twf[...].astype(BF16)


def activations(w_taps, w_act, field, cot, width):
    mid = w_act.shape[0]
    taps = dot(w_taps, field)
    act = dot(w_act, cot)
    hids, grads = [], []
    for first in range(0, field.shape[1], width):
        cols = slice(first, first + width)
        pre = taps[mid : 2 * mid, cols] + moved(taps[:mid, cols], 1) + moved(taps[2 * mid :, cols], -1)
        s = 0.5 * jnp.tanh(0.5 * pre) + 0.5
        hids.append(pre * s)
        grads.append(act[:, cols] * s * (1.0 + pre * (1.0 - s)))
    return hids, grads


def gathered(xp, up, h, picked):
    depth = 3 * xp.shape[2]
    width = xp.shape[3]
    field = jnp.concatenate([xp[f, pl.ds(h, 3)].reshape(depth, width) for f in picked], 1)
    cot = jnp.concatenate([jnp.concatenate([up[f + d, h] for d in range(3)], 0) for f in picked], 1)
    return field, cot


def inner_rows(axial_count, rows):
    if axial_count == 2:
        low = lax.axis_index("axial") == 0
        return jnp.where(low, 0, 1), rows - 1, [jnp.where(low, rows - 1, 0)]
    return 1, rows - 2, [0, rows - 1]


def cell_grads(xp, up, w_taps, w_act, groups, store):
    fields, cots, shifts, owns = [], [], [], []
    width = xp.shape[3]
    for h, picked in groups:
        field, cot = gathered(xp, up, h, picked)
        hids, grads = activations(w_taps, w_act, field, cot, width)
        shifts.append(
            jnp.concatenate(
                [
                    jnp.concatenate([moved(v, -1) for v in grads], 1),
                    jnp.concatenate(grads, 1),
                    jnp.concatenate([moved(v, 1) for v in grads], 1),
                ],
                0,
            ).astype(BF16)
        )
        hids = [with_rows(v, padded(v.shape[0])).astype(BF16) for v in hids]
        owns.append(jnp.concatenate(hids, 1))
        for f, hid, grad in zip(picked, hids, grads):
            store(h, f, hid, with_rows(grad, padded(grad.shape[0])).astype(BF16))
        fields.append(field)
        cots.append(cot)
    return (
        dot_nt(jnp.concatenate(fields, 1), jnp.concatenate(shifts, 1)),
        dot_nt(jnp.concatenate(cots, 1), jnp.concatenate(owns, 1))[:, : w_act.shape[0]],
    )


def inner_kernel(dims, *refs):
    frames, rows, channels, width, mid, own_c, rank_count, axial_count, group = dims
    x, u, sw, tw = refs[:4]
    hid_out, grad_out, acc_out, xp, up, taps_out, act_out, wf, twf = refs[4:]
    for f in range(frames):
        for at in (0, rows + 1):
            xp[f, at] = jnp.zeros((channels, width), BF16)
        for h in range(rows):
            xp[f, h + 1] = x[f, h]
            up[f + 1, h] = u[f, h]
    for at in (0, frames + 1):
        up[at] = jnp.zeros(up.shape[1:], BF16)
    w_taps, w_act = prepare(sw, tw, wf, twf)
    taps_out[...] = w_taps
    act_out[...] = w_act

    first, count, _ = inner_rows(axial_count, rows)

    def store(h, f, hid, grad):
        hid_out[h - first, f - 1] = hid
        grad_out[h - first, f - 1] = grad

    groups = [(first + i, (f, f + 1)) for i in range(count) for f in range(1, frames - 1, 2)]
    w_part, t_part = cell_grads(xp, up, w_taps, w_act, groups, store)
    acc_out[:, : 3 * mid] = w_part
    acc_out[:, 3 * mid :] = t_part


def grads_kernel(dims, *refs):
    frames, rows, channels, width, mid, own_c, rank_count, axial_count, group = dims
    hid_in, grad_in, acc_in, x, u, edge, frame, swapped, taps_in, act_in = refs[:10]
    hid_out, grad_out, xp, up, half_0, half_1, edges, acc, packed = refs[10:]
    axial = lax.axis_index("axial")
    core = lax.axis_index("chan")
    w_taps, w_act = taps_in[...], act_in[...]

    has_lo = (axial > 0).astype(BF16)
    has_hi = (axial < axial_count - 1).astype(BF16)
    part = edge.shape[0]
    edges[pl.ds(core * part, part)] = edge[...]
    edges[pl.ds((1 - core) * part, part)] = swapped[0:part]
    at_hi = 2 * part - frames
    for f in range(frames):
        xp[f, 0] = edges[f] * has_lo
        xp[f, rows + 1] = edges[at_hi + f] * has_hi
        for h in range(rows):
            xp[f, h + 1] = x[f, h + 1]
            up[f + 1, h] = u[f + 1, h]
    up[core * (frames + 1)] = frame[...]
    up[(1 - core) * (frames + 1)] = swapped[part:]

    first, count, others = inner_rows(axial_count, rows)

    def store(h, f, hid, grad):
        hid_out[h, f] = hid
        grad_out[h, f] = grad

    for i in range(count):
        for f in range(1, frames - 1):
            store(first + i, f, hid_in[i, f - 1], grad_in[i, f - 1])
    groups = [(first + i, (0, frames - 1)) for i in range(count)]
    groups += [(h, (f, f + 1)) for h in others for f in range(0, frames, 2)]
    w_part, t_part = cell_grads(xp, up, w_taps, w_act, groups, store)
    factor = 1.0 / math.sqrt(frames * rows * width * rank_count)
    acc[:, : 3 * mid] = (acc_in[:, : 3 * mid] + w_part) * factor
    acc[:, 3 * mid :] = (acc_in[:, 3 * mid :] + t_part) * factor

    blocks, used = pieces(*acc.shape)
    size = packed.shape[0] // 2
    packed[used:] = jnp.zeros((2 * size - used, LANES), F32)
    for at, lane, source, column, depth, total in blocks:
        packed[at : at + depth, lane : lane + total] = acc[source : source + depth, column : column + total]
    half_0[...] = packed[:size].astype(half_0.dtype)
    half_1[...] = packed[size:].astype(half_1.dtype)


def others_kernel(dims, *refs):
    frames, rows, channels, width, mid, own_c, rank_count, axial_count, group = dims
    xp, up, sw, tw, hid_out, grad_out, wf, twf = refs
    w_taps, w_act = prepare(sw, tw, wf, twf)
    for h in range(rows):
        for first in range(0, frames, group):
            picked = range(first, first + group)
            field, cot = gathered(xp, up, h, picked)
            for f, hid, grad in zip(picked, *activations(w_taps, w_act, field, cot, width)):
                hid_out[h, f] = with_rows(hid, padded(mid)).astype(BF16)
                grad_out[h, f] = with_rows(grad, padded(mid)).astype(BF16)


def fields_kernel(dims, fast, *refs):
    frames, rows, channels, width, mid, own_c, rank_count, axial_count, group = dims
    hid_in, grad_in, hid_other, grad_other, sw, tw, sw_other, tw_other = refs[:8]
    out, out_a, out_b, ig, ig_a, ig_b, twt, wg, ig_acc, out_edges = refs[8:]
    own = pl.ds(pl.multiple_of(lax.axis_index("chan") * own_c, own_c), own_c)
    blank = jnp.zeros((own_c, padded(mid) - mid), F32)

    def both(a, b):
        return jnp.concatenate([a.astype(F32), blank, b.astype(F32), blank], 1).astype(BF16)

    for k in range(3):
        twt[k * own_c : (k + 1) * own_c] = both(tw[k, own], tw_other[k, own])
    for i in range(3):
        for j in range(3):
            at = (i * 3 + j) * own_c
            wg[at : at + own_c] = both(sw[i, j, own], sw_other[i, j, own])
    w_out, w_in = twt[...], wg[...]

    for h in range(rows):
        out_terms = {}
        for first in range(0, frames, group):
            picked = range(first, first + group)
            hid = jnp.concatenate([jnp.concatenate([hid_in[h, f], hid_other[h, f]], 0) for f in picked], 1)
            grad = jnp.concatenate([jnp.concatenate([grad_in[h, f], grad_other[h, f]], 0) for f in picked], 1)
            y_out = dot(w_out, hid)
            y_in = dot(w_in, grad)
            for g, f in enumerate(picked):
                cols = slice(g * width, (g + 1) * width)
                for k in range(3):
                    out_terms.setdefault(f - k + 1, []).append(y_out[k * own_c : (k + 1) * own_c, cols])
                for i in range(3):
                    at = i * 3 * own_c
                    total = (
                        y_in[at + own_c : at + 2 * own_c, cols]
                        + moved(y_in[at : at + own_c, cols], -1)
                        + moved(y_in[at + 2 * own_c : at + 3 * own_c, cols], 1)
                    )
                    if h == 0 or i == 2:
                        ig_acc[f, h + i] = total
                    else:
                        ig_acc[f, h + i] += total
        for f, terms in out_terms.items():
            total = functools.reduce(lambda a, b: a + b, terms)
            if f < 0:
                out_edges[0, h] = total.astype(BF16)
            elif f >= frames:
                out_edges[1, h] = total.astype(BF16)
            else:
                out[f, h] = total

    odd = lax.rem(lax.axis_index("tm"), 2) if fast else 1
    high = jnp.where(lax.axis_index("axial") == 0, rows + 1, 0) if fast else 0
    out_a[...] = out_edges[1 - odd]
    out_b[...] = out_edges[odd]
    for f in range(frames):
        ig_a[f] = ig_acc[f, high].astype(BF16)
        ig_b[f] = ig_acc[f, rows + 1].astype(BF16)
        for h in range(rows):
            ig[f, h] = ig_acc[f, h + 1]


def rest_kernel(dims, fast, *refs):
    hid, grad, xp, up, sw, tw, sw_other, tw_other = refs[:8]
    outs, (wf, twf, hid_other, grad_other), scratch = refs[8:14], refs[14:18], refs[18:]
    others_kernel(dims, xp, up, sw_other, tw_other, hid_other, grad_other, wf, twf)
    fields_kernel(dims, fast, hid, grad, hid_other, grad_other, sw, tw, sw_other, tw_other, *outs, *scratch)


def unpack(packed, acc, sg, tg):
    channels, mid = tg.shape[1:]
    for at, lane, source, column, depth, total in pieces(*acc.shape)[0]:
        acc[source : source + depth, column : column + total] = packed[at : at + depth, lane : lane + total]
    for i in range(3):
        rows = slice(i * channels, (i + 1) * channels)
        for j in range(3):
            sg[i, j] = acc[rows, j * mid : (j + 1) * mid]
        tg[2 - i] = acc[rows, 3 * mid :]


def add_edges(axial_count, own, from_lo, from_hi, ig_own, ig_from_lo, ig_from_hi, out, ig):
    frames, rows = own.shape[:2]
    axial = lax.axis_index("axial")
    has_lo = (axial > 0).astype(F32)
    has_hi = (axial < axial_count - 1).astype(F32)
    for f in range(frames):
        for h in range(rows):
            total = own[f, h]
            if f == 0:
                total = total + from_lo(h).astype(F32)
            if f == frames - 1:
                total = total + from_hi(h).astype(F32)
            out[f, h] = total.astype(BF16)
            total = ig_own[f, h]
            if h == 0:
                total = total + ig_from_lo(f).astype(F32) * has_lo
            if h == rows - 1:
                total = total + ig_from_hi(f).astype(F32) * has_hi
            ig[f, h] = total.astype(BF16)


def last_kernel(own, ig_own, half_0, half_1, across, near, far, ig_edge, out, ig, sg, tg, packed, acc, edges):
    frames, rows, own_c, width = own.shape
    size = half_0.shape[0]
    odd = lax.rem(lax.axis_index("tm"), 2)
    edges[1 - odd] = near[size:].reshape(rows, own_c, width)
    edges[odd] = far[size:].reshape(rows, own_c, width)
    add_edges(
        2,
        own,
        lambda h: edges[0, h],
        lambda h: edges[1, h],
        ig_own,
        lambda f: ig_edge[f],
        lambda f: ig_edge[f],
        out,
        ig,
    )
    packed[:size] = half_0[...].astype(F32) + across[...].astype(F32)
    packed[size:] = half_1[...].astype(F32) + far[:size].astype(F32)
    unpack(packed, acc, sg, tg)


def last_kernel_general(axial_count, *refs):
    own, ig_own, half_0, half_1, from_lo, from_hi, ig_from_lo, ig_from_hi, out, ig, sg, tg, packed, acc, edges = refs
    add_edges(
        axial_count,
        own,
        lambda h: from_lo[h],
        lambda h: from_hi[h],
        ig_own,
        lambda f: ig_from_lo[f],
        lambda f: ig_from_hi[f],
        out,
        ig,
    )
    size = half_0.shape[0]
    packed[:size] = half_0[...]
    packed[size:] = half_1[...]
    unpack(packed, acc, sg, tg)


def call(kernel, name, out_shape, count, limit, scratch=(), in_specs=None, flops=0):
    return pl.pallas_call(
        kernel,
        out_shape=out_shape,
        in_specs=in_specs or [VMEM] * count,
        out_specs=[VMEM] * len(out_shape),
        scratch_shapes=list(scratch),
        compiler_params=pltpu.CompilerParams(vmem_limit_bytes=int(limit * 1024 * 1024)),
        cost_estimate=pl.CostEstimate(flops=flops, bytes_accessed=1 << 20, transcendentals=0) if flops else None,
        name=name,
    )


def shards(frames_in, spatial_weight, temporal_weight, upstream):
    frames, rows, channels, width = frames_in.shape
    mid = temporal_weight.shape[1]
    axial_count = lax.axis_size("axial")
    tm_count = lax.axis_size("tm")
    core_count = lax.axis_size("chan")
    rank_count = tm_count * axial_count
    axial = lax.axis_index("axial")
    own_c = channels // core_count
    group = 2 if frames % 2 == 0 else 1
    dims = (frames, rows, channels, width, mid, own_c, rank_count, axial_count, group)
    size = half_rows(3 * channels, 4 * mid)
    sds = jax.ShapeDtypeStruct

    split = axial_count == 2 and frames % 2 == 0
    edge_count = frames // 2 if split else frames
    turned = jnp.swapaxes(temporal_weight, 1, 2)
    edge, frame = call(
        functools.partial(stage_kernel, split),
        "stage",
        [sds((edge_count, channels, width), BF16), sds((rows, channels, width), BF16)],
        4,
        60,
        [pltpu.SemaphoreType.DMA((2,))],
        [HBM] * 4,
    )(frames_in, upstream, spatial_weight, turned)
    frame = lax.ppermute(frame, ("tm", "chan"), facing(tm_count))
    tw_other = lax.ppermute(turned, "chan", ring(2, 1))
    if split:
        edge = lax.ppermute(edge, "axial", ring(2, 1))
    else:
        edge = lax.ppermute(edge, ("axial", "chan"), facing(axial_count))
    sw_other = lax.ppermute(spatial_weight, "chan", ring(2, 1))

    own_shape = (frames, rows, own_c, width)
    inner = (inner_rows(axial_count, rows)[1], frames - 2, padded(mid), width)
    cells = (rows, frames, padded(mid), width)
    xp_shape = (frames, rows + 2, channels, width)
    up_shape = (frames + 2, rows, channels, width)
    total = (3 * channels, 4 * mid)
    forms = [pltpu.VMEM((3 * mid, 3 * channels), F32), pltpu.VMEM((mid, 3 * channels), F32)]
    fast = axial_count == 2 and tm_count == 4
    hid, grad, acc, xp, up, w_taps, w_act = call(
        functools.partial(inner_kernel, dims),
        "inner_cells",
        [
            sds(inner, BF16),
            sds(inner, BF16),
            sds(total, F32),
            sds(xp_shape, BF16),
            sds(up_shape, BF16),
            sds((3 * mid, 3 * channels), BF16),
            sds((mid, 3 * channels), BF16),
        ],
        4,
        16,
        forms,
        flops=1 << 31,
    )(frames_in, upstream, spatial_weight, turned)
    edge, frame, acc = lax.optimization_barrier((edge, frame, acc))
    swapped = lax.ppermute(jnp.concatenate([edge, frame], 0), "chan", ring(2, 1))
    hid, grad, xp, up, half_0, half_1 = call(
        functools.partial(grads_kernel, dims),
        "weight_grads",
        [
            sds(cells, BF16),
            sds(cells, BF16),
            sds(xp_shape, BF16),
            sds(up_shape, BF16),
            sds((size, LANES), BF16 if fast else F32),
            sds((size, LANES), BF16 if fast else F32),
        ],
        10,
        16,
        [
            pltpu.VMEM((2 * edge_count, channels, width), BF16),
            pltpu.VMEM(total, F32),
            pltpu.VMEM((2 * size, LANES), F32),
        ],
    )(hid, grad, acc, xp, up, edge, frame, swapped, w_taps, w_act)

    if fast:
        got_0 = lax.ppermute(half_0, "tm", pairs(4, 1))
        got_1 = lax.ppermute(half_1, "axial", ring(2, 1))

    own_shape = (frames, rows, own_c, width)
    out_edge, ig_edge = sds((rows, own_c, width), BF16), sds((frames, own_c, width), BF16)
    out_own, out_a, out_b, ig_own, ig_a, ig_b = call(
        functools.partial(rest_kernel, dims, fast),
        "field_products",
        [sds(own_shape, F32), out_edge, out_edge, sds(own_shape, F32), ig_edge, ig_edge],
        8,
        16,
        forms
        + [
            pltpu.VMEM(cells, BF16),
            pltpu.VMEM(cells, BF16),
            pltpu.VMEM((3 * own_c, 2 * padded(mid)), BF16),
            pltpu.VMEM((9 * own_c, 2 * padded(mid)), BF16),
            pltpu.VMEM((frames, rows + 2, own_c, width), F32),
            pltpu.VMEM((2, rows, own_c, width), BF16),
        ],
        flops=1 << 31,
    )(hid, grad, xp, up, spatial_weight, turned, sw_other, tw_other)

    outs = [
        sds(own_shape, BF16),
        sds(own_shape, BF16),
        sds((3, 3, channels, mid), F32),
        sds((3, channels, mid), F32),
    ]
    scratch = [
        pltpu.VMEM((2 * size, LANES), F32),
        pltpu.VMEM(total, F32),
        pltpu.VMEM((2, rows, own_c, width), BF16),
    ]
    if fast:
        got_0, out_a, out_b, ig_a = lax.optimization_barrier((got_0, out_a, out_b, ig_a))
        half_0 = lax.optimization_barrier(half_0 + got_0)
        apart = lax.ppermute(half_0, "tm", pairs(4, 2))
        half_1 = lax.optimization_barrier(half_1 + got_1)
        near = lax.ppermute(jnp.concatenate([half_1, out_a.reshape(-1, width)], 0), "tm", pairs(4, 1))
        half_1 = lax.optimization_barrier(half_1 + near[:size])
        far = lax.ppermute(jnp.concatenate([half_1, out_b.reshape(-1, width)], 0), "tm", pairs(4, 3))
        ig_edge = lax.ppermute(ig_a, "axial", ring(2, 1))
        apart, half_1, ig_edge = lax.optimization_barrier((apart, half_1, ig_edge))
        half_0 = lax.optimization_barrier(half_0 + apart)
        across = lax.ppermute(half_0, "axial", ring(2, 1))
        results = call(last_kernel, "last", outs, 8, 8, scratch)(
            out_own, ig_own, half_0, half_1, across, near, far, ig_edge
        )
    else:
        half_0, half_1 = lax.psum((half_0, half_1), ("tm", "axial"))
        from_hi = lax.ppermute(out_a, "tm", ring(tm_count, -1))
        from_lo = lax.ppermute(out_b, "tm", ring(tm_count, 1))
        ig_from_hi = lax.ppermute(ig_a, "axial", ring(axial_count, -1))
        ig_from_lo = lax.ppermute(ig_b, "axial", ring(axial_count, 1))
        results = call(functools.partial(last_kernel_general, axial_count), "last", outs, 8, 8, scratch)(
            out_own, ig_own, half_0, half_1, from_lo, from_hi, ig_from_lo, ig_from_hi
        )
    output, input_grad, spatial_grad, temporal_grad = results
    return output, input_grad, spatial_grad, jnp.swapaxes(temporal_grad, 1, 2)


def solution(mesh):
    placed = (
        P(("parts", "tm"), "axial", None, None),
        P("parts", None, None, "chan"),
        P("parts", "chan", None),
        P(("parts", "tm"), "axial", None, None),
    )
    return jax.shard_map(
        shards,
        mesh=mesh,
        in_specs=placed,
        out_specs=(
            P(("parts", "tm"), "axial", "chan", None),
            P(("parts", "tm"), "axial", "chan", None),
            P("parts", None, None, "chan"),
            P("parts", "chan", None),
        ),
        check_vma=False,
    )
```

```python
import functools
import math

import jax
import jax.numpy as jnp
from jax import lax
from jax.experimental import pallas as pl
from jax.experimental.pallas import tpu as pltpu
from jax.sharding import PartitionSpec as P

F32 = jnp.float32
BF16 = jnp.bfloat16
LANES = 128
HBM = pl.BlockSpec(memory_space=pltpu.HBM)
VMEM = pl.BlockSpec(memory_space=pltpu.VMEM)


def ring(count, step):
    return [(i, (i + step) % count) for i in range(count)]


def pairs(count, stride):
    return [(i, i ^ stride) for i in range(count)]


def facing(count):
    order = []
    for i in range(count):
        order += [(2 * i, 2 * ((i - 1) % count) + 1), (2 * i + 1, 2 * ((i + 1) % count))]
    return order


def dot(a, b):
    return jnp.dot(a, b, preferred_element_type=F32)


def dot_nt(a, b):
    return lax.dot_general(a, b, (((1,), (1,)), ((), ())), preferred_element_type=F32)


def moved(value, step):
    width = value.shape[1]
    column = lax.broadcasted_iota(jnp.int32, value.shape, 1)
    edge = 0 if step > 0 else width - 1
    return jnp.where(column == edge, 0.0, pltpu.roll(value, step % width, 1))


def pieces(depth, total):
    blocks, row = [], 0
    for first in range(0, total - total % LANES, LANES):
        blocks.append((row, 0, 0, first, depth, LANES))
        row += depth
    rest = total % LANES
    if rest:
        fold = LANES // rest
        if LANES % rest or depth % (8 * fold):
            fold = 1
        part = depth // fold
        for g in range(fold):
            blocks.append((row, g * rest, g * part, total - rest, part, rest))
        row += part
    return blocks, row


def padded(count):
    return -(-count // 16) * 16


def with_rows(value, count):
    if value.shape[0] == count:
        return value
    return jnp.concatenate([value, jnp.zeros((count - value.shape[0], value.shape[1]), value.dtype)], 0)


def half_rows(depth, total):
    return -(-pieces(depth, total)[1] // 32) * 16


def stage_kernel(split, x, u, sw, tw, edge, frame, sems):
    frames, rows = x.shape[:2]
    core = lax.axis_index("chan")
    if split:
        row = jnp.where(lax.axis_index("axial") == 0, rows - 1, 0)
        picked = pl.ds(core * (frames // 2), frames // 2)
    else:
        row = core * (rows - 1)
        picked = pl.ds(0, frames)
    copies = [
        pltpu.make_async_copy(u.at[core * (frames - 1)], frame, sems.at[0]),
        pltpu.make_async_copy(x.at[picked, row], edge, sems.at[1]),
    ]
    for copy in copies:
        copy.start()
    for copy in copies:
        copy.wait()


def prepare(sw, tw, wf, twf):
    channels, mid = tw.shape[1:]
    for j in range(3):
        wf[j * mid : (j + 1) * mid] = sw[:, j].reshape(3 * channels, mid).astype(F32).T
    twf[...] = jnp.concatenate([tw[k].astype(F32) for k in (2, 1, 0)], 0).T
    return wf[...].astype(BF16), twf[...].astype(BF16)


def activations(w_taps, w_act, field, cot, width):
    mid = w_act.shape[0]
    taps = dot(w_taps, field)
    act = dot(w_act, cot)
    hids, grads = [], []
    for first in range(0, field.shape[1], width):
        cols = slice(first, first + width)
        pre = taps[mid : 2 * mid, cols] + moved(taps[:mid, cols], 1) + moved(taps[2 * mid :, cols], -1)
        s = 0.5 * jnp.tanh(0.5 * pre) + 0.5
        hids.append(pre * s)
        grads.append(act[:, cols] * s * (1.0 + pre * (1.0 - s)))
    return hids, grads


def gathered(xp, up, h, picked):
    depth = 3 * xp.shape[2]
    width = xp.shape[3]
    field = jnp.concatenate([xp[f, pl.ds(h, 3)].reshape(depth, width) for f in picked], 1)
    cot = jnp.concatenate([jnp.concatenate([up[f + d, h] for d in range(3)], 0) for f in picked], 1)
    return field, cot


def inner_rows(axial_count, rows):
    if axial_count == 2:
        low = lax.axis_index("axial") == 0
        return jnp.where(low, 0, 1), rows - 1, [jnp.where(low, rows - 1, 0)]
    return 1, rows - 2, [0, rows - 1]


def cell_grads(xp, up, w_taps, w_act, groups, store):
    fields, cots, shifts, owns = [], [], [], []
    width = xp.shape[3]
    for h, picked in groups:
        field, cot = gathered(xp, up, h, picked)
        hids, grads = activations(w_taps, w_act, field, cot, width)
        shifts.append(
            jnp.concatenate(
                [
                    jnp.concatenate([moved(v, -1) for v in grads], 1),
                    jnp.concatenate(grads, 1),
                    jnp.concatenate([moved(v, 1) for v in grads], 1),
                ],
                0,
            ).astype(BF16)
        )
        hids = [with_rows(v, padded(v.shape[0])).astype(BF16) for v in hids]
        owns.append(jnp.concatenate(hids, 1))
        for f, hid, grad in zip(picked, hids, grads):
            store(h, f, hid, with_rows(grad, padded(grad.shape[0])).astype(BF16))
        fields.append(field)
        cots.append(cot)
    return (
        dot_nt(jnp.concatenate(fields, 1), jnp.concatenate(shifts, 1)),
        dot_nt(jnp.concatenate(cots, 1), jnp.concatenate(owns, 1))[:, : w_act.shape[0]],
    )


def inner_kernel(dims, *refs):
    frames, rows, channels, width, mid, own_c, rank_count, axial_count, group = dims
    x, u, sw, tw = refs[:4]
    hid_out, grad_out, acc_out, xp, up, taps_out, act_out, wf, twf = refs[4:]
    for f in range(frames):
        for at in (0, rows + 1):
            xp[f, at] = jnp.zeros((channels, width), BF16)
        for h in range(rows):
            xp[f, h + 1] = x[f, h]
            up[f + 1, h] = u[f, h]
    for at in (0, frames + 1):
        up[at] = jnp.zeros(up.shape[1:], BF16)
    w_taps, w_act = prepare(sw, tw, wf, twf)
    taps_out[...] = w_taps
    act_out[...] = w_act

    first, count, _ = inner_rows(axial_count, rows)

    def store(h, f, hid, grad):
        hid_out[h - first, f - 1] = hid
        grad_out[h - first, f - 1] = grad

    groups = [(first + i, (f, f + 1)) for i in range(count) for f in range(1, frames - 1, 2)]
    w_part, t_part = cell_grads(xp, up, w_taps, w_act, groups, store)
    acc_out[:, : 3 * mid] = w_part
    acc_out[:, 3 * mid :] = t_part


def grads_kernel(dims, *refs):
    frames, rows, channels, width, mid, own_c, rank_count, axial_count, group = dims
    hid_in, grad_in, acc_in, x, u, edge, frame, swapped, taps_in, act_in = refs[:10]
    hid_out, grad_out, xp, up, half_0, half_1, edges, acc, packed = refs[10:]
    axial = lax.axis_index("axial")
    core = lax.axis_index("chan")
    w_taps, w_act = taps_in[...], act_in[...]

    has_lo = (axial > 0).astype(BF16)
    has_hi = (axial < axial_count - 1).astype(BF16)
    part = edge.shape[0]
    edges[pl.ds(core * part, part)] = edge[...]
    edges[pl.ds((1 - core) * part, part)] = swapped[0:part]
    at_hi = 2 * part - frames
    for f in range(frames):
        xp[f, 0] = edges[f] * has_lo
        xp[f, rows + 1] = edges[at_hi + f] * has_hi
        for h in range(rows):
            xp[f, h + 1] = x[f, h + 1]
            up[f + 1, h] = u[f + 1, h]
    up[core * (frames + 1)] = frame[...]
    up[(1 - core) * (frames + 1)] = swapped[part:]

    first, count, others = inner_rows(axial_count, rows)

    def store(h, f, hid, grad):
        hid_out[h, f] = hid
        grad_out[h, f] = grad

    for i in range(count):
        for f in range(1, frames - 1):
            store(first + i, f, hid_in[i, f - 1], grad_in[i, f - 1])
    groups = [(first + i, (0, frames - 1)) for i in range(count)]
    groups += [(h, (f, f + 1)) for h in others for f in range(0, frames, 2)]
    w_part, t_part = cell_grads(xp, up, w_taps, w_act, groups, store)
    factor = 1.0 / math.sqrt(frames * rows * width * rank_count)
    acc[:, : 3 * mid] = (acc_in[:, : 3 * mid] + w_part) * factor
    acc[:, 3 * mid :] = (acc_in[:, 3 * mid :] + t_part) * factor

    blocks, used = pieces(*acc.shape)
    size = packed.shape[0] // 2
    packed[used:] = jnp.zeros((2 * size - used, LANES), F32)
    for at, lane, source, column, depth, total in blocks:
        packed[at : at + depth, lane : lane + total] = acc[source : source + depth, column : column + total]
    half_0[...] = packed[:size].astype(half_0.dtype)
    half_1[...] = packed[size:].astype(half_1.dtype)


def others_kernel(dims, *refs):
    frames, rows, channels, width, mid, own_c, rank_count, axial_count, group = dims
    xp, up, sw, tw, hid_out, grad_out, wf, twf = refs
    w_taps, w_act = prepare(sw, tw, wf, twf)
    for h in range(rows):
        for first in range(0, frames, group):
            picked = range(first, first + group)
            field, cot = gathered(xp, up, h, picked)
            for f, hid, grad in zip(picked, *activations(w_taps, w_act, field, cot, width)):
                hid_out[h, f] = with_rows(hid, padded(mid)).astype(BF16)
                grad_out[h, f] = with_rows(grad, padded(mid)).astype(BF16)


def fields_kernel(dims, fast, *refs):
    frames, rows, channels, width, mid, own_c, rank_count, axial_count, group = dims
    hid_in, grad_in, hid_other, grad_other, sw, tw, sw_other, tw_other = refs[:8]
    out, out_a, out_b, ig_acc, ig_a, ig_b, twt, wg, out_edges = refs[8:]
    own = pl.ds(pl.multiple_of(lax.axis_index("chan") * own_c, own_c), own_c)
    blank = jnp.zeros((own_c, padded(mid) - mid), F32)

    def both(a, b):
        return jnp.concatenate([a.astype(F32), blank, b.astype(F32), blank], 1).astype(BF16)

    for k in range(3):
        twt[k * own_c : (k + 1) * own_c] = both(tw[k, own], tw_other[k, own])
    for i in range(3):
        for j in range(3):
            at = (i * 3 + j) * own_c
            wg[at : at + own_c] = both(sw[i, j, own], sw_other[i, j, own])
    w_out, w_in = twt[...], wg[...]

    for h in range(rows):
        out_terms = {}
        for first in range(0, frames, group):
            picked = range(first, first + group)
            hid = jnp.concatenate([jnp.concatenate([hid_in[h, f], hid_other[h, f]], 0) for f in picked], 1)
            grad = jnp.concatenate([jnp.concatenate([grad_in[h, f], grad_other[h, f]], 0) for f in picked], 1)
            y_out = dot(w_out, hid)
            y_in = dot(w_in, grad)
            for g, f in enumerate(picked):
                cols = slice(g * width, (g + 1) * width)
                for k in range(3):
                    out_terms.setdefault(f - k + 1, []).append(y_out[k * own_c : (k + 1) * own_c, cols])
                for i in range(3):
                    at = i * 3 * own_c
                    total = (
                        y_in[at + own_c : at + 2 * own_c, cols]
                        + moved(y_in[at : at + own_c, cols], -1)
                        + moved(y_in[at + 2 * own_c : at + 3 * own_c, cols], 1)
                    )
                    if h == 0 or i == 2:
                        ig_acc[f, h + i] = total
                    else:
                        ig_acc[f, h + i] += total
        for f, terms in out_terms.items():
            total = functools.reduce(lambda a, b: a + b, terms)
            if f < 0:
                out_edges[0, h] = total.astype(BF16)
            elif f >= frames:
                out_edges[1, h] = total.astype(BF16)
            else:
                out[f, h] = total

    odd = lax.rem(lax.axis_index("tm"), 2) if fast else 1
    high = jnp.where(lax.axis_index("axial") == 0, rows + 1, 0) if fast else 0
    out_a[...] = out_edges[1 - odd]
    out_b[...] = out_edges[odd]
    for f in range(frames):
        ig_a[f] = ig_acc[f, high].astype(BF16)
        ig_b[f] = ig_acc[f, rows + 1].astype(BF16)


def rest_kernel(dims, fast, *refs):
    hid, grad, xp, up, sw, tw, sw_other, tw_other = refs[:8]
    outs, (wf, twf, hid_other, grad_other), scratch = refs[8:14], refs[14:18], refs[18:]
    others_kernel(dims, xp, up, sw_other, tw_other, hid_other, grad_other, wf, twf)
    fields_kernel(dims, fast, hid, grad, hid_other, grad_other, sw, tw, sw_other, tw_other, *outs, *scratch)


def unpack(packed, acc, sg, tg):
    channels, mid = tg.shape[1:]
    for at, lane, source, column, depth, total in pieces(*acc.shape)[0]:
        acc[source : source + depth, column : column + total] = packed[at : at + depth, lane : lane + total]
    for i in range(3):
        rows = slice(i * channels, (i + 1) * channels)
        for j in range(3):
            sg[i, j] = acc[rows, j * mid : (j + 1) * mid]
        tg[2 - i] = acc[rows, 3 * mid :]


def add_edges(axial_count, own, from_lo, from_hi, ig_own, ig_from_lo, ig_from_hi, out, ig):
    frames, rows = own.shape[:2]
    axial = lax.axis_index("axial")
    has_lo = (axial > 0).astype(F32)
    has_hi = (axial < axial_count - 1).astype(F32)
    for f in range(frames):
        for h in range(rows):
            total = own[f, h]
            if f == 0:
                total = total + from_lo(h).astype(F32)
            if f == frames - 1:
                total = total + from_hi(h).astype(F32)
            out[f, h] = total.astype(BF16)
            total = ig_own[f, h + 1]
            if h == 0:
                total = total + ig_from_lo(f).astype(F32) * has_lo
            if h == rows - 1:
                total = total + ig_from_hi(f).astype(F32) * has_hi
            ig[f, h] = total.astype(BF16)


def last_kernel(own, ig_own, half_0, half_1, across, near, far, ig_edge, out, ig, sg, tg, packed, acc, edges):
    frames, rows, own_c, width = own.shape
    size = half_0.shape[0]
    odd = lax.rem(lax.axis_index("tm"), 2)
    edges[1 - odd] = near[size:].reshape(rows, own_c, width)
    edges[odd] = far[size:].reshape(rows, own_c, width)
    add_edges(
        2,
        own,
        lambda h: edges[0, h],
        lambda h: edges[1, h],
        ig_own,
        lambda f: ig_edge[f],
        lambda f: ig_edge[f],
        out,
        ig,
    )
    packed[:size] = half_0[...].astype(F32) + across[...].astype(F32)
    packed[size:] = half_1[...].astype(F32) + far[:size].astype(F32)
    unpack(packed, acc, sg, tg)


def last_kernel_general(axial_count, *refs):
    own, ig_own, half_0, half_1, from_lo, from_hi, ig_from_lo, ig_from_hi, out, ig, sg, tg, packed, acc, edges = refs
    add_edges(
        axial_count,
        own,
        lambda h: from_lo[h],
        lambda h: from_hi[h],
        ig_own,
        lambda f: ig_from_lo[f],
        lambda f: ig_from_hi[f],
        out,
        ig,
    )
    size = half_0.shape[0]
    packed[:size] = half_0[...]
    packed[size:] = half_1[...]
    unpack(packed, acc, sg, tg)


def call(kernel, name, out_shape, count, limit, scratch=(), in_specs=None, flops=0):
    return pl.pallas_call(
        kernel,
        out_shape=out_shape,
        in_specs=in_specs or [VMEM] * count,
        out_specs=[VMEM] * len(out_shape),
        scratch_shapes=list(scratch),
        compiler_params=pltpu.CompilerParams(vmem_limit_bytes=int(limit * 1024 * 1024)),
        cost_estimate=pl.CostEstimate(flops=flops, bytes_accessed=1 << 20, transcendentals=0) if flops else None,
        name=name,
    )


def shards(frames_in, spatial_weight, temporal_weight, upstream):
    frames, rows, channels, width = frames_in.shape
    mid = temporal_weight.shape[1]
    axial_count = lax.axis_size("axial")
    tm_count = lax.axis_size("tm")
    core_count = lax.axis_size("chan")
    rank_count = tm_count * axial_count
    axial = lax.axis_index("axial")
    own_c = channels // core_count
    group = 2 if frames % 2 == 0 else 1
    dims = (frames, rows, channels, width, mid, own_c, rank_count, axial_count, group)
    size = half_rows(3 * channels, 4 * mid)
    sds = jax.ShapeDtypeStruct

    split = axial_count == 2 and frames % 2 == 0
    edge_count = frames // 2 if split else frames
    turned = jnp.swapaxes(temporal_weight, 1, 2)
    edge, frame = call(
        functools.partial(stage_kernel, split),
        "stage",
        [sds((edge_count, channels, width), BF16), sds((rows, channels, width), BF16)],
        4,
        60,
        [pltpu.SemaphoreType.DMA((2,))],
        [HBM] * 4,
    )(frames_in, upstream, spatial_weight, turned)
    frame = lax.ppermute(frame, ("tm", "chan"), facing(tm_count))
    tw_other = lax.ppermute(turned, "chan", ring(2, 1))
    if split:
        edge = lax.ppermute(edge, "axial", ring(2, 1))
    else:
        edge = lax.ppermute(edge, ("axial", "chan"), facing(axial_count))
    sw_other = lax.ppermute(spatial_weight, "chan", ring(2, 1))

    own_shape = (frames, rows, own_c, width)
    inner = (inner_rows(axial_count, rows)[1], frames - 2, padded(mid), width)
    cells = (rows, frames, padded(mid), width)
    xp_shape = (frames, rows + 2, channels, width)
    up_shape = (frames + 2, rows, channels, width)
    total = (3 * channels, 4 * mid)
    forms = [pltpu.VMEM((3 * mid, 3 * channels), F32), pltpu.VMEM((mid, 3 * channels), F32)]
    fast = axial_count == 2 and tm_count == 4
    hid, grad, acc, xp, up, w_taps, w_act = call(
        functools.partial(inner_kernel, dims),
        "inner_cells",
        [
            sds(inner, BF16),
            sds(inner, BF16),
            sds(total, F32),
            sds(xp_shape, BF16),
            sds(up_shape, BF16),
            sds((3 * mid, 3 * channels), BF16),
            sds((mid, 3 * channels), BF16),
        ],
        4,
        16,
        forms,
        flops=1 << 31,
    )(frames_in, upstream, spatial_weight, turned)
    edge, frame, acc = lax.optimization_barrier((edge, frame, acc))
    swapped = lax.ppermute(jnp.concatenate([edge, frame], 0), "chan", ring(2, 1))
    hid, grad, xp, up, half_0, half_1 = call(
        functools.partial(grads_kernel, dims),
        "weight_grads",
        [
            sds(cells, BF16),
            sds(cells, BF16),
            sds(xp_shape, BF16),
            sds(up_shape, BF16),
            sds((size, LANES), BF16 if fast else F32),
            sds((size, LANES), BF16 if fast else F32),
        ],
        10,
        16,
        [
            pltpu.VMEM((2 * edge_count, channels, width), BF16),
            pltpu.VMEM(total, F32),
            pltpu.VMEM((2 * size, LANES), F32),
        ],
    )(hid, grad, acc, xp, up, edge, frame, swapped, w_taps, w_act)

    if fast:
        got_0 = lax.ppermute(half_0, "tm", pairs(4, 1))
        got_1 = lax.ppermute(half_1, "axial", ring(2, 1))

    own_shape = (frames, rows, own_c, width)
    out_edge, ig_edge = sds((rows, own_c, width), BF16), sds((frames, own_c, width), BF16)
    out_own, out_a, out_b, ig_own, ig_a, ig_b = call(
        functools.partial(rest_kernel, dims, fast),
        "field_products",
        [sds(own_shape, F32), out_edge, out_edge, sds((frames, rows + 2, own_c, width), F32), ig_edge, ig_edge],
        8,
        16,
        forms
        + [
            pltpu.VMEM(cells, BF16),
            pltpu.VMEM(cells, BF16),
            pltpu.VMEM((3 * own_c, 2 * padded(mid)), BF16),
            pltpu.VMEM((9 * own_c, 2 * padded(mid)), BF16),
            pltpu.VMEM((2, rows, own_c, width), BF16),
        ],
        flops=1 << 31,
    )(hid, grad, xp, up, spatial_weight, turned, sw_other, tw_other)

    outs = [
        sds(own_shape, BF16),
        sds(own_shape, BF16),
        sds((3, 3, channels, mid), F32),
        sds((3, channels, mid), F32),
    ]
    scratch = [
        pltpu.VMEM((2 * size, LANES), F32),
        pltpu.VMEM(total, F32),
        pltpu.VMEM((2, rows, own_c, width), BF16),
    ]
    if fast:
        got_0, out_a, out_b, ig_a = lax.optimization_barrier((got_0, out_a, out_b, ig_a))
        half_0 = lax.optimization_barrier(half_0 + got_0)
        apart = lax.ppermute(half_0, "tm", pairs(4, 2))
        half_1 = lax.optimization_barrier(half_1 + got_1)
        near = lax.ppermute(jnp.concatenate([half_1, out_a.reshape(-1, width)], 0), "tm", pairs(4, 1))
        half_1 = lax.optimization_barrier(half_1 + near[:size])
        far = lax.ppermute(jnp.concatenate([half_1, out_b.reshape(-1, width)], 0), "tm", pairs(4, 3))
        ig_edge = lax.ppermute(ig_a, "axial", ring(2, 1))
        apart, half_1, ig_edge = lax.optimization_barrier((apart, half_1, ig_edge))
        half_0 = lax.optimization_barrier(half_0 + apart)
        across = lax.ppermute(half_0, "axial", ring(2, 1))
        results = call(last_kernel, "last", outs, 8, 8, scratch)(
            out_own, ig_own, half_0, half_1, across, near, far, ig_edge
        )
    else:
        half_0, half_1 = lax.psum((half_0, half_1), ("tm", "axial"))
        from_hi = lax.ppermute(out_a, "tm", ring(tm_count, -1))
        from_lo = lax.ppermute(out_b, "tm", ring(tm_count, 1))
        ig_from_hi = lax.ppermute(ig_a, "axial", ring(axial_count, -1))
        ig_from_lo = lax.ppermute(ig_b, "axial", ring(axial_count, 1))
        results = call(functools.partial(last_kernel_general, axial_count), "last", outs, 8, 8, scratch)(
            out_own, ig_own, half_0, half_1, from_lo, from_hi, ig_from_lo, ig_from_hi
        )
    output, input_grad, spatial_grad, temporal_grad = results
    return output, input_grad, spatial_grad, jnp.swapaxes(temporal_grad, 1, 2)


def solution(mesh):
    placed = (
        P(("parts", "tm"), "axial", None, None),
        P("parts", None, None, "chan"),
        P("parts", "chan", None),
        P(("parts", "tm"), "axial", None, None),
    )
    return jax.shard_map(
        shards,
        mesh=mesh,
        in_specs=placed,
        out_specs=(
            P(("parts", "tm"), "axial", "chan", None),
            P(("parts", "tm"), "axial", "chan", None),
            P("parts", None, None, "chan"),
            P("parts", "chan", None),
        ),
        check_vma=False,
    )
```
